32 devices in a mesh: section: 2 (over x), dp: 4 (over z), tensor: 4 (over y, core).
Axes of the slice: x: 2, y: 2, z: 4, core: 2. Of those that a mesh axis runs over, the one named last changes fastest.
Arguments:
- decoder_in: bfloat16 [16384, 1024], P(('section', 'dp'), 'tensor'), may hold values from -6 to 6
- encoder_out: bfloat16 [16384, 1024], P(('section', 'dp'), 'tensor'), may hold values from -6 to 6
- segments: int32 [8, 2048], P(('section', 'dp')), may hold values from 0 to 5, never falling along the last dimension, each value on 1 to 1024 neighbouring positions
- w_skip: bfloat16 [2, 1024, 1024], P(None, 'tensor'), may hold values from -0.125 to 0.125
- b_skip: float32 [1024], replicated, may hold values from -2 to 2
- ln1_gain: float32 [1024], replicated, may hold values from 0.5 to 1.5
- ln1_bias: float32 [1024], replicated, may hold values from -2 to 2
- w_qkv: bfloat16 [1024, 3, 1024], P(None, None, 'tensor'), may hold values from -0.1875 to 0.1875
- w_out: bfloat16 [1024, 1024], P('tensor'), may hold values from -0.5 to 0.5
- ln2_gain: float32 [1024], replicated, may hold values from 0.5 to 1.5
- ln2_bias: float32 [1024], replicated, may hold values from -2 to 2
- w_up: bfloat16 [1024, 4096], P(None, 'tensor'), may hold values from -0.1875 to 0.1875
- c_up: float32 [4096], P('tensor'), may hold values from -3 to 3
- w_down: bfloat16 [4096, 1024], P('tensor'), may hold values from -0.09375 to 0.09375
- cotangent: bfloat16 [16384, 1024], P(('section', 'dp')), may hold values from -6 to 6
Outputs:
- layer_out: float32 [16384, 1024], P(('section', 'dp', 'tensor'))
- d_decoder_in: float32 [16384, 1024], P(('section', 'dp'), 'tensor')
- d_encoder_out: bfloat16 [16384, 1024], P(('section', 'dp'), 'tensor')
- d_w_skip: float32 [2, 1024, 1024], P(None, 'tensor')
- d_b_skip: float32 [1024], replicated
- d_ln1_gain: float32 [1024], replicated
- d_ln1_bias: float32 [1024], replicated
- d_w_qkv: float32 [1024, 3, 1024], P(None, None, 'tensor')
- d_w_out: float32 [1024, 1024], P('tensor')
- d_ln2_gain: float32 [1024], replicated
- d_ln2_bias: float32 [1024], replicated
- d_w_up: float32 [1024, 4096], P(None, 'tensor')
- d_c_up: float32 [4096], P('tensor')
- d_w_down: float32 [4096, 1024], P('tensor')
The draws below stay inside these ranges and needn't reach their ends.
Inputs may be any that keep to these rules, and one draw needn't show every extreme that they name: `segments`: along each packed row of 2048 frames the ids never fall; each utterance holds 1 to 1024 frames, and one of each row holds exactly 1024.
All inputs are finite; a program needn't handle non-finite values.
Results may differ from the reference program's by a relative error of at most 0.019.
Values may be sent and summed in bfloat16 or wider, within the bound.
No kernel may reach another device: no remote copies, remote signals or barrier semaphores. Data moves between devices by JAX's collectives and lax.ppermute only.
A program may use at most 192 MiB of HBM per device.

```python
import math
import jax
import jax.numpy as jnp
import numpy as np
from jax import lax

D = 1024
HEADS = 16
FF = 4096
LEN = 2048
UTTS = 6
UTT_MOST = 1024
PACKS = 8
TOKENS = 16384


def levels(key, dims, cuts, smallest, top_value):
    def one(dim, blocks):
        draws = jax.random.uniform(jax.random.fold_in(jax.random.fold_in(key, 6), dim), (blocks,), jnp.float32, smallest / len(cuts), top_value / len(cuts))
        return jnp.repeat(jnp.exp(draws), dims[dim] // blocks).reshape((-1,) + (1,) * (len(dims) - dim - 1))

    level = one(*cuts[0])
    for cut in cuts[1:]:
        level = level * one(*cut)
    return level


def profile(number_of, total, bound, skew):
    loads = [(1 << 20) // math.isqrt(standing ** skew) + 1 for standing in range(2, number_of + 1)]
    rest, counts = total - bound - (number_of - 1), [1] * (number_of - 1)
    while rest > 0:
        movable = [i for i in range(number_of - 1) if counts[i] < bound]
        mass, budget = sum([loads[i] for i in movable]), rest
        for i in movable:
            extra = min(bound - counts[i], max(1, budget * loads[i] // mass), rest)
            counts[i] = counts[i] + extra
            rest = rest - extra
    return np.array([bound] + counts)


def ragged_sizes(rng, amount, total, limit, lean):
    if amount == 2:
        one = jax.random.randint(rng, (), max(1, total - limit), min(limit, total - 1) + 1)
        return jnp.stack([one, total - one])
    sizes = jnp.asarray(profile(amount, total, limit, lean), jnp.int32)
    couples = (amount - 1) // 2
    source_of, receiver = sizes[1:1 + 2 * couples:2], sizes[2:2 + 2 * couples:2]
    margin = jnp.minimum(source_of - 1, limit - receiver)
    moved = jax.random.randint(jax.random.fold_in(rng, 1), (couples,), 0, 1 << 20) % (margin + 1)
    sizes = sizes.at[1:1 + 2 * couples:2].set(source_of - moved).at[2:2 + 2 * couples:2].set(receiver + moved)
    return sizes[jax.random.permutation(jax.random.fold_in(rng, 2), amount)]


def noise(own_key, shape, width, reach, split=(), held_as=jnp.bfloat16):
    values = width * jax.random.normal(own_key, shape, jnp.float32)
    if split:
        values = values * levels(own_key, shape, split, -0.22, 0.18)
    return jnp.clip(values, -reach, reach).astype(held_as)


def setup_inputs(seed: int = 0) -> dict:
    seeds = jax.random.split(jax.random.key(seed), 16)
    return {
        "decoder_in": noise(seeds[0], (TOKENS, D), 1.0, 6.0, ((0, 8), (1, 4))),
        "encoder_out": noise(seeds[1], (TOKENS, D), 1.0, 6.0, ((0, 8), (1, 4))),
        "segments": jax.vmap(lambda own: jnp.searchsorted(jnp.cumsum(ragged_sizes(own, UTTS, LEN, UTT_MOST, 1)), jnp.arange(LEN), side="right"))(jax.random.split(seeds[2], PACKS)).reshape((PACKS, LEN)).astype(jnp.int32),
        "w_skip": noise(seeds[3], (2, D, D), (2 * D) ** -0.5, 0.125, ((1, 4),)),
        "b_skip": noise(seeds[4], (D,), 0.3, 2.0, (), jnp.float32),
        "ln1_gain": jnp.clip(1.0 + 0.1 * jax.random.normal(seeds[5], (D,), jnp.float32), 0.5, 1.5),
        "ln1_bias": noise(seeds[6], (D,), 0.3, 2.0, (), jnp.float32),
        "w_qkv": noise(seeds[7], (D, 3, D), D ** -0.5, 0.1875, ((2, 4),)),
        "w_out": noise(seeds[8], (D, D), (D // 8) ** -0.5, 0.5, ((0, 4),)),
        "ln2_gain": jnp.clip(1.0 + 0.1 * jax.random.normal(seeds[9], (D,), jnp.float32), 0.5, 1.5),
        "ln2_bias": noise(seeds[10], (D,), 0.3, 2.0, (), jnp.float32),
        "w_up": noise(seeds[11], (D, FF), D ** -0.5, 0.1875, ((1, 4),)),
        "c_up": noise(seeds[12], (FF,), 0.5, 3.0, ((0, 4),), jnp.float32),
        "w_down": noise(seeds[13], (FF, D), FF ** -0.5, 0.09375, ((0, 4),)),
        "cotangent": noise(seeds[14], (TOKENS, D), 1.0, 6.0, ((0, 8),)),
    }


EPSILON = 1e-05
MASKED = -1e+30
ROOT_HALF = 0.7071067811865476
PRECISE = lax.Precision.HIGHEST

@jax.custom_vjp
def low(v):
    return lax.optimization_barrier(v.astype(jnp.bfloat16)).astype(jnp.float32)

@jax.custom_vjp
def low_back(v):
    return v

def low_keep(v):
    return (low(v), None)

def low_pass(kept, grad):
    return (grad,)

def back_keep(v):
    return (v, None)

def back_low(kept, grad):
    return (low(grad),)
low.defvjp(low_keep, low_pass)
low_back.defvjp(back_keep, back_low)

def matmul(left, right):
    return jnp.dot(left, right, precision=PRECISE, preferred_element_type=jnp.float32)

def layer_norm(values, gain, shift):
    row_mean = lax.optimization_barrier(jnp.mean(values, axis=-1, keepdims=True))
    centered = values - row_mean
    inv_std = lax.rsqrt(lax.optimization_barrier(jnp.mean(centered * centered, axis=-1, keepdims=True)) + EPSILON)
    return centered * inv_std * gain + shift

def gelu_exact(values):
    return 0.5 * values * (1.0 + lax.erf(values * ROOT_HALF))

def attend_pack(pieces):
    queries, key_rows, val_rows, seg_row = pieces
    head_dim = queries.shape[-1]
    positions = jnp.arange(LEN, dtype=jnp.int32)
    distance = jnp.abs(positions[:, None] - positions[None, :]).astype(jnp.float32)
    slopes = jnp.exp2(-8.0 * (jnp.arange(HEADS, dtype=jnp.int32) + 1).astype(jnp.float32) / HEADS)
    scores = jnp.einsum('qhe,khe->hqk', queries, key_rows, precision=PRECISE) * head_dim ** (-0.5)
    scores = low_back(scores - slopes[:, None, None] * distance[None])
    scores = jnp.where((seg_row[:, None] == seg_row[None, :])[None], scores, MASKED)
    row_max = lax.optimization_barrier(jnp.max(scores, axis=-1, keepdims=True))
    exponent = jnp.exp(scores - row_max)
    weights = low(exponent / lax.optimization_barrier(jnp.sum(exponent, axis=-1, keepdims=True)))
    return jnp.einsum('hqk,khe->qhe', weights, val_rows, precision=PRECISE)

def reference(decoder_in, encoder_out, segments, w_skip, b_skip, ln1_gain, ln1_bias, w_qkv, w_out, ln2_gain, ln2_bias, w_up, c_up, w_down, cotangent):
    head_dim = D // HEADS

    def layer(dec_rows, enc_rows, skip_weight, skip_bias, gain_one, shift_one, qkv_weight, out_weight, gain_two, shift_two, up_weight, up_bias, down_weight):
        encoder_used = jnp.roll(low_back(enc_rows), TOKENS // 2, axis=0)
        merged = low_back(matmul(dec_rows, skip_weight[0]) + matmul(encoder_used, skip_weight[1])) + skip_bias
        norm_one = low(layer_norm(merged, gain_one, shift_one))
        qkv = low_back(low(matmul(norm_one, qkv_weight.reshape(D, 3 * D))))
        qkv = qkv.reshape(PACKS, LEN, 3, HEADS, head_dim)
        mixed = lax.map(jax.checkpoint(attend_pack), (qkv[:, :, 0], qkv[:, :, 1], qkv[:, :, 2], segments))
        heads_out = low_back(low(mixed.reshape(TOKENS, D)))
        attended = merged + low_back(matmul(heads_out, out_weight))
        norm_two = low(layer_norm(attended, gain_two, shift_two))
        pre = low_back(matmul(norm_two, up_weight) + up_bias)
        return attended + low_back(matmul(low(gelu_exact(pre)), down_weight))
    floats = tuple((value.astype(jnp.float32) for value in (decoder_in, encoder_out, w_skip, b_skip, ln1_gain, ln1_bias, w_qkv, w_out, ln2_gain, ln2_bias, w_up, c_up, w_down)))
    layer_out, pullback = jax.vjp(layer, *floats)
    grads = pullback(cotangent.astype(jnp.float32))
    return (layer_out, grads[0], grads[1].astype(jnp.bfloat16), grads[2], grads[3], grads[4], grads[5], grads[6], grads[7], grads[8], grads[9], grads[10], grads[11], grads[12])
```

```python
import functools
import jax
import jax.numpy as jnp
from jax import lax
from jax.experimental import pallas as pl
from jax.experimental.pallas import tpu as pltpu
from jax.sharding import PartitionSpec as P

D = 1024
HEADS = 16
UTTS = 6
HEAD_DIM = D // HEADS
SCALE = HEAD_DIM**-0.5

EPSILON = 1e-05
FAR = 1e30
ROOT_HALF = 0.7071067811865476
INV_ROOT_TAU = 0.3989422804014327
BF16 = jnp.bfloat16
F32 = jnp.float32
NT = (((1,), (1,)), ((), ()))
NN = (((1,), (0,)), ((), ()))
TN = (((0,), (0,)), ((), ()))
CHUNKS = 2


def mm(left, right, dims):
    return lax.dot_general(left, right, dims, preferred_element_type=F32)


def starts_of(seg):
    return [jnp.sum((seg < u).astype(jnp.int32)) for u in range(1, UTTS)]


def tile_range(starts, first, count, tile, total):
    low = jnp.int32(0)
    high = jnp.int32(total)
    for s in starts:
        low = jnp.maximum(low, jnp.where(s <= first, s, 0))
        high = jnp.minimum(high, jnp.where(s >= first + count, s, total))
    return low // tile, (high + tile - 1) // tile


def eye(n):
    r = lax.broadcasted_iota(jnp.int32, (n, n), 0)
    c = lax.broadcasted_iota(jnp.int32, (n, n), 1)
    return jnp.where(r == c, 1.0, 0.0).astype(BF16)


def far_tile(starts, seg_row, q_first, k_first, bk, bq):
    kpos = k_first + lax.broadcasted_iota(jnp.int32, (bk, bq), 0)
    qpos = q_first + lax.broadcasted_iota(jnp.int32, (bk, bq), 1)
    lo = jnp.zeros_like(seg_row)
    hi = jnp.full_like(seg_row, starts[0])
    for u in range(1, UTTS):
        lo = jnp.where(seg_row == u, starts[u - 1], lo)
        hi = jnp.where(seg_row == u, starts[u] if u < UTTS - 1 else 1 << 30, hi)
    ok = (kpos >= lo) & (kpos < hi)
    return jnp.where(ok, jnp.abs(kpos - qpos).astype(F32), FAR)


def head_masked(pair, which):
    lane = lax.broadcasted_iota(jnp.int32, pair.shape, 1)
    keep = (lane < HEAD_DIM) if which == 0 else (lane >= HEAD_DIM)
    return jnp.where(keep, pair, 0.0).astype(BF16)


def load_pieces(core, pieces, whole_ref, sems):
    copies = []
    rows = pieces[0].shape[1]
    for n, piece in enumerate(pieces):
        chunk, side = n // 2, n % 2
        for y in range(2):
            first = y * (4 * rows) + (core ^ side) * (2 * rows) + chunk * rows
            copy = pltpu.make_async_copy(
                piece.at[y], whole_ref.at[pl.ds(pl.multiple_of(first, rows), rows)], sems.at[n, y]
            )
            copy.start()
            copies.append(copy)
    for copy in copies:
        copy.wait()


def fwd_kernel(
    heads, bk, chunk, core_ref, slope_ref, seg_ref, q00, q01, q10, q11,
    out_ref, lse_ref, qkv_ref, vt_ref, acc_ref, s_ref, top_ref, sems,
):
    total = seg_ref.shape[1]
    width = heads * HEAD_DIM
    bq = out_ref.shape[1] // 2
    core = core_ref[0]
    load_pieces(core, (q00, q01, q10, q11), qkv_ref, sems)
    starts = starts_of(seg_ref[...])
    ident = eye(width)

    def prep(j, c):
        at = pl.ds(pl.multiple_of(j * bk, bk), bk)
        vt = mm(ident, qkv_ref[at, 2 * width : 3 * width], NT).astype(BF16)
        for h in range(heads):
            vt_ref[h * 80 : h * 80 + 64, at] = vt[h * 64 : (h + 1) * 64]
            vt_ref[h * 80 + 64 : (h + 1) * 80, at] = jnp.ones((16, bk), BF16)
        return c

    lax.fori_loop(0, total // bk, prep, 0)

    def q_step(i, c):
        side, y = i // 2, i % 2
        qi = pl.multiple_of(y * (4 * bq) + (core ^ side) * (2 * bq) + chunk * bq, bq)
        lo, hi = tile_range(starts, qi, bq, bk, total)
        seg_row = seg_ref[:, pl.ds(qi, bq)]
        acc_ref[...] = jnp.zeros_like(acc_ref)
        top_ref[...] = jnp.full_like(top_ref, -3e38)
        qs = []
        for h in range(heads):
            p = h // 2
            qp = qkv_ref[pl.ds(qi, bq), p * 128 : (p + 1) * 128].astype(F32) * SCALE
            qs.append(head_masked(qp, h % 2))

        def score_step(j, c):
            kj = pl.multiple_of(j * bk, bk)
            far = far_tile(starts, seg_row, qi, kj, bk, bq)
            for h in range(heads):
                p = h // 2
                kp = qkv_ref[pl.ds(kj, bk), width + p * 128 : width + (p + 1) * 128]
                s = mm(kp, qs[h], NT) - far * slope_ref[h]
                s_ref[h, pl.ds(kj, bk)] = s
                top_ref[h] = jnp.maximum(top_ref[h], jnp.max(s.reshape(bk // 8, 8, bq), axis=0))
            return c

        lax.fori_loop(lo, hi, score_step, 0)
        tops = [jnp.max(top_ref[h], axis=0, keepdims=True) for h in range(heads)]

        def mix_step(j, c):
            kj = pl.multiple_of(j * bk, bk)
            for h in range(heads):
                e = jnp.exp(s_ref[h, pl.ds(kj, bk)] - tops[h]).astype(BF16)
                hs = slice(h * 80, (h + 1) * 80)
                acc_ref[hs] = acc_ref[hs] + mm(vt_ref[hs, pl.ds(kj, bk)], e, NN)
            return c

        lax.fori_loop(lo, hi, mix_step, 0)
        outs = []
        for h in range(heads):
            whole = acc_ref[h * 80 + 64 : h * 80 + 65]
            outs.append((acc_ref[h * 80 : h * 80 + 64] * (1.0 / whole)).astype(BF16))
            lse_ref[i, h : h + 1] = tops[h] + jnp.log(whole)
        ot = jnp.concatenate(outs, axis=0)
        out_ref[side, pl.ds(pl.multiple_of(y * bq, bq), bq)] = mm(eye(bq), ot, NT).astype(BF16)
        return c

    lax.fori_loop(0, 4, q_step, 0)


def attend(chunk, core, slopes, seg, pieces):
    total = seg.shape[1]
    rows = pieces[0].shape[1]
    heads = pieces[0].shape[2] // (3 * HEAD_DIM)
    width = heads * HEAD_DIM
    bk = 256
    smem = pl.BlockSpec(memory_space=pltpu.SMEM)
    vmem = pl.BlockSpec(memory_space=pltpu.VMEM)
    hbm = pl.BlockSpec(memory_space=pl.ANY)
    return pl.pallas_call(
        functools.partial(fwd_kernel, heads, bk, chunk),
        out_shape=(
            jax.ShapeDtypeStruct((2, 2 * rows, width), BF16),
            jax.ShapeDtypeStruct((4, heads, rows), F32),
        ),
        in_specs=[smem, smem, vmem] + [hbm] * 4,
        out_specs=(vmem, vmem),
        scratch_shapes=[
            pltpu.VMEM((total, 3 * width), BF16),
            pltpu.VMEM((heads * 80, total), BF16),
            pltpu.VMEM((heads * 80, rows), F32),
            pltpu.VMEM((heads, total, rows), F32),
            pltpu.VMEM((heads, 8, rows), F32),
            pltpu.SemaphoreType.DMA((4, 2)),
        ],
        compiler_params=pltpu.CompilerParams(vmem_limit_bytes=40 << 20),
        name="attend",
    )(core, slopes, seg, *pieces)


def bwd_kernel(heads, bk, chunk, *refs):
    core_ref, slope_ref, seg_ref, q00, q01, q10, q11, do0, do1, o_ref, lse_ref = refs[:11]
    if chunk == 0:
        dq_ref, dkv_ref = refs[11:13]
        rest = refs[13:]
    else:
        dq_in, dkv_in, dqkv_ref = refs[11:14]
        rest = refs[14:]
    qkv_ref, kt_ref, dqt_ref, dk_ref, dv_ref, delta_ref, sems = rest
    total = seg_ref.shape[1]
    width = heads * HEAD_DIM
    bq = o_ref.shape[1] // 2
    core = core_ref[0]
    load_pieces(core, (q00, q01, q10, q11), qkv_ref, sems)
    starts = starts_of(seg_ref[...])
    ident = eye(width)
    hr = lax.broadcasted_iota(jnp.int32, (8, width), 0)
    hc = lax.broadcasted_iota(jnp.int32, (8, width), 1)
    pick = jnp.where(hr == hc // HEAD_DIM, 1.0, 0.0)

    def prep(j, c):
        at = pl.ds(pl.multiple_of(j * bk, bk), bk)
        kj = qkv_ref[at, width : 2 * width]
        kt_ref[:, at] = (mm(ident, kj, NT) * SCALE).astype(BF16)
        if chunk == 0:
            dk_ref[at] = jnp.zeros((bk, width), F32)
            dv_ref[at] = jnp.zeros((bk, width), F32)
        else:
            dk_ref[at] = dkv_in[at, :width]
            dv_ref[at] = dkv_in[at, width:]
        return c

    lax.fori_loop(0, total // bk, prep, 0)
    for side, do_ref in enumerate((do0, do1)):
        for y in range(2):
            at = slice(y * bq, (y + 1) * bq)
            prod = do_ref[at].astype(F32) * o_ref[side, at].astype(F32)
            delta_ref[side * 2 + y] = lax.dot_general(
                pick, prod, NT, precision=lax.Precision.HIGHEST, preferred_element_type=F32
            )

    for side, do_ref in enumerate((do0, do1)):

        def q_step(y, c, side=side, do_ref=do_ref):
            i = side * 2 + y
            qi = pl.multiple_of(y * (4 * bq) + (core ^ side) * (2 * bq) + chunk * bq, bq)
            here = pl.ds(pl.multiple_of(y * bq, bq), bq)
            lo, hi = tile_range(starts, qi, bq, bk, total)
            seg_row = seg_ref[:, pl.ds(qi, bq)]
            dqt_ref[...] = jnp.zeros_like(dqt_ref)
            qs, dos = [], []
            for h in range(heads):
                p = h // 2
                qp = qkv_ref[pl.ds(qi, bq), p * 128 : (p + 1) * 128].astype(F32) * SCALE
                qs.append(head_masked(qp, h % 2))
                dp = do_ref[here, p * 128 : (p + 1) * 128].astype(F32)
                dos.append(head_masked(dp, h % 2))
            lses = [lse_ref[i, h : h + 1] for h in range(heads)]
            deltas = [delta_ref[i, h : h + 1] for h in range(heads)]

            def k_step(j, c):
                kj = pl.multiple_of(j * bk, bk)
                at = pl.ds(kj, bk)
                far = far_tile(starts, seg_row, qi, kj, bk, bq)
                for p in range(heads // 2):
                    cols = slice(p * 128, (p + 1) * 128)
                    kp = qkv_ref[at, width + p * 128 : width + (p + 1) * 128]
                    vp = qkv_ref[at, 2 * width + p * 128 : 2 * width + (p + 1) * 128]
                    dv = dv_ref[at, cols]
                    dk = dk_ref[at, cols]
                    for h in (2 * p, 2 * p + 1):
                        s = mm(kp, qs[h], NT) - far * slope_ref[h]
                        w = jnp.exp(s - lses[h])
                        dw = mm(vp, dos[h], NT)
                        ds = (w * (dw - deltas[h])).astype(BF16)
                        dv = dv + mm(w.astype(BF16), dos[h], NN)
                        dk = dk + mm(ds, qs[h], NN)
                        hs = slice(h * HEAD_DIM, (h + 1) * HEAD_DIM)
                        dqt_ref[hs] = dqt_ref[hs] + mm(kt_ref[hs, at], ds, NN)
                    dv_ref[at, cols] = dv
                    dk_ref[at, cols] = dk
                return c

            lax.fori_loop(lo, hi, k_step, 0)
            dq = mm(eye(bq), dqt_ref[...].astype(BF16), NT).astype(BF16)
            if chunk == 0:
                dq_ref[side, here] = dq
            else:
                dqkv_ref[2 + side, here, :width] = dq
            return c

        lax.fori_loop(0, 2, q_step, 0)

    if chunk == 0:

        def finish(j, c):
            at = pl.ds(pl.multiple_of(j * bk, bk), bk)
            dkv_ref[at, :width] = dk_ref[at]
            dkv_ref[at, width:] = dv_ref[at]
            return c

        lax.fori_loop(0, total // bk, finish, 0)
    else:
        for side in range(2):
            dqkv_ref[side, :, :width] = dq_in[side]
        for n in range(4):
            part, side = n // 2, n % 2
            for y in range(2):
                first = y * (4 * bq) + (core ^ side) * (2 * bq) + part * bq
                at = pl.ds(pl.multiple_of(first, bq), bq)
                here = slice(y * bq, (y + 1) * bq)
                dqkv_ref[n, here, width : 2 * width] = dk_ref[at].astype(BF16)
                dqkv_ref[n, here, 2 * width :] = dv_ref[at].astype(BF16)


def attend_back(chunk, core, slopes, seg, pieces, d_heads, heads_out, lse, before=()):
    total = seg.shape[1]
    rows = pieces[0].shape[1]
    heads = pieces[0].shape[2] // (3 * HEAD_DIM)
    width = heads * HEAD_DIM
    bk = 256
    smem = pl.BlockSpec(memory_space=pltpu.SMEM)
    vmem = pl.BlockSpec(memory_space=pltpu.VMEM)
    hbm = pl.BlockSpec(memory_space=pl.ANY)
    if chunk == 0:
        out_shape = (
            jax.ShapeDtypeStruct((2, 2 * rows, width), BF16),
            jax.ShapeDtypeStruct((total, 2 * width), F32),
        )
        out_specs = (vmem, vmem)
    else:
        out_shape = jax.ShapeDtypeStruct((4, 2 * rows, 3 * width), BF16)
        out_specs = vmem
    return pl.pallas_call(
        functools.partial(bwd_kernel, heads, bk, chunk),
        out_shape=out_shape,
        in_specs=[smem, smem, vmem] + [hbm] * 4 + [vmem] * (4 + len(before)),
        out_specs=out_specs,
        scratch_shapes=[
            pltpu.VMEM((total, 3 * width), BF16),
            pltpu.VMEM((width, total), BF16),
            pltpu.VMEM((width, rows), F32),
            pltpu.VMEM((total, width), F32),
            pltpu.VMEM((total, width), F32),
            pltpu.VMEM((4, 8, rows), F32),
            pltpu.SemaphoreType.DMA((4, 2)),
        ],
        compiler_params=pltpu.CompilerParams(vmem_limit_bytes=48 << 20),
        name="attend_back",
    )(core, slopes, seg, *pieces, *d_heads, heads_out, lse, *before)


def swap(value, axis, bit):
    pairs = [(source, source ^ (1 << bit)) for source in range(lax.axis_size(axis))]
    return lax.ppermute(value, axis, pairs)


core_swap = functools.partial(swap, axis="tensor", bit=0)
chip_swap = functools.partial(swap, axis="tensor", bit=1)
partner_swap = functools.partial(swap, axis="section", bit=0)


def add_low(*terms):
    return sum(term.astype(F32) for term in terms).astype(BF16)


def group_steps():
    steps = [("section", 0)]
    for bit in range((lax.axis_size("dp") - 1).bit_length()):
        steps.append(("dp", bit))
    return steps


def group_sum(value, steps):
    sides = []
    for axis, bit in steps:
        mine = (lax.axis_index(axis) >> bit) & 1
        halves = value.reshape(2, value.shape[0] // 2, value.shape[1])
        sent = lax.dynamic_index_in_dim(halves, 1 - mine, 0, keepdims=False)
        kept = lax.dynamic_index_in_dim(halves, mine, 0, keepdims=False)
        value = add_low(kept, swap(sent, axis, bit))
        sides.append((axis, bit, mine))
    for axis, bit, mine in reversed(sides):
        other = swap(value, axis, bit)
        first = mine == 0
        value = jnp.concatenate(
            [jnp.where(first, value, other), jnp.where(first, other, value)], axis=0
        )
    return value


def layer_norm(values, gain, shift):
    row_mean = jnp.mean(values, axis=-1, keepdims=True)
    centered = values - row_mean
    inv_std = lax.rsqrt(jnp.mean(centered * centered, axis=-1, keepdims=True) + EPSILON)
    normed = centered * inv_std
    return (normed * gain + shift, normed, inv_std)


def norm_back(d_output, normed, inv_std, gain):
    d_normed = d_output * gain
    d_input = inv_std * (
        d_normed
        - jnp.mean(d_normed, axis=-1, keepdims=True)
        - normed * jnp.mean(d_normed * normed, axis=-1, keepdims=True)
    )
    return (d_input, jnp.sum(d_output * normed, axis=0), jnp.sum(d_output, axis=0))


def gelu_exact(values):
    return 0.5 * values * (1.0 + lax.erf(values * ROOT_HALF))


def gelu_slope(values):
    return (
        0.5 * (1.0 + lax.erf(values * ROOT_HALF))
        + values * jnp.exp(-0.5 * values * values) * INV_ROOT_TAU
    )


def shards(
    decoder_in,
    encoder_out,
    segments,
    w_skip,
    b_skip,
    ln1_gain,
    ln1_bias,
    w_qkv,
    w_out,
    ln2_gain,
    ln2_bias,
    w_up,
    c_up,
    w_down,
    cotangent,
):
    group_rows = decoder_in.shape[0]
    tensor_rank = lax.axis_index("tensor")
    core = tensor_rank & 1
    chip = tensor_rank >> 1
    heads_here = HEADS // lax.axis_size("tensor")
    local_width = heads_here * HEAD_DIM
    block = group_rows // (4 * CHUNKS)
    qkv_matrix = w_qkv.reshape(D, 3 * local_width)
    core_scalar = core.reshape(1).astype(jnp.int32)
    slopes = jnp.exp2(
        -8.0
        * (tensor_rank * heads_here + jnp.arange(heads_here, dtype=jnp.int32) + 1).astype(F32)
        / HEADS
    )
    spots = [(chunk, side) for chunk in range(CHUNKS) for side in range(2)]

    def piece_of(array, chunk, side):
        width = array.shape[-1]
        parts = array.reshape(2, 2, CHUNKS, block, width)[:, :, chunk]
        return lax.dynamic_index_in_dim(parts, core ^ side, 1, keepdims=False).reshape(
            2 * block, width
        )

    def whole_of(pieces):
        width = pieces[0].shape[-1]
        sides = []
        for side in range(2):
            sides.append(
                jnp.stack(
                    [pieces[2 * n + side].reshape(2, block, width) for n in range(CHUNKS)], axis=1
                )
            )
        zero = core == 0
        return jnp.stack(
            [jnp.where(zero, sides[0], sides[1]), jnp.where(zero, sides[1], sides[0])], axis=1
        ).reshape(group_rows, width)

    encoder_parts = encoder_out.reshape(2, 2, CHUNKS, block, encoder_out.shape[1])
    partner = [
        partner_swap(encoder_parts[:, :, chunk].reshape(4 * block, -1)) for chunk in range(CHUNKS)
    ]

    def partner_piece(chunk, side):
        parts = partner[chunk].reshape(2, 2, block, -1)
        return lax.dynamic_index_in_dim(parts, core ^ side, 1, keepdims=False).reshape(
            2 * block, -1
        )

    merged, normed_one, inv_std_one, norm_one, qkv = [], [], [], {}, {}
    for chunk in range(CHUNKS):
        halves = [
            (
                jnp.dot(piece_of(decoder_in, chunk, side), w_skip[0], preferred_element_type=F32)
                + jnp.dot(partner_piece(chunk, side), w_skip[1], preferred_element_type=F32)
            ).astype(BF16)
            for side in range(2)
        ]
        chip_sum = add_low(halves[0], core_swap(halves[1]))
        value = chip_sum.astype(F32) + chip_swap(chip_sum).astype(F32) + b_skip
        normal, normed, inv_std = layer_norm(value, ln1_gain, ln1_bias)
        merged.append(value)
        normed_one.append(normed)
        inv_std_one.append(inv_std)
        normal = normal.astype(BF16)
        norm_one[chunk, 0] = normal
        norm_one[chunk, 1] = core_swap(normal)
        for side in range(2):
            qkv[chunk, side] = jnp.dot(
                norm_one[chunk, side], qkv_matrix, preferred_element_type=F32
            ).astype(BF16)
    qkv_pieces = [qkv[spot].reshape(2, block, 3 * local_width) for spot in spots]

    heads_out, lse, attended, d_attended, d_attended_rows = [], [], [], [], {}
    gain_two_sum = shift_two_sum = c_up_sum = 0.0
    norm_two, activated, d_pre, cot = {}, {}, {}, {}
    normed_two, inv_std_two = [], []
    for chunk in range(CHUNKS):
        mixed, log_total = attend(chunk, core_scalar, slopes, segments, qkv_pieces)
        heads_out.append(mixed)
        lse.append(log_total)
        halves = [
            jnp.dot(mixed[side], w_out, preferred_element_type=F32).astype(BF16)
            for side in range(2)
        ]
        chip_sum = add_low(halves[0], core_swap(halves[1]))
        value = merged[chunk] + (chip_sum.astype(F32) + chip_swap(chip_sum).astype(F32))
        attended.append(value)
        normal, normed, inv_std = layer_norm(value, ln2_gain, ln2_bias)
        normed_two.append(normed)
        inv_std_two.append(inv_std)
        normal = normal.astype(BF16)
        norm_two[chunk, 0] = normal
        norm_two[chunk, 1] = core_swap(normal)
    for chunk in range(CHUNKS):
        halves = []
        for side in range(2):
            spot = chunk, side
            cot[spot] = piece_of(cotangent, chunk, side)
            pre = jnp.dot(norm_two[spot], w_up, preferred_element_type=F32) + c_up
            activated[spot] = gelu_exact(pre).astype(BF16)
            d_act = mm(cot[spot], w_down, NT)
            d_pre[spot] = (d_act * gelu_slope(pre)).astype(BF16)
            c_up_sum = c_up_sum + jnp.sum(d_pre[spot], axis=0, dtype=F32)
            halves.append(mm(d_pre[spot], w_up, NT).astype(BF16))
        chip_sum = add_low(halves[0], core_swap(halves[1]))
        d_norm = chip_sum.astype(F32) + chip_swap(chip_sum).astype(F32)
        d_value, d_gain, d_shift = norm_back(
            d_norm, normed_two[chunk], inv_std_two[chunk], ln2_gain
        )
        gain_two_sum = gain_two_sum + d_gain
        shift_two_sum = shift_two_sum + d_shift
        d_value = cot[chunk, 0].astype(F32) + d_value
        d_attended.append(d_value)
        low = d_value.astype(BF16)
        d_attended_rows[chunk, 0] = low
        d_attended_rows[chunk, 1] = core_swap(low)

    d_heads = {
        spot: mm(d_attended_rows[spot], w_out, NT).astype(BF16) for spot in spots
    }
    d_q, d_kv = attend_back(
        0, core_scalar, slopes, segments, qkv_pieces,
        [d_heads[0, 0], d_heads[0, 1]], heads_out[0], lse[0],
    )
    d_qkv = attend_back(
        1, core_scalar, slopes, segments, qkv_pieces,
        [d_heads[1, 0], d_heads[1, 1]], heads_out[1], lse[1], (d_q, d_kv),
    )

    d_w_down = sum(mm(activated[spot], cot[spot], TN) for spot in spots)
    d_w_up = sum(mm(norm_two[spot], d_pre[spot], TN) for spot in spots)
    d_w_out = sum(
        mm(heads_out[spot[0]][spot[1]], d_attended_rows[spot], TN) for spot in spots
    )
    d_w_down, d_w_up = lax.psum((d_w_down.astype(BF16), d_w_up.astype(BF16)), ("section", "dp"))

    halves = []
    for side in range(2):
        acts = jnp.concatenate(
            [activated[chunk, side].reshape(2, 1, block, -1) for chunk in range(CHUNKS)], axis=1
        ).reshape(2 * CHUNKS * block, -1)
        halves.append(jnp.dot(acts, w_down, preferred_element_type=F32).astype(BF16))
    chip_sum = add_low(halves[0], core_swap(halves[1])).reshape(2, CHUNKS * block, D)
    away = lax.dynamic_index_in_dim(chip_sum, 1 - chip, 0, keepdims=False)
    home = lax.dynamic_index_in_dim(chip_sum, chip, 0, keepdims=False)
    kept = jnp.concatenate(
        [
            lax.dynamic_index_in_dim(value.reshape(2, block, D), chip, 0, keepdims=False)
            for value in attended
        ],
        axis=0,
    )
    layer_out = kept + (home.astype(F32) + chip_swap(away).astype(F32))

    d_merged, d_merged_rows = [], {}
    gain_one_sum = shift_one_sum = skip_sum = 0.0
    for chunk in range(CHUNKS):
        halves = [
            mm(d_qkv[2 * chunk + side], qkv_matrix, NT).astype(BF16) for side in range(2)
        ]
        chip_sum = add_low(halves[0], core_swap(halves[1]))
        d_norm = chip_sum.astype(F32) + chip_swap(chip_sum).astype(F32)
        d_value, d_gain, d_shift = norm_back(
            d_norm, normed_one[chunk], inv_std_one[chunk], ln1_gain
        )
        d_value = d_attended[chunk] + d_value
        gain_one_sum = gain_one_sum + d_gain
        shift_one_sum = shift_one_sum + d_shift
        skip_sum = skip_sum + jnp.sum(d_value, axis=0)
        low = d_value.astype(BF16)
        d_merged_rows[chunk, 0] = low
        d_merged_rows[chunk, 1] = core_swap(low)
    d_w_qkv = sum(mm(norm_one[spot], d_qkv[n], TN) for n, spot in enumerate(spots))

    d_partner = whole_of(
        [mm(d_merged_rows[spot], w_skip[1], NT).astype(BF16) for spot in spots]
    )
    d_encoder_out = partner_swap(d_partner)
    d_w_skip = [
        sum(mm(piece_of(decoder_in, *spot), d_merged_rows[spot], TN) for spot in spots),
        sum(mm(partner_piece(*spot), d_merged_rows[spot], TN) for spot in spots),
    ]
    d_decoder_in = whole_of([mm(d_merged_rows[spot], w_skip[0], NT) for spot in spots])

    steps = group_steps()
    d_w_out, d_w_qkv = d_w_out.astype(BF16), d_w_qkv.astype(BF16)
    late = group_sum(
        jnp.concatenate([d_w_out, d_w_qkv.reshape(3 * local_width, D)], axis=0), steps
    )
    d_w_out, d_w_qkv = late[:local_width], late[local_width:].reshape(w_qkv.shape)
    last = group_sum(jnp.concatenate([part.astype(BF16) for part in d_w_skip], axis=0), steps)
    d_w_skip = last.reshape(w_skip.shape)

    small = jnp.stack([skip_sum, gain_one_sum, shift_one_sum, gain_two_sum, shift_two_sum]) * 0.5
    small = small + core_swap(small)
    small = small + chip_swap(small)
    small = jnp.concatenate([small, c_up_sum[None]], axis=0)
    for axis, bit in steps:
        small = small + swap(small, axis, bit)
    return (
        layer_out,
        d_decoder_in,
        d_encoder_out,
        d_w_skip.astype(F32),
        small[0],
        small[1],
        small[2],
        d_w_qkv.astype(F32),
        d_w_out.astype(F32),
        small[3],
        small[4],
        d_w_up.astype(F32),
        small[5],
        d_w_down.astype(F32),
    )


def solution(mesh):
    return jax.shard_map(
        shards,
        mesh=mesh,
        in_specs=(
            P(("section", "dp"), "tensor"),
            P(("section", "dp"), "tensor"),
            P(("section", "dp"), None),
            P(None, "tensor", None),
            P(),
            P(),
            P(),
            P(None, None, "tensor"),
            P("tensor", None),
            P(),
            P(),
            P(None, "tensor"),
            P("tensor"),
            P("tensor", None),
            P(("section", "dp"), None),
        ),
        out_specs=(
            P(("section", "dp", "tensor"), None),
            P(("section", "dp"), "tensor"),
            P(("section", "dp"), "tensor"),
            P(None, "tensor", None),
            P(),
            P(),
            P(),
            P(None, None, "tensor"),
            P("tensor", None),
            P(),
            P(),
            P(None, "tensor"),
            P("tensor"),
            P("tensor", None),
        ),
        check_vma=False,
    )
```

```python
import functools
import jax
import jax.numpy as jnp
from jax import lax
from jax.experimental import pallas as pl
from jax.experimental.pallas import tpu as pltpu
from jax.sharding import PartitionSpec as P

D = 1024
HEADS = 16
UTTS = 6
HEAD_DIM = D // HEADS
SCALE = HEAD_DIM**-0.5

EPSILON = 1e-05
FAR = 1e30
ROOT_HALF = 0.7071067811865476
INV_ROOT_TAU = 0.3989422804014327
BF16 = jnp.bfloat16
F32 = jnp.float32
NT = (((1,), (1,)), ((), ()))
NN = (((1,), (0,)), ((), ()))
TN = (((0,), (0,)), ((), ()))
CHUNKS = 2
PARTS = 4
SMALL_ROWS = 64


def mm(left, right, dims):
    return lax.dot_general(left, right, dims, preferred_element_type=F32)


def starts_of(seg):
    return [jnp.sum((seg < u).astype(jnp.int32)) for u in range(1, UTTS)]


def tile_range(starts, first, count, tile, total):
    low = jnp.int32(0)
    high = jnp.int32(total)
    for s in starts:
        low = jnp.maximum(low, jnp.where(s <= first, s, 0))
        high = jnp.minimum(high, jnp.where(s >= first + count, s, total))
    return low // tile, (high + tile - 1) // tile


def eye(n):
    r = lax.broadcasted_iota(jnp.int32, (n, n), 0)
    c = lax.broadcasted_iota(jnp.int32, (n, n), 1)
    return jnp.where(r == c, 1.0, 0.0).astype(BF16)


def far_tile(starts, seg_row, q_first, k_first, bk, bq):
    kpos = k_first + lax.broadcasted_iota(jnp.int32, (bk, bq), 0)
    qpos = q_first + lax.broadcasted_iota(jnp.int32, (bk, bq), 1)
    lo = jnp.zeros_like(seg_row)
    hi = jnp.full_like(seg_row, starts[0])
    for u in range(1, UTTS):
        lo = jnp.where(seg_row == u, starts[u - 1], lo)
        hi = jnp.where(seg_row == u, starts[u] if u < UTTS - 1 else 1 << 30, hi)
    ok = (kpos >= lo) & (kpos < hi)
    return jnp.where(ok, jnp.abs(kpos - qpos).astype(F32), FAR)


def head_masked(pair, which):
    lane = lax.broadcasted_iota(jnp.int32, pair.shape, 1)
    keep = (lane < HEAD_DIM) if which == 0 else (lane >= HEAD_DIM)
    return jnp.where(keep, pair, 0.0).astype(BF16)


def load_pieces(core, pieces, whole_ref, sems):
    copies = []
    rows = pieces[0].shape[1]
    for n, piece in enumerate(pieces):
        chunk, side = n // 2, n % 2
        for y in range(2):
            first = y * (4 * rows) + (core ^ side) * (2 * rows) + chunk * rows
            copy = pltpu.make_async_copy(
                piece.at[y], whole_ref.at[pl.ds(pl.multiple_of(first, rows), rows)], sems.at[n, y]
            )
            copy.start()
            copies.append(copy)
    for copy in copies:
        copy.wait()


def fwd_kernel(
    heads, bk, chunk, core_ref, slope_ref, seg_ref, w_ref, q00, q01, q10, q11, *refs
):
    out_ref, lse_ref, own_ref, *sib_refs = refs[-9 - PARTS : -6]
    qkv_ref, vt_ref, acc_ref, s_ref, top_ref, sems = refs[-6:]
    strip = sib_refs[0].shape[0]
    total = seg_ref.shape[1]
    width = heads * HEAD_DIM
    bq = out_ref.shape[1] // 2
    core = core_ref[0]
    load_pieces(core, (q00, q01, q10, q11), qkv_ref, sems)
    starts = starts_of(seg_ref[...])
    ident = eye(width)

    def prep(j, c):
        at = pl.ds(pl.multiple_of(j * bk, bk), bk)
        vt = mm(ident, qkv_ref[at, 2 * width : 3 * width], NT).astype(BF16)
        for h in range(heads):
            vt_ref[h * 80 : h * 80 + 64, at] = vt[h * 64 : (h + 1) * 64]
            vt_ref[h * 80 + 64 : (h + 1) * 80, at] = jnp.ones((16, bk), BF16)
        return c

    lax.fori_loop(0, total // bk, prep, 0)

    def q_step(i, c):
        side, y = i // 2, i % 2
        qi = pl.multiple_of(y * (4 * bq) + (core ^ side) * (2 * bq) + chunk * bq, bq)
        lo, hi = tile_range(starts, qi, bq, bk, total)
        seg_row = seg_ref[:, pl.ds(qi, bq)]
        acc_ref[...] = jnp.zeros_like(acc_ref)
        top_ref[...] = jnp.full_like(top_ref, -3e38)
        qs = []
        for h in range(heads):
            p = h // 2
            qp = qkv_ref[pl.ds(qi, bq), p * 128 : (p + 1) * 128].astype(F32) * SCALE
            qs.append(head_masked(qp, h % 2))

        def score_step(j, c):
            kj = pl.multiple_of(j * bk, bk)
            far = far_tile(starts, seg_row, qi, kj, bk, bq)
            for h in range(heads):
                p = h // 2
                kp = qkv_ref[pl.ds(kj, bk), width + p * 128 : width + (p + 1) * 128]
                s = mm(kp, qs[h], NT) - far * slope_ref[h]
                s_ref[h, pl.ds(kj, bk)] = s
                top_ref[h] = jnp.maximum(top_ref[h], jnp.max(s.reshape(bk // 8, 8, bq), axis=0))
            return c

        lax.fori_loop(lo, hi, score_step, 0)
        tops = [jnp.max(top_ref[h], axis=0, keepdims=True) for h in range(heads)]

        def mix_step(j, c):
            kj = pl.multiple_of(j * bk, bk)
            for h in range(heads):
                e = jnp.exp(s_ref[h, pl.ds(kj, bk)] - tops[h]).astype(BF16)
                hs = slice(h * 80, (h + 1) * 80)
                acc_ref[hs] = acc_ref[hs] + mm(vt_ref[hs, pl.ds(kj, bk)], e, NN)
            return c

        lax.fori_loop(lo, hi, mix_step, 0)
        outs = []
        for h in range(heads):
            whole = acc_ref[h * 80 + 64 : h * 80 + 65]
            outs.append((acc_ref[h * 80 : h * 80 + 64] * (1.0 / whole)).astype(BF16))
            lse_ref[i, h : h + 1] = tops[h] + jnp.log(whole)
        ot = jnp.concatenate(outs, axis=0)
        here = pl.ds(pl.multiple_of(y * bq, bq), bq)
        mixed = mm(eye(bq), ot, NT).astype(BF16)
        out_ref[side, here] = mixed
        part = mm(mixed, w_ref[...], NN).astype(BF16)

        @pl.when(side == 0)
        def _():
            own_ref[here] = part

        for n, sib_ref in enumerate(sib_refs):
            first = n * strip % bq

            @pl.when((side == 1) & (y == n * strip // bq))
            def _(sib_ref=sib_ref, first=first):
                sib_ref[...] = part[first : first + strip]

        return c

    lax.fori_loop(0, 4, q_step, 0)


def attend(chunk, core, slopes, seg, w_out, pieces, ahead=()):
    total = seg.shape[1]
    rows = pieces[0].shape[1]
    heads = pieces[0].shape[2] // (3 * HEAD_DIM)
    width = heads * HEAD_DIM
    bk = 256
    smem = pl.BlockSpec(memory_space=pltpu.SMEM)
    vmem = pl.BlockSpec(memory_space=pltpu.VMEM)
    hbm = pl.BlockSpec(memory_space=pl.ANY)
    return pl.pallas_call(
        functools.partial(fwd_kernel, heads, bk, chunk),
        out_shape=(
            jax.ShapeDtypeStruct((2, 2 * rows, width), BF16),
            jax.ShapeDtypeStruct((4, heads, rows), F32),
            jax.ShapeDtypeStruct((2 * rows, w_out.shape[1]), BF16),
        )
        + (jax.ShapeDtypeStruct((2 * rows // PARTS, w_out.shape[1]), BF16),) * PARTS,
        in_specs=[smem, smem, vmem, vmem] + [hbm] * (4 + len(ahead)),
        out_specs=(vmem,) * (3 + PARTS),
        scratch_shapes=[
            pltpu.VMEM((total, 3 * width), BF16),
            pltpu.VMEM((heads * 80, total), BF16),
            pltpu.VMEM((heads * 80, rows), F32),
            pltpu.VMEM((heads, total, rows), F32),
            pltpu.VMEM((heads, 8, rows), F32),
            pltpu.SemaphoreType.DMA((4, 2)),
        ],
        compiler_params=pltpu.CompilerParams(vmem_limit_bytes=28 << 20),
        name="attend",
    )(core, slopes, seg, w_out, *pieces, *ahead)


def bwd_kernel(heads, bk, chunk, *refs):
    core_ref, slope_ref, seg_ref, q00, q01, q10, q11, do0, do1, o_ref, lse_ref = refs[:11]
    if chunk == 0:
        dq_ref, dkv_ref = refs[-9:-7]
    else:
        dq_in, dkv_in = refs[11:13]
        dqkv_ref = refs[-8]
    qkv_ref, kt_ref, dqt_ref, dk_ref, dv_ref, delta_ref, sems = refs[-7:]
    total = seg_ref.shape[1]
    width = heads * HEAD_DIM
    bq = o_ref.shape[1] // 2
    core = core_ref[0]
    load_pieces(core, (q00, q01, q10, q11), qkv_ref, sems)
    starts = starts_of(seg_ref[...])
    ident = eye(width)
    hr = lax.broadcasted_iota(jnp.int32, (8, width), 0)
    hc = lax.broadcasted_iota(jnp.int32, (8, width), 1)
    pick = jnp.where(hr == hc // HEAD_DIM, 1.0, 0.0)

    def prep(j, c):
        at = pl.ds(pl.multiple_of(j * bk, bk), bk)
        kj = qkv_ref[at, width : 2 * width]
        kt_ref[:, at] = (mm(ident, kj, NT) * SCALE).astype(BF16)
        if chunk == 0:
            dk_ref[at] = jnp.zeros((bk, width), F32)
            dv_ref[at] = jnp.zeros((bk, width), F32)
        else:
            dk_ref[at] = dkv_in[at, :width]
            dv_ref[at] = dkv_in[at, width:]
        return c

    lax.fori_loop(0, total // bk, prep, 0)
    for side, do_ref in enumerate((do0, do1)):
        for y in range(2):
            at = slice(y * bq, (y + 1) * bq)
            prod = do_ref[at].astype(F32) * o_ref[side, at].astype(F32)
            delta_ref[side * 2 + y] = lax.dot_general(
                pick, prod, NT, precision=lax.Precision.HIGHEST, preferred_element_type=F32
            )

    for side, do_ref in enumerate((do0, do1)):

        def q_step(y, c, side=side, do_ref=do_ref):
            i = side * 2 + y
            qi = pl.multiple_of(y * (4 * bq) + (core ^ side) * (2 * bq) + chunk * bq, bq)
            here = pl.ds(pl.multiple_of(y * bq, bq), bq)
            lo, hi = tile_range(starts, qi, bq, bk, total)
            seg_row = seg_ref[:, pl.ds(qi, bq)]
            dqt_ref[...] = jnp.zeros_like(dqt_ref)
            qs, dos = [], []
            for h in range(heads):
                p = h // 2
                qp = qkv_ref[pl.ds(qi, bq), p * 128 : (p + 1) * 128].astype(F32) * SCALE
                qs.append(head_masked(qp, h % 2))
                dp = do_ref[here, p * 128 : (p + 1) * 128].astype(F32)
                dos.append(head_masked(dp, h % 2))
            lses = [lse_ref[i, h : h + 1] for h in range(heads)]
            deltas = [delta_ref[i, h : h + 1] for h in range(heads)]

            def k_step(j, c):
                kj = pl.multiple_of(j * bk, bk)
                at = pl.ds(kj, bk)
                far = far_tile(starts, seg_row, qi, kj, bk, bq)
                for p in range(heads // 2):
                    cols = slice(p * 128, (p + 1) * 128)
                    kp = qkv_ref[at, width + p * 128 : width + (p + 1) * 128]
                    vp = qkv_ref[at, 2 * width + p * 128 : 2 * width + (p + 1) * 128]
                    dv = dv_ref[at, cols]
                    dk = dk_ref[at, cols]
                    for h in (2 * p, 2 * p + 1):
                        s = mm(kp, qs[h], NT) - far * slope_ref[h]
                        w = jnp.exp(s - lses[h])
                        dw = mm(vp, dos[h], NT)
                        ds = (w * (dw - deltas[h])).astype(BF16)
                        dv = dv + mm(w.astype(BF16), dos[h], NN)
                        dk = dk + mm(ds, qs[h], NN)
                        hs = slice(h * HEAD_DIM, (h + 1) * HEAD_DIM)
                        dqt_ref[hs] = dqt_ref[hs] + mm(kt_ref[hs, at], ds, NN)
                    dv_ref[at, cols] = dv
                    dk_ref[at, cols] = dk
                return c

            lax.fori_loop(lo, hi, k_step, 0)
            dq = mm(eye(bq), dqt_ref[...].astype(BF16), NT).astype(BF16)
            if chunk == 0:
                dq_ref[side, here] = dq
            else:
                dqkv_ref[2 + side, here, :width] = dq
            return c

        lax.fori_loop(0, 2, q_step, 0)

    if chunk == 0:

        def finish(j, c):
            at = pl.ds(pl.multiple_of(j * bk, bk), bk)
            dkv_ref[at, :width] = dk_ref[at]
            dkv_ref[at, width:] = dv_ref[at]
            return c

        lax.fori_loop(0, total // bk, finish, 0)
    else:
        for side in range(2):
            dqkv_ref[side, :, :width] = dq_in[side]
        for n in range(4):
            part, side = n // 2, n % 2
            for y in range(2):
                first = y * (4 * bq) + (core ^ side) * (2 * bq) + part * bq
                at = pl.ds(pl.multiple_of(first, bq), bq)
                here = slice(y * bq, (y + 1) * bq)
                dqkv_ref[n, here, width : 2 * width] = dk_ref[at].astype(BF16)
                dqkv_ref[n, here, 2 * width :] = dv_ref[at].astype(BF16)


def attend_back(chunk, core, slopes, seg, pieces, d_heads, heads_out, lse, before=(), ahead=()):
    total = seg.shape[1]
    rows = pieces[0].shape[1]
    heads = pieces[0].shape[2] // (3 * HEAD_DIM)
    width = heads * HEAD_DIM
    bk = 256
    smem = pl.BlockSpec(memory_space=pltpu.SMEM)
    vmem = pl.BlockSpec(memory_space=pltpu.VMEM)
    hbm = pl.BlockSpec(memory_space=pl.ANY)
    if chunk == 0:
        out_shape = (
            jax.ShapeDtypeStruct((2, 2 * rows, width), BF16),
            jax.ShapeDtypeStruct((total, 2 * width), F32),
        )
        out_specs = (vmem, vmem)
    else:
        out_shape = jax.ShapeDtypeStruct((4, 2 * rows, 3 * width), BF16)
        out_specs = vmem
    return pl.pallas_call(
        functools.partial(bwd_kernel, heads, bk, chunk),
        out_shape=out_shape,
        in_specs=[smem, smem, vmem] + [hbm] * 4 + [vmem] * (4 + len(before)) + [hbm] * len(ahead),
        out_specs=out_specs,
        scratch_shapes=[
            pltpu.VMEM((total, 3 * width), BF16),
            pltpu.VMEM((width, total), BF16),
            pltpu.VMEM((width, rows), F32),
            pltpu.VMEM((total, width), F32),
            pltpu.VMEM((total, width), F32),
            pltpu.VMEM((4, 8, rows), F32),
            pltpu.SemaphoreType.DMA((4, 2)),
        ],
        compiler_params=pltpu.CompilerParams(vmem_limit_bytes=34 << 20),
        name="attend_back",
    )(core, slopes, seg, *pieces, *d_heads, heads_out, lse, *before, *ahead)


def swap(value, axis, bit):
    pairs = [(source, source ^ (1 << bit)) for source in range(lax.axis_size(axis))]
    return lax.ppermute(value, axis, pairs)


core_swap = functools.partial(swap, axis="tensor", bit=0)
chip_swap = functools.partial(swap, axis="tensor", bit=1)
partner_swap = functools.partial(swap, axis="section", bit=0)


def add_low(*terms):
    return sum(term.astype(F32) for term in terms).astype(BF16)


def group_steps():
    steps = [("section", 0)]
    for bit in range((lax.axis_size("dp") - 1).bit_length()):
        steps.append(("dp", bit))
    return steps


def gate(values, *ahead):
    hbm = pl.BlockSpec(memory_space=pl.ANY)
    many = isinstance(values, (list, tuple))
    values = tuple(values) if many else (values,)
    out = pl.pallas_call(
        lambda *refs: None,
        out_shape=tuple(jax.ShapeDtypeStruct(value.shape, value.dtype) for value in values),
        in_specs=[hbm] * (len(values) + len(ahead)),
        out_specs=(hbm,) * len(values),
        input_output_aliases={n: n for n in range(len(values))},
        name="gate",
    )(*values, *ahead)
    return out if many else out[0]


class GroupSum:
    def __init__(self, value, steps):
        self.value = value
        self.ways = list(steps) + list(reversed(steps))
        self.sides = [(lax.axis_index(axis) >> bit) & 1 for axis, bit in steps]
        self.send()

    def send(self):
        self.done = len(self.ways) == 0
        if self.done:
            return
        axis, bit = self.ways[0]
        self.halving = len(self.ways) > len(self.sides)
        sent = self.value
        if self.halving:
            index = len(self.ways) - len(self.sides)
            mine = self.sides[len(self.sides) - index]
            halves = self.value.reshape(2, self.value.shape[0] // 2, self.value.shape[1])
            sent = lax.dynamic_index_in_dim(halves, 1 - mine, 0, keepdims=False)
            self.kept = lax.dynamic_index_in_dim(halves, mine, 0, keepdims=False)
        self.came = swap(sent, axis, bit)

    def step(self, *ahead):
        came = gate(self.came, *ahead) if ahead else self.came
        if self.halving:
            self.value = add_low(self.kept, came)
        else:
            first = self.sides[len(self.ways) - 1] == 0
            self.value = jnp.concatenate(
                [jnp.where(first, self.value, came), jnp.where(first, came, self.value)], axis=0
            )
        self.ways.pop(0)
        self.send()
        return self.value

    def finish(self):
        while not self.done:
            self.step()
        return self.value


def row_stats(values):
    row_mean = jnp.mean(values, axis=-1, keepdims=True)
    centered = values - row_mean
    inv_std = lax.rsqrt(jnp.mean(centered * centered, axis=-1, keepdims=True) + EPSILON)
    return centered * inv_std, inv_std


def norm_kernel(base_ref, mine_ref, other_ref, gain_ref, shift_ref, *refs):
    value_ref, low_ref = refs[-2:]
    value = base_ref[...] + (mine_ref[...].astype(F32) + other_ref[...].astype(F32))
    value_ref[...] = value
    normed, _ = row_stats(value)
    low_ref[...] = (normed * gain_ref[...] + shift_ref[...]).astype(BF16)


def norm_rows(base, mine, other, gain, shift, ahead=(), tile=128):
    rows, width = mine.shape
    wide = pl.BlockSpec((tile, width), lambda i: (i, 0))
    one = pl.BlockSpec((1, width), lambda i: (0, 0))
    return pl.pallas_call(
        norm_kernel,
        grid=(rows // tile,),
        out_shape=(
            jax.ShapeDtypeStruct((rows, width), F32),
            jax.ShapeDtypeStruct((rows, width), BF16),
        ),
        in_specs=[wide if base.shape[0] == rows else one, wide, wide, one, one]
        + [pl.BlockSpec(memory_space=pl.ANY)] * len(ahead),
        out_specs=(wide, wide),
        compiler_params=pltpu.CompilerParams(vmem_limit_bytes=24 << 20),
        name="norm_rows",
    )(base, mine, other, gain[None], shift[None], *ahead)


def back_kernel(past_ref, value_ref, mine_ref, other_ref, gain_ref, sums_in, *refs):
    grad_ref, low_ref, sums_ref = refs[-3:]
    d_output = mine_ref[...].astype(F32) + other_ref[...].astype(F32)
    normed, inv_std = row_stats(value_ref[...])
    d_normed = d_output * gain_ref[...]
    grad = past_ref[...].astype(F32) + inv_std * (
        d_normed
        - jnp.mean(d_normed, axis=-1, keepdims=True)
        - normed * jnp.mean(d_normed * normed, axis=-1, keepdims=True)
    )
    grad_ref[...] = grad
    low_ref[...] = grad.astype(BF16)

    @pl.when(pl.program_id(0) == 0)
    def _():
        sums_ref[...] = sums_in[...]

    for n, terms in enumerate((d_output * normed, d_output, grad)):
        part = jnp.sum(terms.reshape(-1, 8, terms.shape[1]), axis=0)
        sums_ref[n] = sums_ref[n] + part


def norm_back_rows(past, value, mine, other, gain, sums, ahead=(), tile=128):
    rows, width = mine.shape
    wide = pl.BlockSpec((tile, width), lambda i: (i, 0))
    one = pl.BlockSpec((1, width), lambda i: (0, 0))
    kept = pl.BlockSpec((3, 8, width), lambda i: (0, 0, 0))
    return pl.pallas_call(
        back_kernel,
        grid=(rows // tile,),
        out_shape=(
            jax.ShapeDtypeStruct((rows, width), F32),
            jax.ShapeDtypeStruct((rows, width), BF16),
            jax.ShapeDtypeStruct((3, 8, width), F32),
        ),
        in_specs=[wide, wide, wide, wide, one, kept]
        + [pl.BlockSpec(memory_space=pl.ANY)] * len(ahead),
        out_specs=(wide, wide, kept),
        compiler_params=pltpu.CompilerParams(vmem_limit_bytes=24 << 20),
        name="norm_back",
    )(past, value, mine, other, gain[None], sums, *ahead)


def feed_kernel(chunk, core_ref, up_ref, bias_ref, down_ref, own_ref, sib_ref, cot_ref, *refs):
    act_ref, grads_ref, bias_out, dn_own, *dn_sib = refs[-8 - PARTS : -4]
    cot_v, d_pre_ref, bias_acc, sems = refs[-4:]
    rows = own_ref.shape[0] // 2
    core = core_ref[0]
    copies = []
    for i in range(4):
        side, y = i // 2, i % 2
        first = y * (4 * rows) + (core ^ side) * (2 * rows) + chunk * rows
        copy = pltpu.make_async_copy(
            cot_ref.at[pl.ds(pl.multiple_of(first, rows), rows)],
            cot_v.at[i * rows : (i + 1) * rows],
            sems.at[i],
        )
        copy.start()
        copies.append(copy)
    bias_acc[...] = refs[1][...] if chunk else jnp.zeros_like(bias_acc)
    for copy in copies:
        copy.wait()
    for side, n_ref in enumerate((own_ref, sib_ref)):
        for y in range(2):
            here = slice(y * rows, (y + 1) * rows)
            there = slice((side * 2 + y) * rows, (side * 2 + y + 1) * rows)
            pre = mm(n_ref[here], up_ref[...], NN) + bias_ref[...]
            d_act = mm(cot_v[there], down_ref[...], NT)
            cdf = 0.5 + 0.5 * lax.erf(pre * ROOT_HALF)
            act_ref[side, here] = (pre * cdf).astype(BF16)
            slope = cdf + pre * jnp.exp(-0.5 * pre * pre) * INV_ROOT_TAU
            d_pre = (d_act * slope).astype(BF16)
            d_pre_ref[there] = d_pre
            parts = d_pre.astype(F32).reshape(-1, 8, d_pre.shape[1])
            bias_acc[...] = bias_acc[...] + jnp.sum(parts, axis=0)
            d_norm = mm(d_pre, up_ref[...], NT).astype(BF16)
            if side == 0:
                dn_own[here] = d_norm
            else:
                strip = dn_sib[0].shape[0]
                for n in range(rows // strip):
                    dn_sib[y * rows // strip + n][...] = d_norm[n * strip : (n + 1) * strip]
    bias_out[...] = bias_acc[...]
    own_rows, sib_rows = slice(0, 2 * rows), slice(2 * rows, 4 * rows)
    units = act_ref.shape[2]
    strip = 256
    for first in range(0, units, strip):
        at = slice(first, first + strip)
        total = mm(act_ref[0, :, at], cot_v[own_rows], TN) + mm(
            act_ref[1, :, at], cot_v[sib_rows], TN
        )
        if chunk:
            total = total + refs[0][at]
        grads_ref[at] = total.astype(grads_ref.dtype)
    for first in range(0, own_ref.shape[1], strip):
        at, to = slice(first, first + strip), slice(units + first, units + first + strip)
        total = mm(own_ref[:, at], d_pre_ref[own_rows], TN) + mm(
            sib_ref[:, at], d_pre_ref[sib_rows], TN
        )
        if chunk:
            total = total + refs[0][to]
        grads_ref[to] = total.astype(grads_ref.dtype)


def feed(chunk, core, w_up, c_up, w_down, own, sib, cot, before=()):
    rows, width = own.shape
    units = w_up.shape[1]
    vmem = pl.BlockSpec(memory_space=pltpu.VMEM)
    return pl.pallas_call(
        functools.partial(feed_kernel, chunk),
        out_shape=(
            jax.ShapeDtypeStruct((2, rows, units), BF16),
            jax.ShapeDtypeStruct((units + width, width), BF16 if chunk else F32),
            jax.ShapeDtypeStruct((8, units), F32),
            jax.ShapeDtypeStruct((rows, width), BF16),
        )
        + (jax.ShapeDtypeStruct((rows // PARTS, width), BF16),) * PARTS,
        in_specs=[pl.BlockSpec(memory_space=pltpu.SMEM)]
        + [vmem] * 5
        + [pl.BlockSpec(memory_space=pl.ANY)]
        + [vmem] * len(before),
        out_specs=(vmem,) * (4 + PARTS),
        scratch_shapes=[
            pltpu.VMEM((2 * rows, width), BF16),
            pltpu.VMEM((2 * rows, units), BF16),
            pltpu.VMEM((8, units), F32),
            pltpu.SemaphoreType.DMA((4,)),
        ],
        compiler_params=pltpu.CompilerParams(vmem_limit_bytes=44 << 20),
        name="feed",
    )(core, w_up, c_up[None], w_down, own, sib, cot, *before)


def row_copies(core, chunk, rows, source, target, sems, reverse=False):
    copies = []
    for i in range(4):
        side, y = i // 2, i % 2
        first = y * (4 * rows) + (core ^ side) * (2 * rows) + chunk * rows
        whole = pl.ds(pl.multiple_of(first, rows), rows)
        here = slice(i * rows, (i + 1) * rows)
        if reverse:
            copy = pltpu.make_async_copy(source.at[here], target.at[whole], sems.at[i])
        else:
            copy = pltpu.make_async_copy(source.at[whole], target.at[here], sems.at[i])
        copy.start()
        copies.append(copy)
    return copies


def skip_grad_kernel(chunk, core_ref, own_ref, sib_ref, dec_ref, enc_ref, *refs):
    out_ref, dec_v, enc_v, sems = refs[-4:]
    rows = own_ref.shape[0] // 2
    width = dec_v.shape[1]
    copies = row_copies(core_ref[0], chunk, rows, dec_ref, dec_v, sems.at[0])
    for i in range(4):
        side, y = i // 2, i % 2
        first = (y * 2 + (core_ref[0] ^ side)) * rows
        copy = pltpu.make_async_copy(
            enc_ref.at[pl.ds(pl.multiple_of(first, rows), rows)],
            enc_v.at[i * rows : (i + 1) * rows],
            sems.at[1, i],
        )
        copy.start()
        copies.append(copy)
    for copy in copies:
        copy.wait()
    half = 2 * rows
    for n, part in enumerate((dec_v, enc_v)):
        at = slice(n * width, (n + 1) * width)
        total = mm(part[:half], own_ref[...], TN) + mm(part[half:], sib_ref[...], TN)
        if chunk:
            total = total + refs[0][at]
        out_ref[at] = total.astype(out_ref.dtype)
    if chunk:
        small = refs[1][...]
        out_ref[2 * width :] = jnp.zeros_like(out_ref[2 * width :])
        out_ref[2 * width : 2 * width + 16] = small.astype(out_ref.dtype)


def skip_grad(chunk, core, own, sib, dec, enc, before=()):
    rows, cols = own.shape
    width = dec.shape[1]
    vmem = pl.BlockSpec(memory_space=pltpu.VMEM)
    hbm = pl.BlockSpec(memory_space=pl.ANY)
    return pl.pallas_call(
        functools.partial(skip_grad_kernel, chunk),
        out_shape=jax.ShapeDtypeStruct(
            (2 * width + (SMALL_ROWS if chunk else 0), cols), BF16 if chunk else F32
        ),
        in_specs=[pl.BlockSpec(memory_space=pltpu.SMEM), vmem, vmem, hbm, hbm]
        + [vmem] * len(before),
        out_specs=vmem,
        scratch_shapes=[
            pltpu.VMEM((2 * rows, width), BF16),
            pltpu.VMEM((2 * rows, width), BF16),
            pltpu.SemaphoreType.DMA((2, 4)),
        ],
        compiler_params=pltpu.CompilerParams(vmem_limit_bytes=24 << 20),
        name="skip_grad",
    )(core, own, sib, dec, enc, *before)


def skip_back_kernel(chunk, core_ref, w_ref, own_ref, sib_ref, *refs):
    back_ref, whole_ref, held, sems = refs[-4:]
    rows = own_ref.shape[0] // 2
    for side, part in enumerate((own_ref, sib_ref)):
        at = slice(side * 2 * rows, (side + 1) * 2 * rows)
        back_ref[at] = mm(part[...], w_ref[1], NT).astype(BF16)
        held[at] = mm(part[...], w_ref[0], NT)
    for copy in row_copies(core_ref[0], chunk, rows, held, whole_ref, sems, reverse=True):
        copy.wait()


def skip_back(chunk, core, w_skip, own, sib, group_rows, before=(), ahead=()):
    rows = own.shape[0]
    width = w_skip.shape[1]
    vmem = pl.BlockSpec(memory_space=pltpu.VMEM)
    hbm = pl.BlockSpec(memory_space=pl.ANY)
    return pl.pallas_call(
        functools.partial(skip_back_kernel, chunk),
        out_shape=(
            jax.ShapeDtypeStruct((2 * rows, width), BF16),
            jax.ShapeDtypeStruct((group_rows, width), F32),
        ),
        in_specs=[pl.BlockSpec(memory_space=pltpu.SMEM), vmem, vmem, vmem]
        + [hbm] * (len(before) + len(ahead)),
        out_specs=(vmem, hbm),
        scratch_shapes=[pltpu.VMEM((2 * rows, width), F32), pltpu.SemaphoreType.DMA((4,))],
        input_output_aliases={4: 1} if before else {},
        compiler_params=pltpu.CompilerParams(vmem_limit_bytes=24 << 20),
        name="skip_back",
    )(core, w_skip, own, sib, *before, *ahead)


def restore_kernel(core_ref, *refs):
    out_ref = refs[-1]
    for chunk, part in enumerate(refs[:-1]):
        rows = part.shape[0] // 4
        for i in range(4):
            side, y = i // 2, i % 2
            first = y * (4 * rows) + (core_ref[0] ^ side) * (2 * rows) + chunk * rows
            out_ref[pl.ds(pl.multiple_of(first, rows), rows)] = part[i * rows : (i + 1) * rows]


def restore(core, parts):
    vmem = pl.BlockSpec(memory_space=pltpu.VMEM)
    rows, width = parts[0].shape
    return pl.pallas_call(
        restore_kernel,
        out_shape=jax.ShapeDtypeStruct((rows * len(parts), width), parts[0].dtype),
        in_specs=[pl.BlockSpec(memory_space=pltpu.SMEM)] + [vmem] * len(parts),
        out_specs=vmem,
        compiler_params=pltpu.CompilerParams(vmem_limit_bytes=12 << 20),
        name="restore",
    )(core, *parts)


def skip_kernel(chunk, core_ref, w_ref, dec_ref, enc_ref, own_ref, *refs):
    sib_refs, (dec_v, enc_v, sems) = refs[:PARTS], refs[PARTS:]
    rows = own_ref.shape[0] // 2
    copies = row_copies(core_ref[0], chunk, rows, dec_ref, dec_v, sems.at[0])
    for i in range(4):
        side, y = i // 2, i % 2
        first = (y * 2 + (core_ref[0] ^ side)) * rows
        copy = pltpu.make_async_copy(
            enc_ref.at[pl.ds(pl.multiple_of(first, rows), rows)],
            enc_v.at[i * rows : (i + 1) * rows],
            sems.at[1, i],
        )
        copy.start()
        copies.append(copy)
    for copy in copies:
        copy.wait()
    half = 2 * rows
    strip = half // PARTS
    for n, sib_ref in enumerate(sib_refs):
        at = slice(half + n * strip, half + (n + 1) * strip)
        sib_ref[...] = (mm(dec_v[at], w_ref[0], NN) + mm(enc_v[at], w_ref[1], NN)).astype(BF16)
    own_ref[...] = (mm(dec_v[:half], w_ref[0], NN) + mm(enc_v[:half], w_ref[1], NN)).astype(BF16)


def skip(chunk, core, w_skip, dec, enc):
    rows = enc.shape[0] // 2
    width, cols = w_skip.shape[1:]
    vmem = pl.BlockSpec(memory_space=pltpu.VMEM)
    hbm = pl.BlockSpec(memory_space=pl.ANY)
    return pl.pallas_call(
        functools.partial(skip_kernel, chunk),
        out_shape=(jax.ShapeDtypeStruct((rows, cols), BF16),)
        + (jax.ShapeDtypeStruct((rows // PARTS, cols), BF16),) * PARTS,
        in_specs=[pl.BlockSpec(memory_space=pltpu.SMEM), vmem, hbm, hbm],
        out_specs=(vmem,) * (1 + PARTS),
        scratch_shapes=[
            pltpu.VMEM((2 * rows, width), BF16),
            pltpu.VMEM((2 * rows, width), BF16),
            pltpu.SemaphoreType.DMA((2, 4)),
        ],
        compiler_params=pltpu.CompilerParams(vmem_limit_bytes=16 << 20),
        name="skip",
    )(core, w_skip, dec, enc)


def shards(
    decoder_in,
    encoder_out,
    segments,
    w_skip,
    b_skip,
    ln1_gain,
    ln1_bias,
    w_qkv,
    w_out,
    ln2_gain,
    ln2_bias,
    w_up,
    c_up,
    w_down,
    cotangent,
):
    group_rows = decoder_in.shape[0]
    tensor_rank = lax.axis_index("tensor")
    core = tensor_rank & 1
    chip = tensor_rank >> 1
    heads_here = HEADS // lax.axis_size("tensor")
    local_width = heads_here * HEAD_DIM
    block = group_rows // (4 * CHUNKS)
    qkv_matrix = w_qkv.reshape(D, 3 * local_width)
    core_scalar = core.reshape(1).astype(jnp.int32)
    slopes = jnp.exp2(
        -8.0
        * (tensor_rank * heads_here + jnp.arange(heads_here, dtype=jnp.int32) + 1).astype(F32)
        / HEADS
    )
    spots = [(chunk, side) for chunk in range(CHUNKS) for side in range(2)]

    def piece_of(array, chunk, side):
        width = array.shape[-1]
        parts = array.reshape(2, 2, CHUNKS, block, width)[:, :, chunk]
        return lax.dynamic_index_in_dim(parts, core ^ side, 1, keepdims=False).reshape(
            2 * block, width
        )

    cot = [piece_of(cotangent, chunk, 0) for chunk in range(CHUNKS)]
    encoder_parts = encoder_out.reshape(2, 2, CHUNKS, block, encoder_out.shape[1])
    partner = [
        partner_swap(encoder_parts[:, :, chunk].reshape(4 * block, -1)) for chunk in range(CHUNKS)
    ]

    def chip_total(half):
        sent = core_swap(half(1).astype(BF16))
        return (half(0) + sent.astype(F32)).astype(BF16)

    merged, norm_one, qkv = [], {}, {}
    sums = []
    for chunk in range(CHUNKS):
        own, *sib = skip(chunk, core_scalar, w_skip, decoder_in, partner[chunk])
        sums.append(add_low(own, jnp.concatenate([core_swap(part) for part in sib], axis=0)))
        if chunk + 1 < CHUNKS:
            partner[chunk + 1] = gate(partner[chunk + 1], sums[chunk])
    others = [chip_swap(part) for part in sums]
    ahead = (qkv_matrix, *sums)
    for chunk in range(CHUNKS):
        value, normal = norm_rows(
            b_skip[None], sums[chunk], others[chunk], ln1_gain, ln1_bias, ahead
        )
        merged.append(value)
        norm_one[chunk, 0] = normal
        norm_one[chunk, 1] = core_swap(normal)
        for side in range(2):
            qkv[chunk, side] = jnp.dot(
                norm_one[chunk, side], qkv_matrix, preferred_element_type=F32
            ).astype(BF16)
        ahead = (qkv[chunk, 0], qkv[chunk, 1], *cot)
    qkv_pieces = [qkv[spot].reshape(2, block, 3 * local_width) for spot in spots]

    heads_out, lse, sums = [], [], []
    for chunk in range(CHUNKS):
        mixed, log_total, own, *sib = attend(
            chunk, core_scalar, slopes, segments, w_out, qkv_pieces, sums
        )
        heads_out.append(mixed)
        lse.append(log_total)
        sums.append(add_low(own, jnp.concatenate([core_swap(part) for part in sib], axis=0)))
    others = [chip_swap(part) for part in sums]

    attended, activated, d_sums, d_others = [], [], [], []
    ahead = tuple(sums)
    grads = ()
    for chunk in range(CHUNKS):
        value, normal = norm_rows(
            merged[chunk], sums[chunk], others[chunk], ln2_gain, ln2_bias, ahead
        )
        attended.append(value)
        acts, weights_sum, bias_sum, own, *sib = feed(
            chunk, core_scalar, w_up, c_up, w_down, normal, core_swap(normal), cotangent, grads
        )
        grads = (weights_sum, bias_sum)
        activated.append(acts)
        sib = gate([core_swap(part) for part in sib], d_others[chunk - 1] if chunk else others[1])
        d_sums.append(add_low(own, jnp.concatenate(sib, axis=0)))
        d_others.append(chip_swap(d_sums[chunk]))
        ahead = (d_sums[chunk],)
    d_w_ff, c_up_sum = grads
    both = ("section", "dp")
    d_w_ff = lax.psum_scatter(
        gate(d_w_ff, d_sums[-1]), both, scatter_dimension=0, tiled=True
    )

    d_attended, d_attended_rows = [], {}
    sums_two = jnp.zeros((3, 8, D), F32)
    before = ()
    for chunk in range(CHUNKS):
        value, low, sums_two = norm_back_rows(
            cot[chunk], attended[chunk], d_sums[chunk], d_others[chunk], ln2_gain, sums_two,
            ahead,
        )
        d_attended.append(value)
        d_attended_rows[chunk, 0] = low
        d_attended_rows[chunk, 1] = core_swap(low)
        d_heads = [
            mm(d_attended_rows[chunk, side], w_out, NT).astype(BF16) for side in range(2)
        ]
        before = attend_back(
            chunk, core_scalar, slopes, segments, qkv_pieces, d_heads, heads_out[chunk],
            lse[chunk], before,
        )
        ahead = (before[0],)
    d_qkv = before

    steps = group_steps()
    sums = [
        chip_total(lambda side: mm(d_qkv[2 * chunk + side], qkv_matrix, NT))
        for chunk in range(CHUNKS)
    ]
    others = [chip_swap(sums[0])]
    others.append(chip_swap(gate(sums[1], others[0])))
    kept = gate(heads_out + [norm_one[spot] for spot in spots] + [d_w_ff], *sums)
    heads_out, norm_one, d_w_ff = kept[:CHUNKS], dict(zip(spots, kept[CHUNKS:-1])), kept[-1]
    d_w_ff = lax.all_gather(d_w_ff, both, axis=0, tiled=True)
    d_w_qkv = sum(mm(norm_one[spot], d_qkv[n], TN) for n, spot in enumerate(spots)).astype(BF16)
    d_w_out = sum(
        mm(heads_out[spot[0]][spot[1]], d_attended_rows[spot], TN) for spot in spots
    ).astype(BF16)
    slab = jnp.concatenate([d_w_out, d_w_qkv.reshape(3 * local_width, D)], axis=0)
    late = GroupSum(slab, steps)
    activated = gate(activated, slab)

    down = [
        chip_total(
            lambda side: jnp.dot(activated[chunk][side], w_down, preferred_element_type=F32)
        )
        for chunk in range(CHUNKS)
    ]

    sums_one = jnp.zeros((3, 8, D), F32)
    ahead = (*sums, d_w_qkv, d_w_out)
    for chunk in range(CHUNKS):
        _, low, sums_one = norm_back_rows(
            d_attended[chunk], merged[chunk], sums[chunk], others[chunk], ln1_gain, sums_one, ahead
        )
        if chunk == 0:
            sib = gate(core_swap(low), late.step())
            d_w_skip = skip_grad(chunk, core_scalar, low, sib, decoder_in, partner[chunk])
            returned, d_decoder_in = skip_back(
                chunk, core_scalar, w_skip, low, sib, group_rows
            )
            d_encoder = [returned]
            ahead = (d_w_skip, returned, late.step(), *down)
        else:
            sib = core_swap(low)
            small = jnp.sum(jnp.concatenate([sums_one, sums_two], axis=0), axis=1) * 0.5
            small = small + core_swap(small)
            small = small + chip_swap(small)
            small = jnp.concatenate([small, jnp.sum(c_up_sum, axis=0)[None]], axis=0)
            small = jnp.pad(small, ((0, 16 - small.shape[0]), (0, 0)))
            slab = skip_grad(
                chunk, core_scalar, low, sib, decoder_in, partner[chunk], (d_w_skip, small)
            )
            last = GroupSum(slab, steps)
            returned, d_decoder_in = skip_back(
                chunk, core_scalar, w_skip, low, sib, group_rows, (d_decoder_in,), (slab,)
            )
            d_encoder.append(returned)
    late.step(returned)
    last.step(returned)
    d_encoder_out = restore(
        core_scalar, [partner_swap(part) for part in gate(d_encoder, last.value)]
    )

    kept = gate([*down, *attended], last.value)
    down, attended = kept[:CHUNKS], kept[CHUNKS:]
    layer_out = []
    for chunk in range(CHUNKS):
        parts = down[chunk].reshape(2, block, D)
        away = lax.dynamic_index_in_dim(parts, 1 - chip, 0, keepdims=False)
        home = lax.dynamic_index_in_dim(parts, chip, 0, keepdims=False)
        base = lax.dynamic_index_in_dim(
            attended[chunk].reshape(2, block, D), chip, 0, keepdims=False
        )
        layer_out.append(base + (home.astype(F32) + chip_swap(away).astype(F32)))
    layer_out = jnp.concatenate(layer_out, axis=0)
    while not (late.done and last.done):
        if len(last.ways) == 2:
            last.step(d_w_ff)
        elif not last.done:
            last.step()
        if not late.done:
            late.step()
    late, last = late.value, last.value
    d_w_down, d_w_up = d_w_ff[: w_down.shape[0]], d_w_ff[w_down.shape[0] :]
    d_w_out, d_w_qkv = late[:local_width], late[local_width:].reshape(w_qkv.shape)
    d_w_skip = last[:-SMALL_ROWS].reshape(w_skip.shape)
    small = last[-SMALL_ROWS:].astype(F32)
    return (
        layer_out,
        d_decoder_in,
        d_encoder_out,
        d_w_skip.astype(F32),
        small[2],
        small[0],
        small[1],
        d_w_qkv.astype(F32),
        d_w_out.astype(F32),
        small[3],
        small[4],
        d_w_up.astype(F32),
        small[6],
        d_w_down.astype(F32),
    )


def solution(mesh):
    return jax.shard_map(
        shards,
        mesh=mesh,
        in_specs=(
            P(("section", "dp"), "tensor"),
            P(("section", "dp"), "tensor"),
            P(("section", "dp"), None),
            P(None, "tensor", None),
            P(),
            P(),
            P(),
            P(None, None, "tensor"),
            P("tensor", None),
            P(),
            P(),
            P(None, "tensor"),
            P("tensor"),
            P("tensor", None),
            P(("section", "dp"), None),
        ),
        out_specs=(
            P(("section", "dp", "tensor"), None),
            P(("section", "dp"), "tensor"),
            P(("section", "dp"), "tensor"),
            P(None, "tensor", None),
            P(),
            P(),
            P(),
            P(None, None, "tensor"),
            P("tensor", None),
            P(),
            P(),
            P(None, "tensor"),
            P("tensor"),
            P("tensor", None),
        ),
        check_vma=False,
    )
```

```python
import functools
import jax
import jax.numpy as jnp
from jax import lax
from jax.experimental import pallas as pl
from jax.experimental.pallas import tpu as pltpu
from jax.sharding import PartitionSpec as P

D = 1024
HEADS = 16
UTTS = 6
HEAD_DIM = D // HEADS
SCALE = HEAD_DIM**-0.5

EPSILON = 1e-05
FAR = 1e30
ROOT_HALF = 0.7071067811865476
INV_ROOT_TAU = 0.3989422804014327
BF16 = jnp.bfloat16
F32 = jnp.float32
NT = (((1,), (1,)), ((), ()))
NN = (((1,), (0,)), ((), ()))
TN = (((0,), (0,)), ((), ()))
CHUNKS = 2
PARTS = 4


def mm(left, right, dims):
    return lax.dot_general(left, right, dims, preferred_element_type=F32)


def starts_of(seg):
    return [jnp.sum((seg < u).astype(jnp.int32)) for u in range(1, UTTS)]


def tile_range(starts, first, count, tile, total):
    low = jnp.int32(0)
    high = jnp.int32(total)
    for s in starts:
        low = jnp.maximum(low, jnp.where(s <= first, s, 0))
        high = jnp.minimum(high, jnp.where(s >= first + count, s, total))
    return low // tile, (high + tile - 1) // tile


def eye(n):
    r = lax.broadcasted_iota(jnp.int32, (n, n), 0)
    c = lax.broadcasted_iota(jnp.int32, (n, n), 1)
    return jnp.where(r == c, 1.0, 0.0).astype(BF16)


def far_tile(starts, seg_row, q_first, k_first, bk, bq):
    kpos = k_first + lax.broadcasted_iota(jnp.int32, (bk, bq), 0)
    qpos = q_first + lax.broadcasted_iota(jnp.int32, (bk, bq), 1)
    lo = jnp.zeros_like(seg_row)
    hi = jnp.full_like(seg_row, starts[0])
    for u in range(1, UTTS):
        lo = jnp.where(seg_row == u, starts[u - 1], lo)
        hi = jnp.where(seg_row == u, starts[u] if u < UTTS - 1 else 1 << 30, hi)
    ok = (kpos >= lo) & (kpos < hi)
    return jnp.where(ok, jnp.abs(kpos - qpos).astype(F32), FAR)


def head_masked(pair, which):
    lane = lax.broadcasted_iota(jnp.int32, pair.shape, 1)
    keep = (lane < HEAD_DIM) if which == 0 else (lane >= HEAD_DIM)
    return jnp.where(keep, pair, 0.0).astype(BF16)


def load_pieces(core, pieces, whole_ref):
    rows = pieces[0].shape[1]
    for n, piece in enumerate(pieces):
        chunk, side = n // 2, n % 2
        for y in range(2):
            first = y * (4 * rows) + (core ^ side) * (2 * rows) + chunk * rows
            whole_ref[pl.ds(pl.multiple_of(first, rows), rows)] = piece[y]


def fwd_kernel(
    heads, bk, chunk, core_ref, slope_ref, seg_ref, w_ref, q00, q01, q10, q11, *refs
):
    out_ref, lse_ref, own_ref, *sib_refs = refs[-8 - PARTS : -5]
    qkv_ref, vt_ref, acc_ref, s_ref, top_ref = refs[-5:]
    strip = sib_refs[0].shape[0]
    total = seg_ref.shape[1]
    width = heads * HEAD_DIM
    bq = out_ref.shape[1] // 2
    core = core_ref[0]
    load_pieces(core, (q00, q01, q10, q11), qkv_ref)
    starts = starts_of(seg_ref[...])
    ident = eye(width)

    def prep(j, c):
        at = pl.ds(pl.multiple_of(j * bk, bk), bk)
        vt = mm(ident, qkv_ref[at, 2 * width : 3 * width], NT).astype(BF16)
        for h in range(heads):
            vt_ref[h * 80 : h * 80 + 64, at] = vt[h * 64 : (h + 1) * 64]
            vt_ref[h * 80 + 64 : (h + 1) * 80, at] = jnp.ones((16, bk), BF16)
        return c

    lax.fori_loop(0, total // bk, prep, 0)

    def q_step(i, c):
        side, y = i // 2, i % 2
        qi = pl.multiple_of(y * (4 * bq) + (core ^ side) * (2 * bq) + chunk * bq, bq)
        lo, hi = tile_range(starts, qi, bq, bk, total)
        seg_row = seg_ref[:, pl.ds(qi, bq)]
        acc_ref[...] = jnp.zeros_like(acc_ref)
        top_ref[...] = jnp.full_like(top_ref, -3e38)
        qs = []
        for h in range(heads):
            p = h // 2
            qp = qkv_ref[pl.ds(qi, bq), p * 128 : (p + 1) * 128].astype(F32) * SCALE
            qs.append(head_masked(qp, h % 2))

        def score_step(j, c):
            kj = pl.multiple_of(j * bk, bk)
            far = far_tile(starts, seg_row, qi, kj, bk, bq)
            for h in range(heads):
                p = h // 2
                kp = qkv_ref[pl.ds(kj, bk), width + p * 128 : width + (p + 1) * 128]
                s = mm(kp, qs[h], NT) - far * slope_ref[h]
                s_ref[h, pl.ds(kj, bk)] = s
                top_ref[h] = jnp.maximum(top_ref[h], jnp.max(s.reshape(bk // 8, 8, bq), axis=0))
            return c

        lax.fori_loop(lo, hi, score_step, 0)
        tops = [jnp.max(top_ref[h], axis=0, keepdims=True) for h in range(heads)]

        def mix_step(j, c):
            kj = pl.multiple_of(j * bk, bk)
            for h in range(heads):
                e = jnp.exp(s_ref[h, pl.ds(kj, bk)] - tops[h]).astype(BF16)
                hs = slice(h * 80, (h + 1) * 80)
                acc_ref[hs] = acc_ref[hs] + mm(vt_ref[hs, pl.ds(kj, bk)], e, NN)
            return c

        lax.fori_loop(lo, hi, mix_step, 0)
        outs = []
        for h in range(heads):
            whole = acc_ref[h * 80 + 64 : h * 80 + 65]
            outs.append((acc_ref[h * 80 : h * 80 + 64] * (1.0 / whole)).astype(BF16))
            lse_ref[i, h : h + 1] = tops[h] + jnp.log(whole)
        ot = jnp.concatenate(outs, axis=0)
        here = pl.ds(pl.multiple_of(y * bq, bq), bq)
        mixed = mm(eye(bq), ot, NT).astype(BF16)
        out_ref[side, here] = mixed
        part = mm(mixed, w_ref[...], NN).astype(BF16)

        @pl.when(side == 0)
        def _():
            own_ref[here] = part

        for n, sib_ref in enumerate(sib_refs):
            first = n * strip % bq

            @pl.when((side == 1) & (y == n * strip // bq))
            def _(sib_ref=sib_ref, first=first):
                sib_ref[...] = part[first : first + strip]

        return c

    lax.fori_loop(0, 4, q_step, 0)


def attend(chunk, core, slopes, seg, w_out, pieces, ahead=()):
    total = seg.shape[1]
    rows = pieces[0].shape[1]
    heads = pieces[0].shape[2] // (3 * HEAD_DIM)
    width = heads * HEAD_DIM
    bk = 256
    smem = pl.BlockSpec(memory_space=pltpu.SMEM)
    vmem = pl.BlockSpec(memory_space=pltpu.VMEM)
    hbm = pl.BlockSpec(memory_space=pl.ANY)
    return pl.pallas_call(
        functools.partial(fwd_kernel, heads, bk, chunk),
        out_shape=(
            jax.ShapeDtypeStruct((2, 2 * rows, width), BF16),
            jax.ShapeDtypeStruct((4, heads, rows), F32),
            jax.ShapeDtypeStruct((2 * rows, w_out.shape[1]), BF16),
        )
        + (jax.ShapeDtypeStruct((2 * rows // PARTS, w_out.shape[1]), BF16),) * PARTS,
        in_specs=[smem, smem] + [vmem] * 6 + [hbm] * len(ahead),
        out_specs=(vmem,) * (3 + PARTS),
        scratch_shapes=[
            pltpu.VMEM((total, 3 * width), BF16),
            pltpu.VMEM((heads * 80, total), BF16),
            pltpu.VMEM((heads * 80, rows), F32),
            pltpu.VMEM((heads, total, rows), F32),
            pltpu.VMEM((heads, 8, rows), F32),
        ],
        compiler_params=pltpu.CompilerParams(vmem_limit_bytes=28 << 20),
        name="attend",
    )(core, slopes, seg, w_out, *pieces, *ahead)


def bwd_kernel(heads, bk, chunk, *refs):
    core_ref, slope_ref, seg_ref, q00, q01, q10, q11, do0, do1, o_ref, lse_ref = refs[:11]
    if chunk == 0:
        dq_ref, dkv_ref = refs[-8:-6]
    else:
        dq_in, dkv_in = refs[11:13]
        dqkv_ref = refs[-7]
    qkv_ref, kt_ref, dqt_ref, dk_ref, dv_ref, delta_ref = refs[-6:]
    total = seg_ref.shape[1]
    width = heads * HEAD_DIM
    bq = o_ref.shape[1] // 2
    core = core_ref[0]
    load_pieces(core, (q00, q01, q10, q11), qkv_ref)
    starts = starts_of(seg_ref[...])
    ident = eye(width)
    hr = lax.broadcasted_iota(jnp.int32, (8, width), 0)
    hc = lax.broadcasted_iota(jnp.int32, (8, width), 1)
    pick = jnp.where(hr == hc // HEAD_DIM, 1.0, 0.0)

    def prep(j, c):
        at = pl.ds(pl.multiple_of(j * bk, bk), bk)
        kj = qkv_ref[at, width : 2 * width]
        kt_ref[:, at] = (mm(ident, kj, NT) * SCALE).astype(BF16)
        if chunk == 0:
            dk_ref[at] = jnp.zeros((bk, width), F32)
            dv_ref[at] = jnp.zeros((bk, width), F32)
        else:
            dk_ref[at] = dkv_in[at, :width]
            dv_ref[at] = dkv_in[at, width:]
        return c

    lax.fori_loop(0, total // bk, prep, 0)
    for side, do_ref in enumerate((do0, do1)):
        for y in range(2):
            at = slice(y * bq, (y + 1) * bq)
            prod = do_ref[at].astype(F32) * o_ref[side, at].astype(F32)
            delta_ref[side * 2 + y] = lax.dot_general(
                pick, prod, NT, precision=lax.Precision.HIGHEST, preferred_element_type=F32
            )

    for side, do_ref in enumerate((do0, do1)):

        def q_step(y, c, side=side, do_ref=do_ref):
            i = side * 2 + y
            qi = pl.multiple_of(y * (4 * bq) + (core ^ side) * (2 * bq) + chunk * bq, bq)
            here = pl.ds(pl.multiple_of(y * bq, bq), bq)
            lo, hi = tile_range(starts, qi, bq, bk, total)
            seg_row = seg_ref[:, pl.ds(qi, bq)]
            dqt_ref[...] = jnp.zeros_like(dqt_ref)
            qs, dos = [], []
            for h in range(heads):
                p = h // 2
                qp = qkv_ref[pl.ds(qi, bq), p * 128 : (p + 1) * 128].astype(F32) * SCALE
                qs.append(head_masked(qp, h % 2))
                dp = do_ref[here, p * 128 : (p + 1) * 128].astype(F32)
                dos.append(head_masked(dp, h % 2))
            lses = [lse_ref[i, h : h + 1] for h in range(heads)]
            deltas = [delta_ref[i, h : h + 1] for h in range(heads)]

            def k_step(j, c):
                kj = pl.multiple_of(j * bk, bk)
                at = pl.ds(kj, bk)
                far = far_tile(starts, seg_row, qi, kj, bk, bq)
                for p in range(heads // 2):
                    cols = slice(p * 128, (p + 1) * 128)
                    kp = qkv_ref[at, width + p * 128 : width + (p + 1) * 128]
                    vp = qkv_ref[at, 2 * width + p * 128 : 2 * width + (p + 1) * 128]
                    dv = dv_ref[at, cols]
                    dk = dk_ref[at, cols]
                    for h in (2 * p, 2 * p + 1):
                        s = mm(kp, qs[h], NT) - far * slope_ref[h]
                        w = jnp.exp(s - lses[h])
                        dw = mm(vp, dos[h], NT)
                        ds = (w * (dw - deltas[h])).astype(BF16)
                        dv = dv + mm(w.astype(BF16), dos[h], NN)
                        dk = dk + mm(ds, qs[h], NN)
                        hs = slice(h * HEAD_DIM, (h + 1) * HEAD_DIM)
                        dqt_ref[hs] = dqt_ref[hs] + mm(kt_ref[hs, at], ds, NN)
                    dv_ref[at, cols] = dv
                    dk_ref[at, cols] = dk
                return c

            lax.fori_loop(lo, hi, k_step, 0)
            dq = mm(eye(bq), dqt_ref[...].astype(BF16), NT).astype(BF16)
            if chunk == 0:
                dq_ref[side, here] = dq
            else:
                dqkv_ref[2 + side, here, :width] = dq
            return c

        lax.fori_loop(0, 2, q_step, 0)

    if chunk == 0:

        def finish(j, c):
            at = pl.ds(pl.multiple_of(j * bk, bk), bk)
            dkv_ref[at, :width] = dk_ref[at]
            dkv_ref[at, width:] = dv_ref[at]
            return c

        lax.fori_loop(0, total // bk, finish, 0)
    else:
        for side in range(2):
            dqkv_ref[side, :, :width] = dq_in[side]
        for n in range(4):
            part, side = n // 2, n % 2
            for y in range(2):
                first = y * (4 * bq) + (core ^ side) * (2 * bq) + part * bq
                at = pl.ds(pl.multiple_of(first, bq), bq)
                here = slice(y * bq, (y + 1) * bq)
                dqkv_ref[n, here, width : 2 * width] = dk_ref[at].astype(BF16)
                dqkv_ref[n, here, 2 * width :] = dv_ref[at].astype(BF16)


def attend_back(chunk, core, slopes, seg, pieces, d_heads, heads_out, lse, before=(), ahead=()):
    total = seg.shape[1]
    rows = pieces[0].shape[1]
    heads = pieces[0].shape[2] // (3 * HEAD_DIM)
    width = heads * HEAD_DIM
    bk = 256
    smem = pl.BlockSpec(memory_space=pltpu.SMEM)
    vmem = pl.BlockSpec(memory_space=pltpu.VMEM)
    hbm = pl.BlockSpec(memory_space=pl.ANY)
    if chunk == 0:
        out_shape = (
            jax.ShapeDtypeStruct((2, 2 * rows, width), BF16),
            jax.ShapeDtypeStruct((total, 2 * width), F32),
        )
        out_specs = (vmem, vmem)
    else:
        out_shape = jax.ShapeDtypeStruct((4, 2 * rows, 3 * width), BF16)
        out_specs = vmem
    return pl.pallas_call(
        functools.partial(bwd_kernel, heads, bk, chunk),
        out_shape=out_shape,
        in_specs=[smem, smem] + [vmem] * (9 + len(before)) + [hbm] * len(ahead),
        out_specs=out_specs,
        scratch_shapes=[
            pltpu.VMEM((total, 3 * width), BF16),
            pltpu.VMEM((width, total), BF16),
            pltpu.VMEM((width, rows), F32),
            pltpu.VMEM((total, width), F32),
            pltpu.VMEM((total, width), F32),
            pltpu.VMEM((4, 8, rows), F32),
        ],
        compiler_params=pltpu.CompilerParams(vmem_limit_bytes=34 << 20),
        name="attend_back",
    )(core, slopes, seg, *pieces, *d_heads, heads_out, lse, *before, *ahead)


def swap(value, axis, bit):
    pairs = [(source, source ^ (1 << bit)) for source in range(lax.axis_size(axis))]
    return lax.ppermute(value, axis, pairs)


core_swap = functools.partial(swap, axis="tensor", bit=0)
chip_swap = functools.partial(swap, axis="tensor", bit=1)
partner_swap = functools.partial(swap, axis="section", bit=0)


def add_low(*terms):
    return sum(term.astype(F32) for term in terms).astype(BF16)


def group_steps():
    steps = [("section", 0)]
    for bit in range((lax.axis_size("dp") - 1).bit_length()):
        steps.append(("dp", bit))
    return steps


def gate(values, *ahead):
    hbm = pl.BlockSpec(memory_space=pl.ANY)
    many = isinstance(values, (list, tuple))
    values = tuple(values) if many else (values,)
    out = pl.pallas_call(
        lambda *refs: None,
        out_shape=tuple(jax.ShapeDtypeStruct(value.shape, value.dtype) for value in values),
        in_specs=[hbm] * (len(values) + len(ahead)),
        out_specs=(hbm,) * len(values),
        input_output_aliases={n: n for n in range(len(values))},
        name="gate",
    )(*values, *ahead)
    return out if many else out[0]


def fold_kernel(halving, mine_ref, kept_ref, came_ref, *refs):
    total = (kept_ref[...].astype(F32) + came_ref[...].astype(F32)).astype(BF16)
    if halving:
        put_halves(mine_ref[0], total, *refs[-2:])
    else:
        refs[-1][...] = total


def put_halves(mine, total, kept_ref, sent_ref, half=None):
    rows = kept_ref.shape[0]
    for n in range(2) if half is None else (half,):
        part = total[n * rows : (n + 1) * rows] if half is None else total

        @pl.when(mine == n)
        def _(part=part):
            kept_ref[...] = part

        @pl.when(mine != n)
        def _(part=part):
            sent_ref[...] = part


def fold(kept, came, mine, ahead):
    rows, width = kept.shape
    vmem = pl.BlockSpec(memory_space=pltpu.VMEM)
    halving = mine is not None
    shape = jax.ShapeDtypeStruct((rows // 2 if halving else rows, width), BF16)
    scalar = mine if halving else jnp.int32(0)
    out = pl.pallas_call(
        functools.partial(fold_kernel, halving),
        out_shape=(shape,) * (2 if halving else 1),
        in_specs=[pl.BlockSpec(memory_space=pltpu.SMEM), vmem, vmem]
        + [pl.BlockSpec(memory_space=pl.ANY)] * len(ahead),
        out_specs=(vmem,) * (2 if halving else 1),
        compiler_params=pltpu.CompilerParams(vmem_limit_bytes=12 << 20),
        name="fold",
    )(scalar.reshape(1), kept, came, *ahead)
    return out if halving else (out[0], None)


def join_kernel(mine_ref, value_ref, came_ref, *refs):
    out_ref = refs[-1]
    rows = value_ref.shape[0]
    mine = mine_ref[0]
    out_ref[pl.ds(pl.multiple_of(mine * rows, rows), rows)] = value_ref[...]
    out_ref[pl.ds(pl.multiple_of((1 - mine) * rows, rows), rows)] = came_ref[...]


def join(value, came, mine, ahead):
    rows, width = value.shape
    if rows % 16:
        came = gate(came, *ahead) if ahead else came
        first = mine == 0
        return jnp.concatenate(
            [jnp.where(first, value, came), jnp.where(first, came, value)], axis=0
        )
    vmem = pl.BlockSpec(memory_space=pltpu.VMEM)
    return pl.pallas_call(
        join_kernel,
        out_shape=jax.ShapeDtypeStruct((2 * rows, width), BF16),
        in_specs=[pl.BlockSpec(memory_space=pltpu.SMEM), vmem, vmem]
        + [pl.BlockSpec(memory_space=pl.ANY)] * len(ahead),
        out_specs=vmem,
        compiler_params=pltpu.CompilerParams(vmem_limit_bytes=12 << 20),
        name="join",
    )(mine.reshape(1), value, came, *ahead)


class GroupSum:
    def __init__(self, kept, sent, steps, mines):
        self.steps, self.mines = steps, mines
        self.count, self.kept = 0, kept
        self.done = False
        self.came = swap(sent, *steps[0])

    def step(self, *ahead):
        levels = len(self.steps)
        self.count += 1
        if self.count <= levels:
            following = self.mines[self.count] if self.count < levels else None
            rows = self.kept.shape[0]
            if self.count < levels and rows % 32:
                came = gate(self.came, *ahead) if ahead else self.came
                halves = add_low(self.kept, came).reshape(2, rows // 2, -1)
                self.kept = lax.dynamic_index_in_dim(halves, following, 0, keepdims=False)
                sent = lax.dynamic_index_in_dim(halves, 1 - following, 0, keepdims=False)
            else:
                self.kept, sent = fold(self.kept, self.came, following, ahead)
            if self.count < levels:
                self.came = swap(sent, *self.steps[self.count])
        else:
            level = 2 * levels - self.count
            self.kept = join(self.kept, self.came, self.mines[level], ahead)
        if self.count == 2 * levels:
            self.done = True
        elif self.count >= levels:
            self.came = swap(self.kept, *self.steps[2 * levels - 1 - self.count])
        return self.kept


def grads_kernel(mine_ref, *refs):
    norms, d_qkv_ref, heads, d_rows = refs[:4], refs[4], refs[5:7], refs[7:11]
    kept_ref, sent_ref, held_ref = refs[-3:]
    width = d_qkv_ref.shape[2]
    strip = 256
    half = kept_ref.shape[0]
    for n in range(2):
        for first in range(0, half, strip):
            at = slice(n * half + first, n * half + first + strip)
            to = slice(first, first + strip)
            total = sum(mm(norms[k][:, at], d_qkv_ref[k], TN) for k in range(4))
            held_ref[to, :width] = total.astype(BF16)
            total = sum(mm(d_rows[k][:, at], heads[k // 2][k % 2], TN) for k in range(4))
            held_ref[to, width:] = total.astype(BF16)
        put_halves(mine_ref[0], held_ref[...], kept_ref, sent_ref, half=n)


def late_grads(mine, norms, d_qkv, heads_out, d_rows, ahead):
    depth = norms[0].shape[1]
    width = d_qkv.shape[2] + heads_out[0].shape[2]
    vmem = pl.BlockSpec(memory_space=pltpu.VMEM)
    shape = jax.ShapeDtypeStruct((depth // 2, width), BF16)
    return pl.pallas_call(
        grads_kernel,
        out_shape=(shape, shape),
        in_specs=[pl.BlockSpec(memory_space=pltpu.SMEM)]
        + [vmem] * 11
        + [pl.BlockSpec(memory_space=pl.ANY)] * len(ahead),
        out_specs=(vmem, vmem),
        scratch_shapes=[pltpu.VMEM((depth // 2, width), BF16)],
        compiler_params=pltpu.CompilerParams(vmem_limit_bytes=32 << 20),
        name="late_grads",
    )(mine.reshape(1), *norms, d_qkv, *heads_out, *d_rows, *ahead)


def row_stats(values):
    row_mean = jnp.mean(values, axis=-1, keepdims=True)
    centered = values - row_mean
    inv_std = lax.rsqrt(jnp.mean(centered * centered, axis=-1, keepdims=True) + EPSILON)
    return centered * inv_std, inv_std


def norm_kernel(base_ref, mine_ref, other_ref, gain_ref, shift_ref, *refs):
    value_ref, low_ref = refs[-2:]
    value = base_ref[...] + (mine_ref[...].astype(F32) + other_ref[...].astype(F32))
    value_ref[...] = value
    normed, _ = row_stats(value)
    low_ref[...] = (normed * gain_ref[...] + shift_ref[...]).astype(BF16)


def norm_rows(base, mine, other, gain, shift, ahead=(), tile=128):
    rows, width = mine.shape
    wide = pl.BlockSpec((tile, width), lambda i: (i, 0))
    one = pl.BlockSpec((1, width), lambda i: (0, 0))
    return pl.pallas_call(
        norm_kernel,
        grid=(rows // tile,),
        out_shape=(
            jax.ShapeDtypeStruct((rows, width), F32),
            jax.ShapeDtypeStruct((rows, width), BF16),
        ),
        in_specs=[wide if base.shape[0] == rows else one, wide, wide, one, one]
        + [pl.BlockSpec(memory_space=pl.ANY)] * len(ahead),
        out_specs=(wide, wide),
        compiler_params=pltpu.CompilerParams(vmem_limit_bytes=24 << 20),
        name="norm_rows",
    )(base, mine, other, gain[None], shift[None], *ahead)


def back_kernel(past_ref, value_ref, mine_ref, other_ref, gain_ref, sums_in, *refs):
    grad_ref, low_ref, sums_ref = refs[-3:]
    d_output = mine_ref[...].astype(F32) + other_ref[...].astype(F32)
    normed, inv_std = row_stats(value_ref[...])
    d_normed = d_output * gain_ref[...]
    grad = past_ref[...].astype(F32) + inv_std * (
        d_normed
        - jnp.mean(d_normed, axis=-1, keepdims=True)
        - normed * jnp.mean(d_normed * normed, axis=-1, keepdims=True)
    )
    grad_ref[...] = grad
    low_ref[...] = grad.astype(BF16)

    @pl.when(pl.program_id(0) == 0)
    def _():
        sums_ref[...] = sums_in[...]

    for n, terms in enumerate((d_output * normed, d_output, grad)):
        part = jnp.sum(terms.reshape(-1, 8, terms.shape[1]), axis=0)
        sums_ref[n] = sums_ref[n] + part


def norm_back_rows(past, value, mine, other, gain, sums, ahead=(), tile=128):
    rows, width = mine.shape
    wide = pl.BlockSpec((tile, width), lambda i: (i, 0))
    one = pl.BlockSpec((1, width), lambda i: (0, 0))
    kept = pl.BlockSpec((3, 8, width), lambda i: (0, 0, 0))
    return pl.pallas_call(
        back_kernel,
        grid=(rows // tile,),
        out_shape=(
            jax.ShapeDtypeStruct((rows, width), F32),
            jax.ShapeDtypeStruct((rows, width), BF16),
            jax.ShapeDtypeStruct((3, 8, width), F32),
        ),
        in_specs=[wide, wide, wide, wide, one, kept]
        + [pl.BlockSpec(memory_space=pl.ANY)] * len(ahead),
        out_specs=(wide, wide, kept),
        compiler_params=pltpu.CompilerParams(vmem_limit_bytes=24 << 20),
        name="norm_back",
    )(past, value, mine, other, gain[None], sums, *ahead)


def feed_kernel(chunk, core_ref, up_ref, bias_ref, down_ref, own_ref, sib_ref, cot_ref, *refs):
    act_ref, grads_ref, bias_out, dn_own, *dn_sib = refs[-8 - PARTS : -4]
    cot_v, d_pre_ref, bias_acc, sems = refs[-4:]
    rows = own_ref.shape[0] // 2
    core = core_ref[0]
    copies = []
    for i in range(4):
        side, y = i // 2, i % 2
        first = y * (4 * rows) + (core ^ side) * (2 * rows) + chunk * rows
        copy = pltpu.make_async_copy(
            cot_ref.at[pl.ds(pl.multiple_of(first, rows), rows)],
            cot_v.at[i * rows : (i + 1) * rows],
            sems.at[i],
        )
        copy.start()
        copies.append(copy)
    bias_acc[...] = refs[1][...] if chunk else jnp.zeros_like(bias_acc)
    for copy in copies:
        copy.wait()
    for side, n_ref in enumerate((own_ref, sib_ref)):
        for y in range(2):
            here = slice(y * rows, (y + 1) * rows)
            there = slice((side * 2 + y) * rows, (side * 2 + y + 1) * rows)
            pre = mm(n_ref[here], up_ref[...], NN) + bias_ref[...]
            d_act = mm(cot_v[there], down_ref[...], NT)
            cdf = 0.5 + 0.5 * lax.erf(pre * ROOT_HALF)
            act_ref[side, here] = (pre * cdf).astype(BF16)
            slope = cdf + pre * jnp.exp(-0.5 * pre * pre) * INV_ROOT_TAU
            d_pre = (d_act * slope).astype(BF16)
            d_pre_ref[there] = d_pre
            parts = d_pre.astype(F32).reshape(-1, 8, d_pre.shape[1])
            bias_acc[...] = bias_acc[...] + jnp.sum(parts, axis=0)
            d_norm = mm(d_pre, up_ref[...], NT).astype(BF16)
            if side == 0:
                dn_own[here] = d_norm
            else:
                strip = dn_sib[0].shape[0]
                for n in range(rows // strip):
                    dn_sib[y * rows // strip + n][...] = d_norm[n * strip : (n + 1) * strip]
    bias_out[...] = bias_acc[...]
    own_rows, sib_rows = slice(0, 2 * rows), slice(2 * rows, 4 * rows)
    units = act_ref.shape[2]
    strip = 256
    for first in range(0, units, strip):
        at = slice(first, first + strip)
        total = mm(act_ref[0, :, at], cot_v[own_rows], TN) + mm(
            act_ref[1, :, at], cot_v[sib_rows], TN
        )
        if chunk:
            total = total + refs[0][at]
        grads_ref[at] = total.astype(grads_ref.dtype)
    for first in range(0, own_ref.shape[1], strip):
        at, to = slice(first, first + strip), slice(units + first, units + first + strip)
        total = mm(own_ref[:, at], d_pre_ref[own_rows], TN) + mm(
            sib_ref[:, at], d_pre_ref[sib_rows], TN
        )
        if chunk:
            total = total + refs[0][to]
        grads_ref[to] = total.astype(grads_ref.dtype)


def feed(chunk, core, w_up, c_up, w_down, own, sib, cot, before=()):
    rows, width = own.shape
    units = w_up.shape[1]
    vmem = pl.BlockSpec(memory_space=pltpu.VMEM)
    return pl.pallas_call(
        functools.partial(feed_kernel, chunk),
        out_shape=(
            jax.ShapeDtypeStruct((2, rows, units), BF16),
            jax.ShapeDtypeStruct((units + width, width), BF16 if chunk else F32),
            jax.ShapeDtypeStruct((8, units), F32),
            jax.ShapeDtypeStruct((rows, width), BF16),
        )
        + (jax.ShapeDtypeStruct((rows // PARTS, width), BF16),) * PARTS,
        in_specs=[pl.BlockSpec(memory_space=pltpu.SMEM)]
        + [vmem] * 5
        + [pl.BlockSpec(memory_space=pl.ANY)]
        + [vmem] * len(before),
        out_specs=(vmem,) * (4 + PARTS),
        scratch_shapes=[
            pltpu.VMEM((2 * rows, width), BF16),
            pltpu.VMEM((2 * rows, units), BF16),
            pltpu.VMEM((8, units), F32),
            pltpu.SemaphoreType.DMA((4,)),
        ],
        compiler_params=pltpu.CompilerParams(vmem_limit_bytes=44 << 20),
        name="feed",
    )(core, w_up, c_up[None], w_down, own, sib, cot, *before)


def row_copies(core, chunk, rows, source, target, sems, reverse=False):
    copies = []
    for i in range(4):
        side, y = i // 2, i % 2
        first = y * (4 * rows) + (core ^ side) * (2 * rows) + chunk * rows
        whole = pl.ds(pl.multiple_of(first, rows), rows)
        here = slice(i * rows, (i + 1) * rows)
        if reverse:
            copy = pltpu.make_async_copy(source.at[here], target.at[whole], sems.at[i])
        else:
            copy = pltpu.make_async_copy(source.at[whole], target.at[here], sems.at[i])
        copy.start()
        copies.append(copy)
    return copies


def skip_grad_kernel(chunk, core_ref, own_ref, sib_ref, dec_ref, enc_ref, *refs):
    outs, (dec_v, enc_v, sems) = refs[2 * chunk : -3], refs[-3:]
    rows = own_ref.shape[0] // 2
    width, cols = dec_v.shape[1], own_ref.shape[1]
    copies = row_copies(core_ref[0], chunk, rows, dec_ref, dec_v, sems.at[0])
    for i in range(4):
        side, y = i // 2, i % 2
        first = (y * 2 + (core_ref[0] ^ side)) * rows
        copy = pltpu.make_async_copy(
            enc_ref.at[pl.ds(pl.multiple_of(first, rows), rows)],
            enc_v.at[i * rows : (i + 1) * rows],
            sems.at[1, i],
        )
        copy.start()
        copies.append(copy)
    for copy in copies:
        copy.wait()
    half = 2 * rows
    for n, part in enumerate((dec_v, enc_v)):
        at = slice(n * width, (n + 1) * width)
        total = mm(part[:half], own_ref[...], TN) + mm(part[half:], sib_ref[...], TN)
        if not chunk:
            outs[0][at] = total
            continue
        total = (total + refs[0][at]).astype(BF16)
        side = jnp.zeros((width, 128), BF16)
        if n == 0:
            small = refs[1]
            lines = [
                small[k : k + 1, j * 128 : (j + 1) * 128] for k in range(8) for j in range(cols // 128)
            ]
            spare = jnp.zeros((width - len(lines), 128), F32)
            side = jnp.concatenate(lines + [spare], axis=0).astype(BF16)
        put_halves(core_ref[1], jnp.concatenate([total, side], axis=1), *outs, half=n)


def skip_grad(chunk, core, own, sib, dec, enc, before=()):
    rows, cols = own.shape
    width = dec.shape[1]
    vmem = pl.BlockSpec(memory_space=pltpu.VMEM)
    hbm = pl.BlockSpec(memory_space=pl.ANY)
    half = jax.ShapeDtypeStruct((width, cols + 128), BF16)
    return pl.pallas_call(
        functools.partial(skip_grad_kernel, chunk),
        out_shape=(half, half) if chunk else (jax.ShapeDtypeStruct((2 * width, cols), F32),),
        in_specs=[pl.BlockSpec(memory_space=pltpu.SMEM), vmem, vmem, hbm, hbm]
        + [vmem] * len(before),
        out_specs=(vmem,) * (1 + chunk),
        scratch_shapes=[
            pltpu.VMEM((2 * rows, width), BF16),
            pltpu.VMEM((2 * rows, width), BF16),
            pltpu.SemaphoreType.DMA((2, 4)),
        ],
        compiler_params=pltpu.CompilerParams(vmem_limit_bytes=24 << 20),
        name="skip_grad",
    )(core, own, sib, dec, enc, *before)


def skip_back_kernel(chunk, core_ref, w_ref, own_ref, sib_ref, *refs):
    back_ref, whole_ref, held, sems = refs[-4:]
    rows = own_ref.shape[0] // 2
    for side, part in enumerate((own_ref, sib_ref)):
        at = slice(side * 2 * rows, (side + 1) * 2 * rows)
        back_ref[at] = mm(part[...], w_ref[1], NT).astype(BF16)
        held[at] = mm(part[...], w_ref[0], NT)
    for copy in row_copies(core_ref[0], chunk, rows, held, whole_ref, sems, reverse=True):
        copy.wait()


def skip_back(chunk, core, w_skip, own, sib, group_rows, before=(), ahead=()):
    rows = own.shape[0]
    width = w_skip.shape[1]
    vmem = pl.BlockSpec(memory_space=pltpu.VMEM)
    hbm = pl.BlockSpec(memory_space=pl.ANY)
    return pl.pallas_call(
        functools.partial(skip_back_kernel, chunk),
        out_shape=(
            jax.ShapeDtypeStruct((2 * rows, width), BF16),
            jax.ShapeDtypeStruct((group_rows, width), F32),
        ),
        in_specs=[pl.BlockSpec(memory_space=pltpu.SMEM), vmem, vmem, vmem]
        + [hbm] * (len(before) + len(ahead)),
        out_specs=(vmem, hbm),
        scratch_shapes=[pltpu.VMEM((2 * rows, width), F32), pltpu.SemaphoreType.DMA((4,))],
        input_output_aliases={4: 1} if before else {},
        compiler_params=pltpu.CompilerParams(vmem_limit_bytes=24 << 20),
        name="skip_back",
    )(core, w_skip, own, sib, *before, *ahead)


def restore_kernel(core_ref, *refs):
    out_ref = refs[-1]
    for chunk, part in enumerate(refs[:-1]):
        rows = part.shape[0] // 4
        for i in range(4):
            side, y = i // 2, i % 2
            first = y * (4 * rows) + (core_ref[0] ^ side) * (2 * rows) + chunk * rows
            out_ref[pl.ds(pl.multiple_of(first, rows), rows)] = part[i * rows : (i + 1) * rows]


def restore(core, parts):
    vmem = pl.BlockSpec(memory_space=pltpu.VMEM)
    rows, width = parts[0].shape
    return pl.pallas_call(
        restore_kernel,
        out_shape=jax.ShapeDtypeStruct((rows * len(parts), width), parts[0].dtype),
        in_specs=[pl.BlockSpec(memory_space=pltpu.SMEM)] + [vmem] * len(parts),
        out_specs=vmem,
        compiler_params=pltpu.CompilerParams(vmem_limit_bytes=12 << 20),
        name="restore",
    )(core, *parts)


def skip_kernel(chunk, core_ref, w_ref, dec_ref, enc_ref, own_ref, *refs):
    sib_refs, (dec_v, enc_v, sems) = refs[:PARTS], refs[PARTS:]
    rows = own_ref.shape[0] // 2
    copies = row_copies(core_ref[0], chunk, rows, dec_ref, dec_v, sems.at[0])
    for i in range(4):
        side, y = i // 2, i % 2
        first = (y * 2 + (core_ref[0] ^ side)) * rows
        copy = pltpu.make_async_copy(
            enc_ref.at[pl.ds(pl.multiple_of(first, rows), rows)],
            enc_v.at[i * rows : (i + 1) * rows],
            sems.at[1, i],
        )
        copy.start()
        copies.append(copy)
    for copy in copies:
        copy.wait()
    half = 2 * rows
    strip = half // PARTS
    for n, sib_ref in enumerate(sib_refs):
        at = slice(half + n * strip, half + (n + 1) * strip)
        sib_ref[...] = (mm(dec_v[at], w_ref[0], NN) + mm(enc_v[at], w_ref[1], NN)).astype(BF16)
    own_ref[...] = (mm(dec_v[:half], w_ref[0], NN) + mm(enc_v[:half], w_ref[1], NN)).astype(BF16)


def skip(chunk, core, w_skip, dec, enc):
    rows = enc.shape[0] // 2
    width, cols = w_skip.shape[1:]
    vmem = pl.BlockSpec(memory_space=pltpu.VMEM)
    hbm = pl.BlockSpec(memory_space=pl.ANY)
    return pl.pallas_call(
        functools.partial(skip_kernel, chunk),
        out_shape=(jax.ShapeDtypeStruct((rows, cols), BF16),)
        + (jax.ShapeDtypeStruct((rows // PARTS, cols), BF16),) * PARTS,
        in_specs=[pl.BlockSpec(memory_space=pltpu.SMEM), vmem, hbm, hbm],
        out_specs=(vmem,) * (1 + PARTS),
        scratch_shapes=[
            pltpu.VMEM((2 * rows, width), BF16),
            pltpu.VMEM((2 * rows, width), BF16),
            pltpu.SemaphoreType.DMA((2, 4)),
        ],
        compiler_params=pltpu.CompilerParams(vmem_limit_bytes=16 << 20),
        name="skip",
    )(core, w_skip, dec, enc)


def shards(
    decoder_in,
    encoder_out,
    segments,
    w_skip,
    b_skip,
    ln1_gain,
    ln1_bias,
    w_qkv,
    w_out,
    ln2_gain,
    ln2_bias,
    w_up,
    c_up,
    w_down,
    cotangent,
):
    group_rows = decoder_in.shape[0]
    tensor_rank = lax.axis_index("tensor")
    core = tensor_rank & 1
    chip = tensor_rank >> 1
    heads_here = HEADS // lax.axis_size("tensor")
    local_width = heads_here * HEAD_DIM
    block = group_rows // (4 * CHUNKS)
    qkv_matrix = w_qkv.reshape(D, 3 * local_width)
    steps = group_steps()
    mines = [((lax.axis_index(axis) >> bit) & 1).astype(jnp.int32) for axis, bit in steps]
    core_scalar = jnp.stack([core.astype(jnp.int32), mines[0]])
    slopes = jnp.exp2(
        -8.0
        * (tensor_rank * heads_here + jnp.arange(heads_here, dtype=jnp.int32) + 1).astype(F32)
        / HEADS
    )
    spots = [(chunk, side) for chunk in range(CHUNKS) for side in range(2)]

    def piece_of(array, chunk, side):
        width = array.shape[-1]
        parts = array.reshape(2, 2, CHUNKS, block, width)[:, :, chunk]
        return lax.dynamic_index_in_dim(parts, core ^ side, 1, keepdims=False).reshape(
            2 * block, width
        )

    cot = [piece_of(cotangent, chunk, 0) for chunk in range(CHUNKS)]
    encoder_parts = encoder_out.reshape(2, 2, CHUNKS, block, encoder_out.shape[1])
    partner = [
        partner_swap(encoder_parts[:, :, chunk].reshape(4 * block, -1)) for chunk in range(CHUNKS)
    ]

    def chip_total(half):
        sent = core_swap(half(1).astype(BF16))
        return (half(0) + sent.astype(F32)).astype(BF16)

    merged, norm_one, qkv = [], {}, {}
    sums = []
    for chunk in range(CHUNKS):
        own, *sib = skip(chunk, core_scalar, w_skip, decoder_in, partner[chunk])
        sums.append(add_low(own, jnp.concatenate([core_swap(part) for part in sib], axis=0)))
        if chunk + 1 < CHUNKS:
            partner[chunk + 1] = gate(partner[chunk + 1], sums[chunk])
    others = [chip_swap(part) for part in sums]
    ahead = (qkv_matrix, *sums)
    for chunk in range(CHUNKS):
        value, normal = norm_rows(
            b_skip[None], sums[chunk], others[chunk], ln1_gain, ln1_bias, ahead
        )
        merged.append(value)
        norm_one[chunk, 0] = normal
        norm_one[chunk, 1] = core_swap(normal)
        for side in range(2):
            qkv[chunk, side] = jnp.dot(
                norm_one[chunk, side], qkv_matrix, preferred_element_type=F32
            ).astype(BF16)
        ahead = (qkv[chunk, 0], qkv[chunk, 1], *cot)
    qkv_pieces = [qkv[spot].reshape(2, block, 3 * local_width) for spot in spots]

    heads_out, lse, sums = [], [], []
    for chunk in range(CHUNKS):
        mixed, log_total, own, *sib = attend(
            chunk, core_scalar, slopes, segments, w_out, qkv_pieces, sums
        )
        heads_out.append(mixed)
        lse.append(log_total)
        sums.append(add_low(own, jnp.concatenate([core_swap(part) for part in sib], axis=0)))
    others = [chip_swap(part) for part in sums]

    attended, activated, d_sums, d_others = [], [], [], []
    ahead = tuple(sums)
    grads = ()
    for chunk in range(CHUNKS):
        value, normal = norm_rows(
            merged[chunk], sums[chunk], others[chunk], ln2_gain, ln2_bias, ahead
        )
        attended.append(value)
        acts, weights_sum, bias_sum, own, *sib = feed(
            chunk, core_scalar, w_up, c_up, w_down, normal, core_swap(normal), cotangent, grads
        )
        grads = (weights_sum, bias_sum)
        activated.append(acts)
        sib = gate([core_swap(part) for part in sib], d_others[chunk - 1] if chunk else others[1])
        d_sums.append(add_low(own, jnp.concatenate(sib, axis=0)))
        d_others.append(chip_swap(d_sums[chunk]))
        ahead = (d_sums[chunk],)
    d_w_ff, c_up_sum = grads
    both = ("section", "dp")
    d_w_ff = lax.psum_scatter(
        gate(d_w_ff, d_sums[-1]), both, scatter_dimension=0, tiled=True
    )

    d_attended, d_attended_rows = [], {}
    sums_two = jnp.zeros((3, 8, D), F32)
    before = ()
    for chunk in range(CHUNKS):
        value, low, sums_two = norm_back_rows(
            cot[chunk], attended[chunk], d_sums[chunk], d_others[chunk], ln2_gain, sums_two,
            ahead,
        )
        d_attended.append(value)
        d_attended_rows[chunk, 0] = low
        d_attended_rows[chunk, 1] = core_swap(low)
        d_heads = [
            mm(d_attended_rows[chunk, side], w_out, NT).astype(BF16) for side in range(2)
        ]
        before = attend_back(
            chunk, core_scalar, slopes, segments, qkv_pieces, d_heads, heads_out[chunk],
            lse[chunk], before,
        )
        ahead = (before[0],)
    d_qkv = before

    sums = [
        chip_total(lambda side: mm(d_qkv[2 * chunk + side], qkv_matrix, NT))
        for chunk in range(CHUNKS)
    ]
    others = [chip_swap(part) for part in sums]
    kept, sent = late_grads(
        mines[0],
        [norm_one[spot] for spot in spots],
        d_qkv,
        heads_out,
        [d_attended_rows[spot] for spot in spots],
        sums,
    )
    late = GroupSum(kept, sent, steps, mines)
    activated = gate(activated, kept)
    down = [
        chip_total(
            lambda side: jnp.dot(activated[chunk][side], w_down, preferred_element_type=F32)
        )
        for chunk in range(CHUNKS)
    ]

    aways = [
        lax.dynamic_index_in_dim(part.reshape(2, block, D), 1 - chip, 0, keepdims=False)
        for part in down
    ]
    lows = []
    sums_one = jnp.zeros((3, 8, D), F32)
    ahead = (kept,)
    for chunk in range(CHUNKS):
        _, low, sums_one = norm_back_rows(
            d_attended[chunk], merged[chunk], sums[chunk], others[chunk], ln1_gain, sums_one, ahead
        )
        lows.append(low)
        if chunk == 0:
            ahead = (late.step(low, *aways),)
    d_w_ff = lax.all_gather(gate(d_w_ff, lows[0]), both, axis=0, tiled=True)
    sibs = [core_swap(low) for low in lows]
    small = jnp.sum(jnp.concatenate([sums_one, sums_two], axis=0), axis=1) * 0.5
    small = small + core_swap(small)
    small = small + chip_swap(small)
    small = jnp.concatenate([small, jnp.sum(c_up_sum, axis=0)[None]], axis=0)
    small = jnp.pad(small, ((0, 16 - small.shape[0]), (0, 0)))
    before = ()
    for chunk in range(CHUNKS):
        before = skip_grad(
            chunk, core_scalar, lows[chunk], sibs[chunk], decoder_in, partner[chunk],
            (*before, small) if chunk else (),
        )
    kept, sent = before
    last = GroupSum(kept, sent, steps, mines)
    d_encoder, before = [], ()
    for chunk in range(CHUNKS):
        returned, *before = skip_back(
            chunk, core_scalar, w_skip, lows[chunk], sibs[chunk], group_rows, before, (kept,)
        )
        d_encoder.append(returned)
    (d_decoder_in,) = before
    d_encoder_out = restore(core_scalar, [partner_swap(part) for part in d_encoder])
    last.step(*d_encoder)

    moved = [chip_swap(part) for part in gate(aways, lows[-1])]
    d_w_down, d_w_up = d_w_ff[: w_down.shape[0]].astype(F32), d_w_ff[w_down.shape[0] :].astype(F32)
    total = 2 * len(steps)
    while last.count < total - 1:
        if late.count < total - 1:
            late.step(last.kept)
        last.step()
    moved = gate(moved, last.kept)
    layer_out = []
    for chunk in range(CHUNKS):
        home, base = (
            lax.dynamic_index_in_dim(part.reshape(2, block, D), chip, 0, keepdims=False)
            for part in (down[chunk], attended[chunk])
        )
        layer_out.append(base + (home.astype(F32) + moved[chunk].astype(F32)))
    layer_out = jnp.concatenate(layer_out, axis=0)
    while not late.done:
        late.step(last.kept, d_w_down, d_w_up, layer_out)
    last.step(d_encoder_out)
    d_w_qkv = late.kept[:, : 3 * local_width].reshape(w_qkv.shape)
    d_w_out = late.kept[:, 3 * local_width :].T
    d_w_skip = last.kept[:, :D].reshape(w_skip.shape)
    small = last.kept[: 8 * D // 128, D:].astype(F32).reshape(8, D)
    return (
        layer_out,
        d_decoder_in,
        d_encoder_out,
        d_w_skip.astype(F32),
        small[2],
        small[0],
        small[1],
        d_w_qkv.astype(F32),
        d_w_out.astype(F32),
        small[3],
        small[4],
        d_w_up,
        small[6],
        d_w_down,
    )


def solution(mesh):
    return jax.shard_map(
        shards,
        mesh=mesh,
        in_specs=(
            P(("section", "dp"), "tensor"),
            P(("section", "dp"), "tensor"),
            P(("section", "dp"), None),
            P(None, "tensor", None),
            P(),
            P(),
            P(),
            P(None, None, "tensor"),
            P("tensor", None),
            P(),
            P(),
            P(None, "tensor"),
            P("tensor"),
            P("tensor", None),
            P(("section", "dp"), None),
        ),
        out_specs=(
            P(("section", "dp", "tensor"), None),
            P(("section", "dp"), "tensor"),
            P(("section", "dp"), "tensor"),
            P(None, "tensor", None),
            P(),
            P(),
            P(),
            P(None, None, "tensor"),
            P("tensor", None),
            P(),
            P(),
            P(None, "tensor"),
            P("tensor"),
            P("tensor", None),
        ),
        check_vma=False,
    )
```

```python
import functools
import jax
import jax.numpy as jnp
from jax import lax
from jax.experimental import pallas as pl
from jax.experimental.pallas import tpu as pltpu
from jax.sharding import PartitionSpec as P

D = 1024
HEADS = 16
UTTS = 6
HEAD_DIM = D // HEADS
SCALE = HEAD_DIM**-0.5

EPSILON = 1e-05
FAR = 1e30
ROOT_HALF = 0.7071067811865476
INV_ROOT_TAU = 0.3989422804014327
BF16 = jnp.bfloat16
F32 = jnp.float32
NT = (((1,), (1,)), ((), ()))
NN = (((1,), (0,)), ((), ()))
TN = (((0,), (0,)), ((), ()))
CHUNKS = 2
PARTS = 4


def mm(left, right, dims):
    return lax.dot_general(left, right, dims, preferred_element_type=F32)


def starts_of(seg):
    return [jnp.sum((seg < u).astype(jnp.int32)) for u in range(1, UTTS)]


def tile_range(starts, first, count, tile, total):
    low = jnp.int32(0)
    high = jnp.int32(total)
    for s in starts:
        low = jnp.maximum(low, jnp.where(s <= first, s, 0))
        high = jnp.minimum(high, jnp.where(s >= first + count, s, total))
    return low // tile, (high + tile - 1) // tile


def eye(n):
    r = lax.broadcasted_iota(jnp.int32, (n, n), 0)
    c = lax.broadcasted_iota(jnp.int32, (n, n), 1)
    return jnp.where(r == c, 1.0, 0.0).astype(BF16)


def far_tile(starts, seg_row, q_first, k_first, bk, bq):
    kpos = k_first + lax.broadcasted_iota(jnp.int32, (bk, bq), 0)
    qpos = q_first + lax.broadcasted_iota(jnp.int32, (bk, bq), 1)
    lo = jnp.zeros_like(seg_row)
    hi = jnp.full_like(seg_row, starts[0])
    for u in range(1, UTTS):
        lo = jnp.where(seg_row == u, starts[u - 1], lo)
        hi = jnp.where(seg_row == u, starts[u] if u < UTTS - 1 else 1 << 30, hi)
    ok = (kpos >= lo) & (kpos < hi)
    return jnp.where(ok, jnp.abs(kpos - qpos).astype(F32), FAR)


def head_masked(pair, which):
    lane = lax.broadcasted_iota(jnp.int32, pair.shape, 1)
    keep = (lane < HEAD_DIM) if which == 0 else (lane >= HEAD_DIM)
    return jnp.where(keep, pair, 0.0).astype(BF16)


def load_pieces(core, pieces, whole_ref):
    rows = pieces[0].shape[1]
    for n, piece in enumerate(pieces):
        chunk, side = n // 2, n % 2
        for y in range(2):
            first = y * (4 * rows) + (core ^ side) * (2 * rows) + chunk * rows
            whole_ref[pl.ds(pl.multiple_of(first, rows), rows)] = piece[y]


def fwd_kernel(
    heads, bk, chunk, core_ref, slope_ref, seg_ref, w_ref, q00, q01, q10, q11, *refs
):
    out_ref, lse_ref, own_ref, *sib_refs = refs[-8 - PARTS : -5]
    qkv_ref, vt_ref, acc_ref, s_ref, top_ref = refs[-5:]
    strip = sib_refs[0].shape[0]
    total = seg_ref.shape[1]
    width = heads * HEAD_DIM
    bq = out_ref.shape[1] // 2
    core = core_ref[0]
    load_pieces(core, (q00, q01, q10, q11), qkv_ref)
    starts = starts_of(seg_ref[...])
    ident = eye(width)

    def prep(j, c):
        at = pl.ds(pl.multiple_of(j * bk, bk), bk)
        vt = mm(ident, qkv_ref[at, 2 * width : 3 * width], NT).astype(BF16)
        for h in range(heads):
            vt_ref[h * 80 : h * 80 + 64, at] = vt[h * 64 : (h + 1) * 64]
            vt_ref[h * 80 + 64 : (h + 1) * 80, at] = jnp.ones((16, bk), BF16)
        return c

    lax.fori_loop(0, total // bk, prep, 0)

    def q_step(i, c):
        side, y = i // 2, i % 2
        qi = pl.multiple_of(y * (4 * bq) + (core ^ side) * (2 * bq) + chunk * bq, bq)
        lo, hi = tile_range(starts, qi, bq, bk, total)
        seg_row = seg_ref[:, pl.ds(qi, bq)]
        acc_ref[...] = jnp.zeros_like(acc_ref)
        top_ref[...] = jnp.full_like(top_ref, -3e38)
        qs = []
        for h in range(heads):
            p = h // 2
            qp = qkv_ref[pl.ds(qi, bq), p * 128 : (p + 1) * 128].astype(F32) * SCALE
            qs.append(head_masked(qp, h % 2))

        def score_step(j, c):
            kj = pl.multiple_of(j * bk, bk)
            far = far_tile(starts, seg_row, qi, kj, bk, bq)
            for h in range(heads):
                p = h // 2
                kp = qkv_ref[pl.ds(kj, bk), width + p * 128 : width + (p + 1) * 128]
                s = mm(kp, qs[h], NT) - far * slope_ref[h]
                s_ref[h, pl.ds(kj, bk)] = s
                top_ref[h] = jnp.maximum(top_ref[h], jnp.max(s.reshape(bk // 8, 8, bq), axis=0))
            return c

        lax.fori_loop(lo, hi, score_step, 0)
        tops = [jnp.max(top_ref[h], axis=0, keepdims=True) for h in range(heads)]

        def mix_step(j, c):
            kj = pl.multiple_of(j * bk, bk)
            for h in range(heads):
                e = jnp.exp(s_ref[h, pl.ds(kj, bk)] - tops[h]).astype(BF16)
                hs = slice(h * 80, (h + 1) * 80)
                acc_ref[hs] = acc_ref[hs] + mm(vt_ref[hs, pl.ds(kj, bk)], e, NN)
            return c

        lax.fori_loop(lo, hi, mix_step, 0)
        outs = []
        for h in range(heads):
            whole = acc_ref[h * 80 + 64 : h * 80 + 65]
            outs.append((acc_ref[h * 80 : h * 80 + 64] * (1.0 / whole)).astype(BF16))
            lse_ref[i, h : h + 1] = tops[h] + jnp.log(whole)
        ot = jnp.concatenate(outs, axis=0)
        here = pl.ds(pl.multiple_of(y * bq, bq), bq)
        mixed = mm(eye(bq), ot, NT).astype(BF16)
        out_ref[side, here] = mixed
        part = mm(mixed, w_ref[...], NN).astype(BF16)

        @pl.when(side == 0)
        def _():
            own_ref[here] = part

        for n, sib_ref in enumerate(sib_refs):
            first = n * strip % bq

            @pl.when((side == 1) & (y == n * strip // bq))
            def _(sib_ref=sib_ref, first=first):
                sib_ref[...] = part[first : first + strip]

        return c

    lax.fori_loop(0, 4, q_step, 0)


def attend(chunk, core, slopes, seg, w_out, pieces, ahead=()):
    total = seg.shape[1]
    rows = pieces[0].shape[1]
    heads = pieces[0].shape[2] // (3 * HEAD_DIM)
    width = heads * HEAD_DIM
    bk = 256
    smem = pl.BlockSpec(memory_space=pltpu.SMEM)
    vmem = pl.BlockSpec(memory_space=pltpu.VMEM)
    hbm = pl.BlockSpec(memory_space=pl.ANY)
    return pl.pallas_call(
        functools.partial(fwd_kernel, heads, bk, chunk),
        out_shape=(
            jax.ShapeDtypeStruct((2, 2 * rows, width), BF16),
            jax.ShapeDtypeStruct((4, heads, rows), F32),
            jax.ShapeDtypeStruct((2 * rows, w_out.shape[1]), BF16),
        )
        + (jax.ShapeDtypeStruct((2 * rows // PARTS, w_out.shape[1]), BF16),) * PARTS,
        in_specs=[smem, smem] + [vmem] * 6 + [hbm] * len(ahead),
        out_specs=(vmem,) * (3 + PARTS),
        scratch_shapes=[
            pltpu.VMEM((total, 3 * width), BF16),
            pltpu.VMEM((heads * 80, total), BF16),
            pltpu.VMEM((heads * 80, rows), F32),
            pltpu.VMEM((heads, total, rows), F32),
            pltpu.VMEM((heads, 8, rows), F32),
        ],
        compiler_params=pltpu.CompilerParams(vmem_limit_bytes=28 << 20),
        name="attend",
    )(core, slopes, seg, w_out, *pieces, *ahead)


def bwd_kernel(heads, bk, chunk, *refs):
    core_ref, slope_ref, seg_ref, q00, q01, q10, q11, do0, do1, o_ref, lse_ref = refs[:11]
    if chunk == 0:
        dq_ref, dkv_ref = refs[-8:-6]
    else:
        dq_in, dkv_in = refs[11:13]
        dqkv_ref = refs[-7]
    qkv_ref, kt_ref, dqt_ref, dk_ref, dv_ref, delta_ref = refs[-6:]
    total = seg_ref.shape[1]
    width = heads * HEAD_DIM
    bq = o_ref.shape[1] // 2
    core = core_ref[0]
    load_pieces(core, (q00, q01, q10, q11), qkv_ref)
    starts = starts_of(seg_ref[...])
    ident = eye(width)
    hr = lax.broadcasted_iota(jnp.int32, (8, width), 0)
    hc = lax.broadcasted_iota(jnp.int32, (8, width), 1)
    pick = jnp.where(hr == hc // HEAD_DIM, 1.0, 0.0)

    def prep(j, c):
        at = pl.ds(pl.multiple_of(j * bk, bk), bk)
        kj = qkv_ref[at, width : 2 * width]
        kt_ref[:, at] = (mm(ident, kj, NT) * SCALE).astype(BF16)
        if chunk == 0:
            dk_ref[at] = jnp.zeros((bk, width), F32)
            dv_ref[at] = jnp.zeros((bk, width), F32)
        else:
            dk_ref[at] = dkv_in[at, :width]
            dv_ref[at] = dkv_in[at, width:]
        return c

    lax.fori_loop(0, total // bk, prep, 0)
    for side, do_ref in enumerate((do0, do1)):
        for y in range(2):
            at = slice(y * bq, (y + 1) * bq)
            prod = do_ref[at].astype(F32) * o_ref[side, at].astype(F32)
            delta_ref[side * 2 + y] = lax.dot_general(
                pick, prod, NT, precision=lax.Precision.HIGHEST, preferred_element_type=F32
            )

    for side, do_ref in enumerate((do0, do1)):

        def q_step(y, c, side=side, do_ref=do_ref):
            i = side * 2 + y
            qi = pl.multiple_of(y * (4 * bq) + (core ^ side) * (2 * bq) + chunk * bq, bq)
            here = pl.ds(pl.multiple_of(y * bq, bq), bq)
            lo, hi = tile_range(starts, qi, bq, bk, total)
            seg_row = seg_ref[:, pl.ds(qi, bq)]
            dqt_ref[...] = jnp.zeros_like(dqt_ref)
            qs, dos = [], []
            for h in range(heads):
                p = h // 2
                qp = qkv_ref[pl.ds(qi, bq), p * 128 : (p + 1) * 128].astype(F32) * SCALE
                qs.append(head_masked(qp, h % 2))
                dp = do_ref[here, p * 128 : (p + 1) * 128].astype(F32)
                dos.append(head_masked(dp, h % 2))
            lses = [lse_ref[i, h : h + 1] for h in range(heads)]
            deltas = [delta_ref[i, h : h + 1] for h in range(heads)]

            def k_step(j, c):
                kj = pl.multiple_of(j * bk, bk)
                at = pl.ds(kj, bk)
                far = far_tile(starts, seg_row, qi, kj, bk, bq)
                for p in range(heads // 2):
                    cols = slice(p * 128, (p + 1) * 128)
                    kp = qkv_ref[at, width + p * 128 : width + (p + 1) * 128]
                    vp = qkv_ref[at, 2 * width + p * 128 : 2 * width + (p + 1) * 128]
                    dv = dv_ref[at, cols]
                    dk = dk_ref[at, cols]
                    for h in (2 * p, 2 * p + 1):
                        s = mm(kp, qs[h], NT) - far * slope_ref[h]
                        w = jnp.exp(s - lses[h])
                        dw = mm(vp, dos[h], NT)
                        ds = (w * (dw - deltas[h])).astype(BF16)
                        dv = dv + mm(w.astype(BF16), dos[h], NN)
                        dk = dk + mm(ds, qs[h], NN)
                        hs = slice(h * HEAD_DIM, (h + 1) * HEAD_DIM)
                        dqt_ref[hs] = dqt_ref[hs] + mm(kt_ref[hs, at], ds, NN)
                    dv_ref[at, cols] = dv
                    dk_ref[at, cols] = dk
                return c

            lax.fori_loop(lo, hi, k_step, 0)
            dq = mm(eye(bq), dqt_ref[...].astype(BF16), NT).astype(BF16)
            if chunk == 0:
                dq_ref[side, here] = dq
            else:
                dqkv_ref[2 + side, here, :width] = dq
            return c

        lax.fori_loop(0, 2, q_step, 0)

    if chunk == 0:

        def finish(j, c):
            at = pl.ds(pl.multiple_of(j * bk, bk), bk)
            dkv_ref[at, :width] = dk_ref[at]
            dkv_ref[at, width:] = dv_ref[at]
            return c

        lax.fori_loop(0, total // bk, finish, 0)
    else:
        for side in range(2):
            dqkv_ref[side, :, :width] = dq_in[side]
        for n in range(4):
            part, side = n // 2, n % 2
            for y in range(2):
                first = y * (4 * bq) + (core ^ side) * (2 * bq) + part * bq
                at = pl.ds(pl.multiple_of(first, bq), bq)
                here = slice(y * bq, (y + 1) * bq)
                dqkv_ref[n, here, width : 2 * width] = dk_ref[at].astype(BF16)
                dqkv_ref[n, here, 2 * width :] = dv_ref[at].astype(BF16)


def attend_back(chunk, core, slopes, seg, pieces, d_heads, heads_out, lse, before=(), ahead=()):
    total = seg.shape[1]
    rows = pieces[0].shape[1]
    heads = pieces[0].shape[2] // (3 * HEAD_DIM)
    width = heads * HEAD_DIM
    bk = 256
    smem = pl.BlockSpec(memory_space=pltpu.SMEM)
    vmem = pl.BlockSpec(memory_space=pltpu.VMEM)
    hbm = pl.BlockSpec(memory_space=pl.ANY)
    if chunk == 0:
        out_shape = (
            jax.ShapeDtypeStruct((2, 2 * rows, width), BF16),
            jax.ShapeDtypeStruct((total, 2 * width), F32),
        )
        out_specs = (vmem, vmem)
    else:
        out_shape = jax.ShapeDtypeStruct((4, 2 * rows, 3 * width), BF16)
        out_specs = vmem
    return pl.pallas_call(
        functools.partial(bwd_kernel, heads, bk, chunk),
        out_shape=out_shape,
        in_specs=[smem, smem] + [vmem] * (9 + len(before)) + [hbm] * len(ahead),
        out_specs=out_specs,
        scratch_shapes=[
            pltpu.VMEM((total, 3 * width), BF16),
            pltpu.VMEM((width, total), BF16),
            pltpu.VMEM((width, rows), F32),
            pltpu.VMEM((total, width), F32),
            pltpu.VMEM((total, width), F32),
            pltpu.VMEM((4, 8, rows), F32),
        ],
        compiler_params=pltpu.CompilerParams(vmem_limit_bytes=34 << 20),
        name="attend_back",
    )(core, slopes, seg, *pieces, *d_heads, heads_out, lse, *before, *ahead)


def swap(value, axis, bit):
    pairs = [(source, source ^ (1 << bit)) for source in range(lax.axis_size(axis))]
    return lax.ppermute(value, axis, pairs)


core_swap = functools.partial(swap, axis="tensor", bit=0)
chip_swap = functools.partial(swap, axis="tensor", bit=1)
partner_swap = functools.partial(swap, axis="section", bit=0)


def add_low(*terms):
    return sum(term.astype(F32) for term in terms).astype(BF16)


def group_steps():
    steps = [("section", 0)]
    for bit in range((lax.axis_size("dp") - 1).bit_length()):
        steps.append(("dp", bit))
    return steps


def gate(values, *ahead):
    hbm = pl.BlockSpec(memory_space=pl.ANY)
    many = isinstance(values, (list, tuple))
    values = tuple(values) if many else (values,)
    out = pl.pallas_call(
        lambda *refs: None,
        out_shape=tuple(jax.ShapeDtypeStruct(value.shape, value.dtype) for value in values),
        in_specs=[hbm] * (len(values) + len(ahead)),
        out_specs=(hbm,) * len(values),
        input_output_aliases={n: n for n in range(len(values))},
        name="gate",
    )(*values, *ahead)
    return out if many else out[0]


def fold_kernel(halving, mine_ref, kept_ref, came_ref, *refs):
    total = (kept_ref[...].astype(F32) + came_ref[...].astype(F32)).astype(BF16)
    if halving:
        put_halves(mine_ref[0], total, *refs[-2:])
    else:
        refs[-1][...] = total


def put_halves(mine, total, kept_ref, sent_ref, half=None):
    rows = kept_ref.shape[0]
    for n in range(2) if half is None else (half,):
        part = total[n * rows : (n + 1) * rows] if half is None else total

        @pl.when(mine == n)
        def _(part=part):
            kept_ref[...] = part

        @pl.when(mine != n)
        def _(part=part):
            sent_ref[...] = part


def fold(kept, came, mine, ahead):
    rows, width = kept.shape
    vmem = pl.BlockSpec(memory_space=pltpu.VMEM)
    halving = mine is not None
    shape = jax.ShapeDtypeStruct((rows // 2 if halving else rows, width), BF16)
    scalar = mine if halving else jnp.int32(0)
    out = pl.pallas_call(
        functools.partial(fold_kernel, halving),
        out_shape=(shape,) * (2 if halving else 1),
        in_specs=[pl.BlockSpec(memory_space=pltpu.SMEM), vmem, vmem]
        + [pl.BlockSpec(memory_space=pl.ANY)] * len(ahead),
        out_specs=(vmem,) * (2 if halving else 1),
        compiler_params=pltpu.CompilerParams(vmem_limit_bytes=12 << 20),
        name="fold",
    )(scalar.reshape(1), kept, came, *ahead)
    return out if halving else (out[0], None)


def join_kernel(mine_ref, value_ref, came_ref, *refs):
    out_ref = refs[-1]
    rows = value_ref.shape[0]
    mine = mine_ref[0]
    out_ref[pl.ds(pl.multiple_of(mine * rows, rows), rows)] = value_ref[...]
    out_ref[pl.ds(pl.multiple_of((1 - mine) * rows, rows), rows)] = came_ref[...]


def join(value, came, mine, ahead):
    rows, width = value.shape
    if rows % 16:
        came = gate(came, *ahead) if ahead else came
        first = mine == 0
        return jnp.concatenate(
            [jnp.where(first, value, came), jnp.where(first, came, value)], axis=0
        )
    vmem = pl.BlockSpec(memory_space=pltpu.VMEM)
    return pl.pallas_call(
        join_kernel,
        out_shape=jax.ShapeDtypeStruct((2 * rows, width), BF16),
        in_specs=[pl.BlockSpec(memory_space=pltpu.SMEM), vmem, vmem]
        + [pl.BlockSpec(memory_space=pl.ANY)] * len(ahead),
        out_specs=vmem,
        compiler_params=pltpu.CompilerParams(vmem_limit_bytes=12 << 20),
        name="join",
    )(mine.reshape(1), value, came, *ahead)


class GroupSum:
    def __init__(self, kept, sent, steps, mines):
        self.steps, self.mines = steps, mines
        self.count, self.kept = 0, kept
        self.done = False
        self.came = swap(sent, *steps[0])

    def step(self, *ahead):
        levels = len(self.steps)
        self.count += 1
        if self.count <= levels:
            following = self.mines[self.count] if self.count < levels else None
            rows = self.kept.shape[0]
            if self.count < levels and rows % 32:
                came = gate(self.came, *ahead) if ahead else self.came
                halves = add_low(self.kept, came).reshape(2, rows // 2, -1)
                self.kept = lax.dynamic_index_in_dim(halves, following, 0, keepdims=False)
                sent = lax.dynamic_index_in_dim(halves, 1 - following, 0, keepdims=False)
            else:
                self.kept, sent = fold(self.kept, self.came, following, ahead)
            if self.count < levels:
                self.came = swap(sent, *self.steps[self.count])
        else:
            level = 2 * levels - self.count
            self.kept = join(self.kept, self.came, self.mines[level], ahead)
        if self.count == 2 * levels:
            self.done = True
        elif self.count >= levels:
            self.came = swap(self.kept, *self.steps[2 * levels - 1 - self.count])
        return self.kept


def grads_kernel(mine_ref, *refs):
    norms, d_qkv_ref, heads, d_rows = refs[:4], refs[4], refs[5:7], refs[7:11]
    kept_ref, sent_ref, held_ref = refs[-3:]
    width = d_qkv_ref.shape[2]
    strip = 256
    half = kept_ref.shape[0]
    for n in range(2):
        for first in range(0, half, strip):
            at = slice(n * half + first, n * half + first + strip)
            to = slice(first, first + strip)
            total = sum(mm(norms[k][:, at], d_qkv_ref[k], TN) for k in range(4))
            held_ref[to, :width] = total.astype(BF16)
            total = sum(mm(d_rows[k][:, at], heads[k // 2][k % 2], TN) for k in range(4))
            held_ref[to, width:] = total.astype(BF16)
        put_halves(mine_ref[0], held_ref[...], kept_ref, sent_ref, half=n)


def late_grads(mine, norms, d_qkv, heads_out, d_rows, ahead):
    depth = norms[0].shape[1]
    width = d_qkv.shape[2] + heads_out[0].shape[2]
    vmem = pl.BlockSpec(memory_space=pltpu.VMEM)
    shape = jax.ShapeDtypeStruct((depth // 2, width), BF16)
    return pl.pallas_call(
        grads_kernel,
        out_shape=(shape, shape),
        in_specs=[pl.BlockSpec(memory_space=pltpu.SMEM)]
        + [vmem] * 11
        + [pl.BlockSpec(memory_space=pl.ANY)] * len(ahead),
        out_specs=(vmem, vmem),
        scratch_shapes=[pltpu.VMEM((depth // 2, width), BF16)],
        compiler_params=pltpu.CompilerParams(vmem_limit_bytes=32 << 20),
        name="late_grads",
    )(mine.reshape(1), *norms, d_qkv, *heads_out, *d_rows, *ahead)


def row_stats(values):
    row_mean = jnp.mean(values, axis=-1, keepdims=True)
    centered = values - row_mean
    inv_std = lax.rsqrt(jnp.mean(centered * centered, axis=-1, keepdims=True) + EPSILON)
    return centered * inv_std, inv_std


def norm_kernel(base_ref, mine_ref, other_ref, gain_ref, shift_ref, *refs):
    value_ref, low_ref = refs[-2:]
    value = base_ref[...] + (mine_ref[...].astype(F32) + other_ref[...].astype(F32))
    value_ref[...] = value
    normed, _ = row_stats(value)
    low_ref[...] = (normed * gain_ref[...] + shift_ref[...]).astype(BF16)


def norm_rows(base, mine, other, gain, shift, ahead=(), tile=128):
    rows, width = mine.shape
    wide = pl.BlockSpec((tile, width), lambda i: (i, 0))
    one = pl.BlockSpec((1, width), lambda i: (0, 0))
    return pl.pallas_call(
        norm_kernel,
        grid=(rows // tile,),
        out_shape=(
            jax.ShapeDtypeStruct((rows, width), F32),
            jax.ShapeDtypeStruct((rows, width), BF16),
        ),
        in_specs=[wide if base.shape[0] == rows else one, wide, wide, one, one]
        + [pl.BlockSpec(memory_space=pl.ANY)] * len(ahead),
        out_specs=(wide, wide),
        compiler_params=pltpu.CompilerParams(vmem_limit_bytes=24 << 20),
        name="norm_rows",
    )(base, mine, other, gain[None], shift[None], *ahead)


def back_kernel(past_ref, value_ref, mine_ref, other_ref, gain_ref, sums_in, *refs):
    grad_ref, low_ref, sums_ref = refs[-3:]
    d_output = mine_ref[...].astype(F32) + other_ref[...].astype(F32)
    normed, inv_std = row_stats(value_ref[...])
    d_normed = d_output * gain_ref[...]
    grad = past_ref[...].astype(F32) + inv_std * (
        d_normed
        - jnp.mean(d_normed, axis=-1, keepdims=True)
        - normed * jnp.mean(d_normed * normed, axis=-1, keepdims=True)
    )
    grad_ref[...] = grad
    low_ref[...] = grad.astype(BF16)

    @pl.when(pl.program_id(0) == 0)
    def _():
        sums_ref[...] = sums_in[...]

    for n, terms in enumerate((d_output * normed, d_output, grad)):
        part = jnp.sum(terms.reshape(-1, 8, terms.shape[1]), axis=0)
        sums_ref[n] = sums_ref[n] + part


def norm_back_rows(past, value, mine, other, gain, sums, ahead=(), tile=128):
    rows, width = mine.shape
    wide = pl.BlockSpec((tile, width), lambda i: (i, 0))
    one = pl.BlockSpec((1, width), lambda i: (0, 0))
    kept = pl.BlockSpec((3, 8, width), lambda i: (0, 0, 0))
    return pl.pallas_call(
        back_kernel,
        grid=(rows // tile,),
        out_shape=(
            jax.ShapeDtypeStruct((rows, width), F32),
            jax.ShapeDtypeStruct((rows, width), BF16),
            jax.ShapeDtypeStruct((3, 8, width), F32),
        ),
        in_specs=[wide, wide, wide, wide, one, kept]
        + [pl.BlockSpec(memory_space=pl.ANY)] * len(ahead),
        out_specs=(wide, wide, kept),
        compiler_params=pltpu.CompilerParams(vmem_limit_bytes=24 << 20),
        name="norm_back",
    )(past, value, mine, other, gain[None], sums, *ahead)


def feed_kernel(chunk, core_ref, up_ref, bias_ref, down_ref, own_ref, sib_ref, cot_ref, *refs):
    act_ref, grads_ref, bias_out, dn_own, *dn_sib = refs[-8 - PARTS : -4]
    cot_v, d_pre_ref, bias_acc, sems = refs[-4:]
    rows = own_ref.shape[0] // 2
    core = core_ref[0]
    copies = []
    for i in range(4):
        side, y = i // 2, i % 2
        first = y * (4 * rows) + (core ^ side) * (2 * rows) + chunk * rows
        copy = pltpu.make_async_copy(
            cot_ref.at[pl.ds(pl.multiple_of(first, rows), rows)],
            cot_v.at[i * rows : (i + 1) * rows],
            sems.at[i],
        )
        copy.start()
        copies.append(copy)
    bias_acc[...] = refs[1][...] if chunk else jnp.zeros_like(bias_acc)
    for copy in copies:
        copy.wait()
    for side, n_ref in enumerate((own_ref, sib_ref)):
        for y in range(2):
            here = slice(y * rows, (y + 1) * rows)
            there = slice((side * 2 + y) * rows, (side * 2 + y + 1) * rows)
            pre = mm(n_ref[here], up_ref[...], NN) + bias_ref[...]
            d_act = mm(cot_v[there], down_ref[...], NT)
            cdf = 0.5 + 0.5 * lax.erf(pre * ROOT_HALF)
            act_ref[side, here] = (pre * cdf).astype(BF16)
            slope = cdf + pre * jnp.exp(-0.5 * pre * pre) * INV_ROOT_TAU
            d_pre = (d_act * slope).astype(BF16)
            d_pre_ref[there] = d_pre
            parts = d_pre.astype(F32).reshape(-1, 8, d_pre.shape[1])
            bias_acc[...] = bias_acc[...] + jnp.sum(parts, axis=0)
            d_norm = mm(d_pre, up_ref[...], NT).astype(BF16)
            if side == 0:
                dn_own[here] = d_norm
            else:
                strip = dn_sib[0].shape[0]
                for n in range(rows // strip):
                    dn_sib[y * rows // strip + n][...] = d_norm[n * strip : (n + 1) * strip]
    bias_out[...] = bias_acc[...]
    own_rows, sib_rows = slice(0, 2 * rows), slice(2 * rows, 4 * rows)
    units = act_ref.shape[2]
    strip = 256
    for first in range(0, units, strip):
        at = slice(first, first + strip)
        total = mm(act_ref[0, :, at], cot_v[own_rows], TN) + mm(
            act_ref[1, :, at], cot_v[sib_rows], TN
        )
        if chunk:
            total = total + refs[0][at]
        grads_ref[at] = total.astype(grads_ref.dtype)
    for first in range(0, own_ref.shape[1], strip):
        at, to = slice(first, first + strip), slice(units + first, units + first + strip)
        total = mm(own_ref[:, at], d_pre_ref[own_rows], TN) + mm(
            sib_ref[:, at], d_pre_ref[sib_rows], TN
        )
        if chunk:
            total = total + refs[0][to]
        grads_ref[to] = total.astype(grads_ref.dtype)


def feed(chunk, core, w_up, c_up, w_down, own, sib, cot, before=()):
    rows, width = own.shape
    units = w_up.shape[1]
    vmem = pl.BlockSpec(memory_space=pltpu.VMEM)
    return pl.pallas_call(
        functools.partial(feed_kernel, chunk),
        out_shape=(
            jax.ShapeDtypeStruct((2, rows, units), BF16),
            jax.ShapeDtypeStruct((units + width, width), BF16 if chunk else F32),
            jax.ShapeDtypeStruct((8, units), F32),
            jax.ShapeDtypeStruct((rows, width), BF16),
        )
        + (jax.ShapeDtypeStruct((rows // PARTS, width), BF16),) * PARTS,
        in_specs=[pl.BlockSpec(memory_space=pltpu.SMEM)]
        + [vmem] * 5
        + [pl.BlockSpec(memory_space=pl.ANY)]
        + [vmem] * len(before),
        out_specs=(vmem,) * (4 + PARTS),
        scratch_shapes=[
            pltpu.VMEM((2 * rows, width), BF16),
            pltpu.VMEM((2 * rows, units), BF16),
            pltpu.VMEM((8, units), F32),
            pltpu.SemaphoreType.DMA((4,)),
        ],
        compiler_params=pltpu.CompilerParams(vmem_limit_bytes=44 << 20),
        name="feed",
    )(core, w_up, c_up[None], w_down, own, sib, cot, *before)


def row_copies(core, chunk, rows, source, target, sems, reverse=False):
    copies = []
    for i in range(4):
        side, y = i // 2, i % 2
        first = y * (4 * rows) + (core ^ side) * (2 * rows) + chunk * rows
        whole = pl.ds(pl.multiple_of(first, rows), rows)
        here = slice(i * rows, (i + 1) * rows)
        if reverse:
            copy = pltpu.make_async_copy(source.at[here], target.at[whole], sems.at[i])
        else:
            copy = pltpu.make_async_copy(source.at[whole], target.at[here], sems.at[i])
        copy.start()
        copies.append(copy)
    return copies


def skip_grad_kernel(chunk, core_ref, own_ref, sib_ref, dec_ref, enc_ref, *refs):
    outs, (dec_v, enc_v, sems) = refs[2 * chunk : -3], refs[-3:]
    rows = own_ref.shape[0] // 2
    width, cols = dec_v.shape[1], own_ref.shape[1]
    copies = row_copies(core_ref[0], chunk, rows, dec_ref, dec_v, sems.at[0])
    for i in range(4):
        side, y = i // 2, i % 2
        first = (y * 2 + (core_ref[0] ^ side)) * rows
        copy = pltpu.make_async_copy(
            enc_ref.at[pl.ds(pl.multiple_of(first, rows), rows)],
            enc_v.at[i * rows : (i + 1) * rows],
            sems.at[1, i],
        )
        copy.start()
        copies.append(copy)
    for copy in copies:
        copy.wait()
    half = 2 * rows
    for n, part in enumerate((dec_v, enc_v)):
        at = slice(n * width, (n + 1) * width)
        total = mm(part[:half], own_ref[...], TN) + mm(part[half:], sib_ref[...], TN)
        if not chunk:
            outs[0][at] = total
            continue
        total = (total + refs[0][at]).astype(BF16)
        side = jnp.zeros((width, 128), BF16)
        if n == 0:
            small = refs[1]
            lines = [
                small[k : k + 1, j * 128 : (j + 1) * 128] for k in range(8) for j in range(cols // 128)
            ]
            spare = jnp.zeros((width - len(lines), 128), F32)
            side = jnp.concatenate(lines + [spare], axis=0).astype(BF16)
        put_halves(core_ref[1], jnp.concatenate([total, side], axis=1), *outs, half=n)


def skip_grad(chunk, core, own, sib, dec, enc, before=()):
    rows, cols = own.shape
    width = dec.shape[1]
    vmem = pl.BlockSpec(memory_space=pltpu.VMEM)
    hbm = pl.BlockSpec(memory_space=pl.ANY)
    half = jax.ShapeDtypeStruct((width, cols + 128), BF16)
    return pl.pallas_call(
        functools.partial(skip_grad_kernel, chunk),
        out_shape=(half, half) if chunk else (jax.ShapeDtypeStruct((2 * width, cols), F32),),
        in_specs=[pl.BlockSpec(memory_space=pltpu.SMEM), vmem, vmem, hbm, hbm]
        + [vmem] * len(before),
        out_specs=(vmem,) * (1 + chunk),
        scratch_shapes=[
            pltpu.VMEM((2 * rows, width), BF16),
            pltpu.VMEM((2 * rows, width), BF16),
            pltpu.SemaphoreType.DMA((2, 4)),
        ],
        compiler_params=pltpu.CompilerParams(vmem_limit_bytes=24 << 20),
        name="skip_grad",
    )(core, own, sib, dec, enc, *before)


def skip_back_kernel(chunk, core_ref, w_ref, own_ref, sib_ref, *refs):
    back_ref, whole_ref, held, sems = refs[-4:]
    rows = own_ref.shape[0] // 2
    for side, part in enumerate((own_ref, sib_ref)):
        at = slice(side * 2 * rows, (side + 1) * 2 * rows)
        back_ref[at] = mm(part[...], w_ref[1], NT).astype(BF16)
        held[at] = mm(part[...], w_ref[0], NT)
    for copy in row_copies(core_ref[0], chunk, rows, held, whole_ref, sems, reverse=True):
        copy.wait()


def skip_back(chunk, core, w_skip, own, sib, group_rows, before=(), ahead=()):
    rows = own.shape[0]
    width = w_skip.shape[1]
    vmem = pl.BlockSpec(memory_space=pltpu.VMEM)
    hbm = pl.BlockSpec(memory_space=pl.ANY)
    return pl.pallas_call(
        functools.partial(skip_back_kernel, chunk),
        out_shape=(
            jax.ShapeDtypeStruct((2 * rows, width), BF16),
            jax.ShapeDtypeStruct((group_rows, width), F32),
        ),
        in_specs=[pl.BlockSpec(memory_space=pltpu.SMEM), vmem, vmem, vmem]
        + [hbm] * (len(before) + len(ahead)),
        out_specs=(vmem, hbm),
        scratch_shapes=[pltpu.VMEM((2 * rows, width), F32), pltpu.SemaphoreType.DMA((4,))],
        input_output_aliases={4: 1} if before else {},
        compiler_params=pltpu.CompilerParams(vmem_limit_bytes=24 << 20),
        name="skip_back",
    )(core, w_skip, own, sib, *before, *ahead)


def restore_kernel(core_ref, *refs):
    out_ref = refs[-1]
    for chunk, part in enumerate(refs[:-1]):
        rows = part.shape[0] // 4
        for i in range(4):
            side, y = i // 2, i % 2
            first = y * (4 * rows) + (core_ref[0] ^ side) * (2 * rows) + chunk * rows
            out_ref[pl.ds(pl.multiple_of(first, rows), rows)] = part[i * rows : (i + 1) * rows]


def restore(core, parts):
    vmem = pl.BlockSpec(memory_space=pltpu.VMEM)
    rows, width = parts[0].shape
    return pl.pallas_call(
        restore_kernel,
        out_shape=jax.ShapeDtypeStruct((rows * len(parts), width), parts[0].dtype),
        in_specs=[pl.BlockSpec(memory_space=pltpu.SMEM)] + [vmem] * len(parts),
        out_specs=vmem,
        compiler_params=pltpu.CompilerParams(vmem_limit_bytes=12 << 20),
        name="restore",
    )(core, *parts)


def skip_kernel(chunk, core_ref, w_ref, dec_ref, enc_ref, own_ref, *refs):
    sib_refs, (dec_v, enc_v, sems) = refs[:PARTS], refs[PARTS:]
    rows = own_ref.shape[0] // 2
    copies = row_copies(core_ref[0], chunk, rows, dec_ref, dec_v, sems.at[0])
    for i in range(4):
        side, y = i // 2, i % 2
        first = (y * 2 + (core_ref[0] ^ side)) * rows
        copy = pltpu.make_async_copy(
            enc_ref.at[pl.ds(pl.multiple_of(first, rows), rows)],
            enc_v.at[i * rows : (i + 1) * rows],
            sems.at[1, i],
        )
        copy.start()
        copies.append(copy)
    for copy in copies:
        copy.wait()
    half = 2 * rows
    strip = half // PARTS
    for n, sib_ref in enumerate(sib_refs):
        at = slice(half + n * strip, half + (n + 1) * strip)
        sib_ref[...] = (mm(dec_v[at], w_ref[0], NN) + mm(enc_v[at], w_ref[1], NN)).astype(BF16)
    own_ref[...] = (mm(dec_v[:half], w_ref[0], NN) + mm(enc_v[:half], w_ref[1], NN)).astype(BF16)


def skip(chunk, core, w_skip, dec, enc):
    rows = enc.shape[0] // 2
    width, cols = w_skip.shape[1:]
    vmem = pl.BlockSpec(memory_space=pltpu.VMEM)
    hbm = pl.BlockSpec(memory_space=pl.ANY)
    return pl.pallas_call(
        functools.partial(skip_kernel, chunk),
        out_shape=(jax.ShapeDtypeStruct((rows, cols), BF16),)
        + (jax.ShapeDtypeStruct((rows // PARTS, cols), BF16),) * PARTS,
        in_specs=[pl.BlockSpec(memory_space=pltpu.SMEM), vmem, hbm, hbm],
        out_specs=(vmem,) * (1 + PARTS),
        scratch_shapes=[
            pltpu.VMEM((2 * rows, width), BF16),
            pltpu.VMEM((2 * rows, width), BF16),
            pltpu.SemaphoreType.DMA((2, 4)),
        ],
        compiler_params=pltpu.CompilerParams(vmem_limit_bytes=16 << 20),
        name="skip",
    )(core, w_skip, dec, enc)


def shards(
    decoder_in,
    encoder_out,
    segments,
    w_skip,
    b_skip,
    ln1_gain,
    ln1_bias,
    w_qkv,
    w_out,
    ln2_gain,
    ln2_bias,
    w_up,
    c_up,
    w_down,
    cotangent,
):
    group_rows = decoder_in.shape[0]
    tensor_rank = lax.axis_index("tensor")
    core = tensor_rank & 1
    chip = tensor_rank >> 1
    heads_here = HEADS // lax.axis_size("tensor")
    local_width = heads_here * HEAD_DIM
    block = group_rows // (4 * CHUNKS)
    qkv_matrix = w_qkv.reshape(D, 3 * local_width)
    steps = group_steps()
    mines = [((lax.axis_index(axis) >> bit) & 1).astype(jnp.int32) for axis, bit in steps]
    core_scalar = jnp.stack([core.astype(jnp.int32), mines[0]])
    slopes = jnp.exp2(
        -8.0
        * (tensor_rank * heads_here + jnp.arange(heads_here, dtype=jnp.int32) + 1).astype(F32)
        / HEADS
    )
    spots = [(chunk, side) for chunk in range(CHUNKS) for side in range(2)]

    def piece_of(array, chunk, side):
        width = array.shape[-1]
        parts = array.reshape(2, 2, CHUNKS, block, width)[:, :, chunk]
        return lax.dynamic_index_in_dim(parts, core ^ side, 1, keepdims=False).reshape(
            2 * block, width
        )

    cot = [piece_of(cotangent, chunk, 0) for chunk in range(CHUNKS)]
    encoder_parts = encoder_out.reshape(2, 2, CHUNKS, block, encoder_out.shape[1])
    partner = [
        partner_swap(encoder_parts[:, :, chunk].reshape(4 * block, -1)) for chunk in range(CHUNKS)
    ]

    def chip_total(half):
        sent = core_swap(half(1).astype(BF16))
        return (half(0) + sent.astype(F32)).astype(BF16)

    merged, norm_one, qkv = [], {}, {}
    sums = []
    for chunk in range(CHUNKS):
        own, *sib = skip(chunk, core_scalar, w_skip, decoder_in, partner[chunk])
        sums.append(add_low(own, jnp.concatenate([core_swap(part) for part in sib], axis=0)))
        if chunk + 1 < CHUNKS:
            partner[chunk + 1] = gate(partner[chunk + 1], sums[chunk])
    others = [chip_swap(part) for part in sums]
    ahead = (qkv_matrix, *sums)
    for chunk in range(CHUNKS):
        value, normal = norm_rows(
            b_skip[None], sums[chunk], others[chunk], ln1_gain, ln1_bias, ahead
        )
        merged.append(value)
        norm_one[chunk, 0] = normal
        norm_one[chunk, 1] = core_swap(normal)
        for side in range(2):
            qkv[chunk, side] = jnp.dot(
                norm_one[chunk, side], qkv_matrix, preferred_element_type=F32
            ).astype(BF16)
        ahead = (qkv[chunk, 0], qkv[chunk, 1], *cot)
    qkv_pieces = [qkv[spot].reshape(2, block, 3 * local_width) for spot in spots]

    heads_out, lse, sums = [], [], []
    for chunk in range(CHUNKS):
        mixed, log_total, own, *sib = attend(
            chunk, core_scalar, slopes, segments, w_out, qkv_pieces, sums
        )
        heads_out.append(mixed)
        lse.append(log_total)
        sums.append(add_low(own, jnp.concatenate([core_swap(part) for part in sib], axis=0)))
    others = [chip_swap(part) for part in sums]

    attended, activated, d_sums, d_others = [], [], [], []
    ahead = tuple(sums)
    grads = ()
    for chunk in range(CHUNKS):
        value, normal = norm_rows(
            merged[chunk], sums[chunk], others[chunk], ln2_gain, ln2_bias, ahead
        )
        attended.append(value)
        acts, weights_sum, bias_sum, own, *sib = feed(
            chunk, core_scalar, w_up, c_up, w_down, normal, core_swap(normal), cotangent, grads
        )
        grads = (weights_sum, bias_sum)
        activated.append(acts)
        sib = gate([core_swap(part) for part in sib], d_others[chunk - 1] if chunk else others[1])
        d_sums.append(add_low(own, jnp.concatenate(sib, axis=0)))
        d_others.append(chip_swap(d_sums[chunk]))
        ahead = (d_sums[chunk],)
    d_w_ff, c_up_sum = grads
    both = ("section", "dp")
    d_w_ff = lax.psum_scatter(
        gate(d_w_ff, d_sums[-1]), both, scatter_dimension=0, tiled=True
    )

    d_attended, d_attended_rows = [], {}
    sums_two = jnp.zeros((3, 8, D), F32)
    before = ()
    for chunk in range(CHUNKS):
        value, low, sums_two = norm_back_rows(
            cot[chunk], attended[chunk], d_sums[chunk], d_others[chunk], ln2_gain, sums_two,
            ahead,
        )
        d_attended.append(value)
        d_attended_rows[chunk, 0] = low
        d_attended_rows[chunk, 1] = core_swap(low)
        d_heads = [
            mm(d_attended_rows[chunk, side], w_out, NT).astype(BF16) for side in range(2)
        ]
        before = attend_back(
            chunk, core_scalar, slopes, segments, qkv_pieces, d_heads, heads_out[chunk],
            lse[chunk], before,
        )
        ahead = (before[0],)
    d_qkv = before

    sums = [
        chip_total(lambda side: mm(d_qkv[2 * chunk + side], qkv_matrix, NT))
        for chunk in range(CHUNKS)
    ]
    others = [chip_swap(part) for part in sums]
    kept, sent = late_grads(
        mines[0],
        [norm_one[spot] for spot in spots],
        d_qkv,
        heads_out,
        [d_attended_rows[spot] for spot in spots],
        sums,
    )
    late = GroupSum(kept, sent, steps, mines)
    activated = gate(activated, kept)
    down = [
        chip_total(
            lambda side: jnp.dot(activated[chunk][side], w_down, preferred_element_type=F32)
        )
        for chunk in range(CHUNKS)
    ]

    aways = [
        lax.dynamic_index_in_dim(part.reshape(2, block, D), 1 - chip, 0, keepdims=False)
        for part in down
    ]
    lows = []
    sums_one = jnp.zeros((3, 8, D), F32)
    ahead = (kept,)
    for chunk in range(CHUNKS):
        _, low, sums_one = norm_back_rows(
            d_attended[chunk], merged[chunk], sums[chunk], others[chunk], ln1_gain, sums_one, ahead
        )
        lows.append(low)
        if chunk == 0:
            ahead = (late.step(low, *aways),)
    d_w_ff = lax.all_gather(gate(d_w_ff, lows[0]), both, axis=0, tiled=True)
    sibs = [core_swap(low) for low in lows]
    small = jnp.sum(jnp.concatenate([sums_one, sums_two], axis=0), axis=1) * 0.5
    small = small + core_swap(small)
    small = small + chip_swap(small)
    small = jnp.concatenate([small, jnp.sum(c_up_sum, axis=0)[None]], axis=0)
    small = jnp.pad(small, ((0, 16 - small.shape[0]), (0, 0)))
    before = ()
    for chunk in range(CHUNKS):
        before = skip_grad(
            chunk, core_scalar, lows[chunk], sibs[chunk], decoder_in, partner[chunk],
            (*before, small) if chunk else (),
        )
    kept, sent = before
    last = GroupSum(kept, sent, steps, mines)
    d_encoder, before = [], ()
    for chunk in range(CHUNKS):
        returned, *before = skip_back(
            chunk, core_scalar, w_skip, lows[chunk], sibs[chunk], group_rows, before, (kept,)
        )
        d_encoder.append(returned)
    (d_decoder_in,) = before
    d_encoder_out = restore(core_scalar, [partner_swap(part) for part in d_encoder])
    last.step(*d_encoder)

    moved = [chip_swap(part) for part in gate(aways, lows[-1])]
    d_w_down, d_w_up = d_w_ff[: w_down.shape[0]].astype(F32), d_w_ff[w_down.shape[0] :].astype(F32)
    total = 2 * len(steps)
    while last.count < total - 1:
        if late.count < total - 1:
            late.step(last.kept)
        last.step()
    moved = gate(moved, last.kept)
    layer_out = []
    for chunk in range(CHUNKS):
        home, base = (
            lax.dynamic_index_in_dim(part.reshape(2, block, D), chip, 0, keepdims=False)
            for part in (down[chunk], attended[chunk])
        )
        layer_out.append(base + (home.astype(F32) + moved[chunk].astype(F32)))
    layer_out = jnp.concatenate(layer_out, axis=0)
    while not late.done:
        late.step(last.kept, d_w_down, d_w_up, layer_out)
    last.step(d_encoder_out)
    d_w_qkv = jnp.stack(
        [late.kept[:, n * local_width : (n + 1) * local_width] for n in range(3)], axis=0
    )
    d_w_qkv = jnp.transpose(d_w_qkv.astype(F32), (1, 0, 2))
    d_w_out = late.kept[:, 3 * local_width :].T
    d_w_skip = last.kept[:, :D].reshape(w_skip.shape)
    small = last.kept[: 8 * D // 128, D:].astype(F32).reshape(8, D)
    return (
        layer_out,
        d_decoder_in,
        d_encoder_out,
        d_w_skip.astype(F32),
        small[2],
        small[0],
        small[1],
        d_w_qkv.astype(F32),
        d_w_out.astype(F32),
        small[3],
        small[4],
        d_w_up,
        small[6],
        d_w_down,
    )


def solution(mesh):
    return jax.shard_map(
        shards,
        mesh=mesh,
        in_specs=(
            P(("section", "dp"), "tensor"),
            P(("section", "dp"), "tensor"),
            P(("section", "dp"), None),
            P(None, "tensor", None),
            P(),
            P(),
            P(),
            P(None, None, "tensor"),
            P("tensor", None),
            P(),
            P(),
            P(None, "tensor"),
            P("tensor"),
            P("tensor", None),
            P(("section", "dp"), None),
        ),
        out_specs=(
            P(("section", "dp", "tensor"), None),
            P(("section", "dp"), "tensor"),
            P(("section", "dp"), "tensor"),
            P(None, "tensor", None),
            P(),
            P(),
            P(),
            P(None, None, "tensor"),
            P("tensor", None),
            P(),
            P(),
            P(None, "tensor"),
            P("tensor"),
            P("tensor", None),
        ),
        check_vma=False,
    )
```

```python
import functools
import jax
import jax.numpy as jnp
from jax import lax
from jax.experimental import pallas as pl
from jax.experimental.pallas import tpu as pltpu
from jax.sharding import PartitionSpec as P

D = 1024
HEADS = 16
UTTS = 6
HEAD_DIM = D // HEADS
SCALE = HEAD_DIM**-0.5

EPSILON = 1e-05
FAR = 1e30
ROOT_HALF = 0.7071067811865476
INV_ROOT_TAU = 0.3989422804014327
BF16 = jnp.bfloat16
F32 = jnp.float32
NT = (((1,), (1,)), ((), ()))
NN = (((1,), (0,)), ((), ()))
TN = (((0,), (0,)), ((), ()))
CHUNKS = 2
PARTS = 4


def mm(left, right, dims):
    return lax.dot_general(left, right, dims, preferred_element_type=F32)


def starts_of(seg):
    return [jnp.sum((seg < u).astype(jnp.int32)) for u in range(1, UTTS)]


def tile_range(starts, first, count, tile, total):
    low = jnp.int32(0)
    high = jnp.int32(total)
    for s in starts:
        low = jnp.maximum(low, jnp.where(s <= first, s, 0))
        high = jnp.minimum(high, jnp.where(s >= first + count, s, total))
    return low // tile, (high + tile - 1) // tile


def eye(n):
    r = lax.broadcasted_iota(jnp.int32, (n, n), 0)
    c = lax.broadcasted_iota(jnp.int32, (n, n), 1)
    return jnp.where(r == c, 1.0, 0.0).astype(BF16)


def far_tile(starts, seg_row, q_first, k_first, bk, bq):
    kpos = k_first + lax.broadcasted_iota(jnp.int32, (bk, bq), 0)
    qpos = q_first + lax.broadcasted_iota(jnp.int32, (bk, bq), 1)
    lo = jnp.zeros_like(seg_row)
    hi = jnp.full_like(seg_row, starts[0])
    for u in range(1, UTTS):
        lo = jnp.where(seg_row == u, starts[u - 1], lo)
        hi = jnp.where(seg_row == u, starts[u] if u < UTTS - 1 else 1 << 30, hi)
    ok = (kpos >= lo) & (kpos < hi)
    return jnp.where(ok, jnp.abs(kpos - qpos).astype(F32), FAR)


def head_masked(pair, which):
    lane = lax.broadcasted_iota(jnp.int32, pair.shape, 1)
    keep = (lane < HEAD_DIM) if which == 0 else (lane >= HEAD_DIM)
    return jnp.where(keep, pair, 0.0).astype(BF16)


def load_pieces(core, pieces, whole_ref):
    rows = pieces[0].shape[1]
    for n, piece in enumerate(pieces):
        chunk, side = n // 2, n % 2
        for y in range(2):
            first = y * (4 * rows) + (core ^ side) * (2 * rows) + chunk * rows
            whole_ref[pl.ds(pl.multiple_of(first, rows), rows)] = piece[y]


def fwd_kernel(
    heads, bk, chunk, core_ref, slope_ref, seg_ref, w_ref, q00, q01, q10, q11, *refs
):
    out_ref, lse_ref, own_ref, *sib_refs = refs[-8 - PARTS : -5]
    qkv_ref, vt_ref, acc_ref, s_ref, top_ref = refs[-5:]
    strip = sib_refs[0].shape[0]
    total = seg_ref.shape[1]
    width = heads * HEAD_DIM
    bq = out_ref.shape[1] // 2
    core = core_ref[0]
    load_pieces(core, (q00, q01, q10, q11), qkv_ref)
    starts = starts_of(seg_ref[...])
    ident = eye(width)

    def prep(j, c):
        at = pl.ds(pl.multiple_of(j * bk, bk), bk)
        vt = mm(ident, qkv_ref[at, 2 * width : 3 * width], NT).astype(BF16)
        for h in range(heads):
            vt_ref[h * 80 : h * 80 + 64, at] = vt[h * 64 : (h + 1) * 64]
            vt_ref[h * 80 + 64 : (h + 1) * 80, at] = jnp.ones((16, bk), BF16)
        return c

    lax.fori_loop(0, total // bk, prep, 0)

    def q_step(i, c):
        side, y = i // 2, i % 2
        qi = pl.multiple_of(y * (4 * bq) + (core ^ side) * (2 * bq) + chunk * bq, bq)
        lo, hi = tile_range(starts, qi, bq, bk, total)
        seg_row = seg_ref[:, pl.ds(qi, bq)]
        acc_ref[...] = jnp.zeros_like(acc_ref)
        top_ref[...] = jnp.full_like(top_ref, -3e38)
        qs = []
        for h in range(heads):
            p = h // 2
            qp = qkv_ref[pl.ds(qi, bq), p * 128 : (p + 1) * 128].astype(F32) * SCALE
            qs.append(head_masked(qp, h % 2))

        def score_step(j, c):
            kj = pl.multiple_of(j * bk, bk)
            far = far_tile(starts, seg_row, qi, kj, bk, bq)
            for h in range(heads):
                p = h // 2
                kp = qkv_ref[pl.ds(kj, bk), width + p * 128 : width + (p + 1) * 128]
                s = mm(kp, qs[h], NT) - far * slope_ref[h]
                s_ref[h, pl.ds(kj, bk)] = s
                top_ref[h] = jnp.maximum(top_ref[h], jnp.max(s.reshape(bk // 8, 8, bq), axis=0))
            return c

        lax.fori_loop(lo, hi, score_step, 0)
        tops = [jnp.max(top_ref[h], axis=0, keepdims=True) for h in range(heads)]

        def mix_step(j, c):
            kj = pl.multiple_of(j * bk, bk)
            for h in range(heads):
                e = jnp.exp(s_ref[h, pl.ds(kj, bk)] - tops[h]).astype(BF16)
                hs = slice(h * 80, (h + 1) * 80)
                acc_ref[hs] = acc_ref[hs] + mm(vt_ref[hs, pl.ds(kj, bk)], e, NN)
            return c

        lax.fori_loop(lo, hi, mix_step, 0)
        outs = []
        for h in range(heads):
            whole = acc_ref[h * 80 + 64 : h * 80 + 65]
            outs.append((acc_ref[h * 80 : h * 80 + 64] * (1.0 / whole)).astype(BF16))
            lse_ref[i, h : h + 1] = tops[h] + jnp.log(whole)
        ot = jnp.concatenate(outs, axis=0)
        here = pl.ds(pl.multiple_of(y * bq, bq), bq)
        mixed = mm(eye(bq), ot, NT).astype(BF16)
        out_ref[side, here] = mixed
        part = mm(mixed, w_ref[...], NN).astype(BF16)

        @pl.when(side == 0)
        def _():
            own_ref[here] = part

        for n, sib_ref in enumerate(sib_refs):
            first = n * strip % bq

            @pl.when((side == 1) & (y == n * strip // bq))
            def _(sib_ref=sib_ref, first=first):
                sib_ref[...] = part[first : first + strip]

        return c

    lax.fori_loop(0, 4, q_step, 0)


def attend(chunk, core, slopes, seg, w_out, pieces, ahead=()):
    total = seg.shape[1]
    rows = pieces[0].shape[1]
    heads = pieces[0].shape[2] // (3 * HEAD_DIM)
    width = heads * HEAD_DIM
    bk = 512
    smem = pl.BlockSpec(memory_space=pltpu.SMEM)
    vmem = pl.BlockSpec(memory_space=pltpu.VMEM)
    hbm = pl.BlockSpec(memory_space=pl.ANY)
    return pl.pallas_call(
        functools.partial(fwd_kernel, heads, bk, chunk),
        out_shape=(
            jax.ShapeDtypeStruct((2, 2 * rows, width), BF16),
            jax.ShapeDtypeStruct((4, heads, rows), F32),
            jax.ShapeDtypeStruct((2 * rows, w_out.shape[1]), BF16),
        )
        + (jax.ShapeDtypeStruct((2 * rows // PARTS, w_out.shape[1]), BF16),) * PARTS,
        in_specs=[smem, smem] + [vmem] * 6 + [hbm] * len(ahead),
        out_specs=(vmem,) * (3 + PARTS),
        scratch_shapes=[
            pltpu.VMEM((total, 3 * width), BF16),
            pltpu.VMEM((heads * 80, total), BF16),
            pltpu.VMEM((heads * 80, rows), F32),
            pltpu.VMEM((heads, total, rows), F32),
            pltpu.VMEM((heads, 8, rows), F32),
        ],
        compiler_params=pltpu.CompilerParams(vmem_limit_bytes=28 << 20),
        name="attend",
    )(core, slopes, seg, w_out, *pieces, *ahead)


def bwd_kernel(heads, bk, chunk, *refs):
    core_ref, slope_ref, seg_ref, q00, q01, q10, q11, do0, do1, o_ref, lse_ref = refs[:11]
    if chunk == 0:
        dq_ref, dkv_ref = refs[-8:-6]
    else:
        dq_in, dkv_in = refs[11:13]
        dqkv_ref = refs[-7]
    qkv_ref, kt_ref, dqt_ref, dk_ref, dv_ref, delta_ref = refs[-6:]
    total = seg_ref.shape[1]
    width = heads * HEAD_DIM
    bq = o_ref.shape[1] // 2
    core = core_ref[0]
    load_pieces(core, (q00, q01, q10, q11), qkv_ref)
    starts = starts_of(seg_ref[...])
    ident = eye(width)
    hr = lax.broadcasted_iota(jnp.int32, (8, width), 0)
    hc = lax.broadcasted_iota(jnp.int32, (8, width), 1)
    pick = jnp.where(hr == hc // HEAD_DIM, 1.0, 0.0)

    def prep(j, c):
        at = pl.ds(pl.multiple_of(j * bk, bk), bk)
        kj = qkv_ref[at, width : 2 * width]
        kt_ref[:, at] = (mm(ident, kj, NT) * SCALE).astype(BF16)
        if chunk == 0:
            dk_ref[at] = jnp.zeros((bk, width), F32)
            dv_ref[at] = jnp.zeros((bk, width), F32)
        else:
            dk_ref[at] = dkv_in[at, :width]
            dv_ref[at] = dkv_in[at, width:]
        return c

    lax.fori_loop(0, total // bk, prep, 0)
    for side, do_ref in enumerate((do0, do1)):
        for y in range(2):
            at = slice(y * bq, (y + 1) * bq)
            prod = do_ref[at].astype(F32) * o_ref[side, at].astype(F32)
            delta_ref[side * 2 + y] = lax.dot_general(
                pick, prod, NT, precision=lax.Precision.HIGHEST, preferred_element_type=F32
            )

    for side, do_ref in enumerate((do0, do1)):

        def q_step(y, c, side=side, do_ref=do_ref):
            i = side * 2 + y
            qi = pl.multiple_of(y * (4 * bq) + (core ^ side) * (2 * bq) + chunk * bq, bq)
            here = pl.ds(pl.multiple_of(y * bq, bq), bq)
            lo, hi = tile_range(starts, qi, bq, bk, total)
            seg_row = seg_ref[:, pl.ds(qi, bq)]
            dqt_ref[...] = jnp.zeros_like(dqt_ref)
            qs, dos = [], []
            for h in range(heads):
                p = h // 2
                qp = qkv_ref[pl.ds(qi, bq), p * 128 : (p + 1) * 128].astype(F32) * SCALE
                qs.append(head_masked(qp, h % 2))
                dp = do_ref[here, p * 128 : (p + 1) * 128].astype(F32)
                dos.append(head_masked(dp, h % 2))
            lses = [lse_ref[i, h : h + 1] for h in range(heads)]
            deltas = [delta_ref[i, h : h + 1] for h in range(heads)]

            def k_step(j, c):
                kj = pl.multiple_of(j * bk, bk)
                at = pl.ds(kj, bk)
                far = far_tile(starts, seg_row, qi, kj, bk, bq)
                for p in range(heads // 2):
                    cols = slice(p * 128, (p + 1) * 128)
                    kp = qkv_ref[at, width + p * 128 : width + (p + 1) * 128]
                    vp = qkv_ref[at, 2 * width + p * 128 : 2 * width + (p + 1) * 128]
                    dv = dv_ref[at, cols]
                    dk = dk_ref[at, cols]
                    for h in (2 * p, 2 * p + 1):
                        s = mm(kp, qs[h], NT) - far * slope_ref[h]
                        w = jnp.exp(s - lses[h])
                        dw = mm(vp, dos[h], NT)
                        ds = (w * (dw - deltas[h])).astype(BF16)
                        dv = dv + mm(w.astype(BF16), dos[h], NN)
                        dk = dk + mm(ds, qs[h], NN)
                        hs = slice(h * HEAD_DIM, (h + 1) * HEAD_DIM)
                        dqt_ref[hs] = dqt_ref[hs] + mm(kt_ref[hs, at], ds, NN)
                    dv_ref[at, cols] = dv
                    dk_ref[at, cols] = dk
                return c

            lax.fori_loop(lo, hi, k_step, 0)
            dq = mm(eye(bq), dqt_ref[...].astype(BF16), NT).astype(BF16)
            if chunk == 0:
                dq_ref[side, here] = dq
            else:
                dqkv_ref[2 + side, here, :width] = dq
            return c

        lax.fori_loop(0, 2, q_step, 0)

    if chunk == 0:

        def finish(j, c):
            at = pl.ds(pl.multiple_of(j * bk, bk), bk)
            dkv_ref[at, :width] = dk_ref[at]
            dkv_ref[at, width:] = dv_ref[at]
            return c

        lax.fori_loop(0, total // bk, finish, 0)
    else:
        for side in range(2):
            dqkv_ref[side, :, :width] = dq_in[side]
        for n in range(4):
            part, side = n // 2, n % 2
            for y in range(2):
                first = y * (4 * bq) + (core ^ side) * (2 * bq) + part * bq
                at = pl.ds(pl.multiple_of(first, bq), bq)
                here = slice(y * bq, (y + 1) * bq)
                dqkv_ref[n, here, width : 2 * width] = dk_ref[at].astype(BF16)
                dqkv_ref[n, here, 2 * width :] = dv_ref[at].astype(BF16)


def attend_back(chunk, core, slopes, seg, pieces, d_heads, heads_out, lse, before=(), ahead=()):
    total = seg.shape[1]
    rows = pieces[0].shape[1]
    heads = pieces[0].shape[2] // (3 * HEAD_DIM)
    width = heads * HEAD_DIM
    bk = 512
    smem = pl.BlockSpec(memory_space=pltpu.SMEM)
    vmem = pl.BlockSpec(memory_space=pltpu.VMEM)
    hbm = pl.BlockSpec(memory_space=pl.ANY)
    if chunk == 0:
        out_shape = (
            jax.ShapeDtypeStruct((2, 2 * rows, width), BF16),
            jax.ShapeDtypeStruct((total, 2 * width), F32),
        )
        out_specs = (vmem, vmem)
    else:
        out_shape = jax.ShapeDtypeStruct((4, 2 * rows, 3 * width), BF16)
        out_specs = vmem
    return pl.pallas_call(
        functools.partial(bwd_kernel, heads, bk, chunk),
        out_shape=out_shape,
        in_specs=[smem, smem] + [vmem] * (9 + len(before)) + [hbm] * len(ahead),
        out_specs=out_specs,
        scratch_shapes=[
            pltpu.VMEM((total, 3 * width), BF16),
            pltpu.VMEM((width, total), BF16),
            pltpu.VMEM((width, rows), F32),
            pltpu.VMEM((total, width), F32),
            pltpu.VMEM((total, width), F32),
            pltpu.VMEM((4, 8, rows), F32),
        ],
        compiler_params=pltpu.CompilerParams(vmem_limit_bytes=34 << 20),
        name="attend_back",
    )(core, slopes, seg, *pieces, *d_heads, heads_out, lse, *before, *ahead)


def swap(value, axis, bit):
    pairs = [(source, source ^ (1 << bit)) for source in range(lax.axis_size(axis))]
    return lax.ppermute(value, axis, pairs)


core_swap = functools.partial(swap, axis="tensor", bit=0)
chip_swap = functools.partial(swap, axis="tensor", bit=1)
partner_swap = functools.partial(swap, axis="section", bit=0)


def add_low(*terms):
    return sum(term.astype(F32) for term in terms).astype(BF16)


def group_steps():
    steps = [("section", 0)]
    for bit in range((lax.axis_size("dp") - 1).bit_length()):
        steps.append(("dp", bit))
    return steps


def gate(values, *ahead):
    hbm = pl.BlockSpec(memory_space=pl.ANY)
    many = isinstance(values, (list, tuple))
    values = tuple(values) if many else (values,)
    out = pl.pallas_call(
        lambda *refs: None,
        out_shape=tuple(jax.ShapeDtypeStruct(value.shape, value.dtype) for value in values),
        in_specs=[hbm] * (len(values) + len(ahead)),
        out_specs=(hbm,) * len(values),
        input_output_aliases={n: n for n in range(len(values))},
        name="gate",
    )(*values, *ahead)
    return out if many else out[0]


def fold_kernel(halving, mine_ref, kept_ref, came_ref, *refs):
    total = (kept_ref[...].astype(F32) + came_ref[...].astype(F32)).astype(BF16)
    if halving:
        put_halves(mine_ref[0], total, *refs[-2:])
    else:
        refs[-1][...] = total


def put_halves(mine, total, kept_ref, sent_ref, half=None):
    rows = kept_ref.shape[0]
    for n in range(2) if half is None else (half,):
        part = total[n * rows : (n + 1) * rows] if half is None else total

        @pl.when(mine == n)
        def _(part=part):
            kept_ref[...] = part

        @pl.when(mine != n)
        def _(part=part):
            sent_ref[...] = part


def fold(kept, came, mine, ahead):
    rows, width = kept.shape
    vmem = pl.BlockSpec(memory_space=pltpu.VMEM)
    halving = mine is not None
    shape = jax.ShapeDtypeStruct((rows // 2 if halving else rows, width), BF16)
    scalar = mine if halving else jnp.int32(0)
    out = pl.pallas_call(
        functools.partial(fold_kernel, halving),
        out_shape=(shape,) * (2 if halving else 1),
        in_specs=[pl.BlockSpec(memory_space=pltpu.SMEM), vmem, vmem]
        + [pl.BlockSpec(memory_space=pl.ANY)] * len(ahead),
        out_specs=(vmem,) * (2 if halving else 1),
        compiler_params=pltpu.CompilerParams(vmem_limit_bytes=12 << 20),
        name="fold",
    )(scalar.reshape(1), kept, came, *ahead)
    return out if halving else (out[0], None)


def join_kernel(mine_ref, value_ref, came_ref, *refs):
    out_ref = refs[-1]
    rows = value_ref.shape[0]
    mine = mine_ref[0]
    out_ref[pl.ds(pl.multiple_of(mine * rows, rows), rows)] = value_ref[...]
    out_ref[pl.ds(pl.multiple_of((1 - mine) * rows, rows), rows)] = came_ref[...]


def join(value, came, mine, ahead):
    rows, width = value.shape
    if rows % 16:
        came = gate(came, *ahead) if ahead else came
        first = mine == 0
        return jnp.concatenate(
            [jnp.where(first, value, came), jnp.where(first, came, value)], axis=0
        )
    vmem = pl.BlockSpec(memory_space=pltpu.VMEM)
    return pl.pallas_call(
        join_kernel,
        out_shape=jax.ShapeDtypeStruct((2 * rows, width), BF16),
        in_specs=[pl.BlockSpec(memory_space=pltpu.SMEM), vmem, vmem]
        + [pl.BlockSpec(memory_space=pl.ANY)] * len(ahead),
        out_specs=vmem,
        compiler_params=pltpu.CompilerParams(vmem_limit_bytes=12 << 20),
        name="join",
    )(mine.reshape(1), value, came, *ahead)


class GroupSum:
    def __init__(self, kept, sent, steps, mines):
        self.steps, self.mines = steps, mines
        self.count, self.kept = 0, kept
        self.done = False
        self.came = swap(sent, *steps[0])

    def step(self, *ahead):
        levels = len(self.steps)
        self.count += 1
        if self.count <= levels:
            following = self.mines[self.count] if self.count < levels else None
            rows = self.kept.shape[0]
            if self.count < levels and rows % 32:
                came = gate(self.came, *ahead) if ahead else self.came
                halves = add_low(self.kept, came).reshape(2, rows // 2, -1)
                self.kept = lax.dynamic_index_in_dim(halves, following, 0, keepdims=False)
                sent = lax.dynamic_index_in_dim(halves, 1 - following, 0, keepdims=False)
            else:
                self.kept, sent = fold(self.kept, self.came, following, ahead)
            if self.count < levels:
                self.came = swap(sent, *self.steps[self.count])
        else:
            level = 2 * levels - self.count
            self.kept = join(self.kept, self.came, self.mines[level], ahead)
        if self.count == 2 * levels:
            self.done = True
        elif self.count >= levels:
            self.came = swap(self.kept, *self.steps[2 * levels - 1 - self.count])
        return self.kept


def grads_kernel(mine_ref, *refs):
    norms, d_qkv_ref, heads, d_rows = refs[:4], refs[4], refs[5:7], refs[7:11]
    kept_ref, sent_ref, held_ref = refs[-3:]
    width = d_qkv_ref.shape[2]
    strip = 256
    half = kept_ref.shape[0]
    for n in range(2):
        for first in range(0, half, strip):
            at = slice(n * half + first, n * half + first + strip)
            to = slice(first, first + strip)
            total = sum(mm(norms[k][:, at], d_qkv_ref[k], TN) for k in range(4))
            held_ref[to, :width] = total.astype(BF16)
            total = sum(mm(d_rows[k][:, at], heads[k // 2][k % 2], TN) for k in range(4))
            held_ref[to, width:] = total.astype(BF16)
        put_halves(mine_ref[0], held_ref[...], kept_ref, sent_ref, half=n)


def late_grads(mine, norms, d_qkv, heads_out, d_rows, ahead):
    depth = norms[0].shape[1]
    width = d_qkv.shape[2] + heads_out[0].shape[2]
    vmem = pl.BlockSpec(memory_space=pltpu.VMEM)
    shape = jax.ShapeDtypeStruct((depth // 2, width), BF16)
    return pl.pallas_call(
        grads_kernel,
        out_shape=(shape, shape),
        in_specs=[pl.BlockSpec(memory_space=pltpu.SMEM)]
        + [vmem] * 11
        + [pl.BlockSpec(memory_space=pl.ANY)] * len(ahead),
        out_specs=(vmem, vmem),
        scratch_shapes=[pltpu.VMEM((depth // 2, width), BF16)],
        compiler_params=pltpu.CompilerParams(vmem_limit_bytes=32 << 20),
        name="late_grads",
    )(mine.reshape(1), *norms, d_qkv, *heads_out, *d_rows, *ahead)


def row_stats(values):
    row_mean = jnp.mean(values, axis=-1, keepdims=True)
    centered = values - row_mean
    inv_std = lax.rsqrt(jnp.mean(centered * centered, axis=-1, keepdims=True) + EPSILON)
    return centered * inv_std, inv_std


def norm_kernel(base_ref, mine_ref, other_ref, gain_ref, shift_ref, *refs):
    value_ref, low_ref = refs[-2:]
    value = base_ref[...] + (mine_ref[...].astype(F32) + other_ref[...].astype(F32))
    value_ref[...] = value
    normed, _ = row_stats(value)
    low_ref[...] = (normed * gain_ref[...] + shift_ref[...]).astype(BF16)


def norm_rows(base, mine, other, gain, shift, ahead=(), tile=128):
    rows, width = mine.shape
    wide = pl.BlockSpec((tile, width), lambda i: (i, 0))
    one = pl.BlockSpec((1, width), lambda i: (0, 0))
    return pl.pallas_call(
        norm_kernel,
        grid=(rows // tile,),
        out_shape=(
            jax.ShapeDtypeStruct((rows, width), F32),
            jax.ShapeDtypeStruct((rows, width), BF16),
        ),
        in_specs=[wide if base.shape[0] == rows else one, wide, wide, one, one]
        + [pl.BlockSpec(memory_space=pl.ANY)] * len(ahead),
        out_specs=(wide, wide),
        compiler_params=pltpu.CompilerParams(vmem_limit_bytes=24 << 20),
        name="norm_rows",
    )(base, mine, other, gain[None], shift[None], *ahead)


def back_kernel(past_ref, value_ref, mine_ref, other_ref, gain_ref, sums_in, *refs):
    grad_ref, low_ref, sums_ref = refs[-3:]
    d_output = mine_ref[...].astype(F32) + other_ref[...].astype(F32)
    normed, inv_std = row_stats(value_ref[...])
    d_normed = d_output * gain_ref[...]
    grad = past_ref[...].astype(F32) + inv_std * (
        d_normed
        - jnp.mean(d_normed, axis=-1, keepdims=True)
        - normed * jnp.mean(d_normed * normed, axis=-1, keepdims=True)
    )
    grad_ref[...] = grad
    low_ref[...] = grad.astype(BF16)

    @pl.when(pl.program_id(0) == 0)
    def _():
        sums_ref[...] = sums_in[...]

    for n, terms in enumerate((d_output * normed, d_output, grad)):
        part = jnp.sum(terms.reshape(-1, 8, terms.shape[1]), axis=0)
        sums_ref[n] = sums_ref[n] + part


def norm_back_rows(past, value, mine, other, gain, sums, ahead=(), tile=128):
    rows, width = mine.shape
    wide = pl.BlockSpec((tile, width), lambda i: (i, 0))
    one = pl.BlockSpec((1, width), lambda i: (0, 0))
    kept = pl.BlockSpec((3, 8, width), lambda i: (0, 0, 0))
    return pl.pallas_call(
        back_kernel,
        grid=(rows // tile,),
        out_shape=(
            jax.ShapeDtypeStruct((rows, width), F32),
            jax.ShapeDtypeStruct((rows, width), BF16),
            jax.ShapeDtypeStruct((3, 8, width), F32),
        ),
        in_specs=[wide, wide, wide, wide, one, kept]
        + [pl.BlockSpec(memory_space=pl.ANY)] * len(ahead),
        out_specs=(wide, wide, kept),
        compiler_params=pltpu.CompilerParams(vmem_limit_bytes=24 << 20),
        name="norm_back",
    )(past, value, mine, other, gain[None], sums, *ahead)


def feed_kernel(chunk, core_ref, up_ref, bias_ref, down_ref, own_ref, sib_ref, cot_ref, *refs):
    act_ref, grads_ref, bias_out, dn_own, *dn_sib = refs[-8 - PARTS : -4]
    cot_v, d_pre_ref, bias_acc, sems = refs[-4:]
    rows = own_ref.shape[0] // 2
    core = core_ref[0]
    copies = []
    for i in range(4):
        side, y = i // 2, i % 2
        first = y * (4 * rows) + (core ^ side) * (2 * rows) + chunk * rows
        copy = pltpu.make_async_copy(
            cot_ref.at[pl.ds(pl.multiple_of(first, rows), rows)],
            cot_v.at[i * rows : (i + 1) * rows],
            sems.at[i],
        )
        copy.start()
        copies.append(copy)
    bias_acc[...] = refs[1][...] if chunk else jnp.zeros_like(bias_acc)
    for copy in copies:
        copy.wait()
    for side, n_ref in enumerate((own_ref, sib_ref)):
        for y in range(2):
            here = slice(y * rows, (y + 1) * rows)
            there = slice((side * 2 + y) * rows, (side * 2 + y + 1) * rows)
            pre = mm(n_ref[here], up_ref[...], NN) + bias_ref[...]
            d_act = mm(cot_v[there], down_ref[...], NT)
            cdf = 0.5 + 0.5 * lax.erf(pre * ROOT_HALF)
            act_ref[side, here] = (pre * cdf).astype(BF16)
            slope = cdf + pre * jnp.exp(-0.5 * pre * pre) * INV_ROOT_TAU
            d_pre = (d_act * slope).astype(BF16)
            d_pre_ref[there] = d_pre
            parts = d_pre.astype(F32).reshape(-1, 8, d_pre.shape[1])
            bias_acc[...] = bias_acc[...] + jnp.sum(parts, axis=0)
            d_norm = mm(d_pre, up_ref[...], NT).astype(BF16)
            if side == 0:
                dn_own[here] = d_norm
            else:
                strip = dn_sib[0].shape[0]
                for n in range(rows // strip):
                    dn_sib[y * rows // strip + n][...] = d_norm[n * strip : (n + 1) * strip]
    bias_out[...] = bias_acc[...]
    own_rows, sib_rows = slice(0, 2 * rows), slice(2 * rows, 4 * rows)
    units = act_ref.shape[2]
    strip = 256
    for first in range(0, units, strip):
        at = slice(first, first + strip)
        total = mm(act_ref[0, :, at], cot_v[own_rows], TN) + mm(
            act_ref[1, :, at], cot_v[sib_rows], TN
        )
        if chunk:
            total = total + refs[0][at]
        grads_ref[at] = total.astype(grads_ref.dtype)
    for first in range(0, own_ref.shape[1], strip):
        at, to = slice(first, first + strip), slice(units + first, units + first + strip)
        total = mm(own_ref[:, at], d_pre_ref[own_rows], TN) + mm(
            sib_ref[:, at], d_pre_ref[sib_rows], TN
        )
        if chunk:
            total = total + refs[0][to]
        grads_ref[to] = total.astype(grads_ref.dtype)


def feed(chunk, core, w_up, c_up, w_down, own, sib, cot, before=()):
    rows, width = own.shape
    units = w_up.shape[1]
    vmem = pl.BlockSpec(memory_space=pltpu.VMEM)
    return pl.pallas_call(
        functools.partial(feed_kernel, chunk),
        out_shape=(
            jax.ShapeDtypeStruct((2, rows, units), BF16),
            jax.ShapeDtypeStruct((units + width, width), BF16 if chunk else F32),
            jax.ShapeDtypeStruct((8, units), F32),
            jax.ShapeDtypeStruct((rows, width), BF16),
        )
        + (jax.ShapeDtypeStruct((rows // PARTS, width), BF16),) * PARTS,
        in_specs=[pl.BlockSpec(memory_space=pltpu.SMEM)]
        + [vmem] * 5
        + [pl.BlockSpec(memory_space=pl.ANY)]
        + [vmem] * len(before),
        out_specs=(vmem,) * (4 + PARTS),
        scratch_shapes=[
            pltpu.VMEM((2 * rows, width), BF16),
            pltpu.VMEM((2 * rows, units), BF16),
            pltpu.VMEM((8, units), F32),
            pltpu.SemaphoreType.DMA((4,)),
        ],
        compiler_params=pltpu.CompilerParams(vmem_limit_bytes=44 << 20),
        name="feed",
    )(core, w_up, c_up[None], w_down, own, sib, cot, *before)


def row_copies(core, chunk, rows, source, target, sems, reverse=False):
    copies = []
    for i in range(4):
        side, y = i // 2, i % 2
        first = y * (4 * rows) + (core ^ side) * (2 * rows) + chunk * rows
        whole = pl.ds(pl.multiple_of(first, rows), rows)
        here = slice(i * rows, (i + 1) * rows)
        if reverse:
            copy = pltpu.make_async_copy(source.at[here], target.at[whole], sems.at[i])
        else:
            copy = pltpu.make_async_copy(source.at[whole], target.at[here], sems.at[i])
        copy.start()
        copies.append(copy)
    return copies


def skip_grad_kernel(chunk, core_ref, own_ref, sib_ref, dec_ref, enc_ref, *refs):
    outs, (dec_v, enc_v, sems) = refs[2 * chunk : -3], refs[-3:]
    rows = own_ref.shape[0] // 2
    width, cols = dec_v.shape[1], own_ref.shape[1]
    copies = row_copies(core_ref[0], chunk, rows, dec_ref, dec_v, sems.at[0])
    for i in range(4):
        side, y = i // 2, i % 2
        first = (y * 2 + (core_ref[0] ^ side)) * rows
        copy = pltpu.make_async_copy(
            enc_ref.at[pl.ds(pl.multiple_of(first, rows), rows)],
            enc_v.at[i * rows : (i + 1) * rows],
            sems.at[1, i],
        )
        copy.start()
        copies.append(copy)
    for copy in copies:
        copy.wait()
    half = 2 * rows
    for n, part in enumerate((dec_v, enc_v)):
        at = slice(n * width, (n + 1) * width)
        total = mm(part[:half], own_ref[...], TN) + mm(part[half:], sib_ref[...], TN)
        if not chunk:
            outs[0][at] = total
            continue
        total = (total + refs[0][at]).astype(BF16)
        side = jnp.zeros((width, 128), BF16)
        if n == 0:
            small = refs[1]
            lines = [
                small[k : k + 1, j * 128 : (j + 1) * 128] for k in range(8) for j in range(cols // 128)
            ]
            spare = jnp.zeros((width - len(lines), 128), F32)
            side = jnp.concatenate(lines + [spare], axis=0).astype(BF16)
        put_halves(core_ref[1], jnp.concatenate([total, side], axis=1), *outs, half=n)


def skip_grad(chunk, core, own, sib, dec, enc, before=()):
    rows, cols = own.shape
    width = dec.shape[1]
    vmem = pl.BlockSpec(memory_space=pltpu.VMEM)
    hbm = pl.BlockSpec(memory_space=pl.ANY)
    half = jax.ShapeDtypeStruct((width, cols + 128), BF16)
    return pl.pallas_call(
        functools.partial(skip_grad_kernel, chunk),
        out_shape=(half, half) if chunk else (jax.ShapeDtypeStruct((2 * width, cols), F32),),
        in_specs=[pl.BlockSpec(memory_space=pltpu.SMEM), vmem, vmem, hbm, hbm]
        + [vmem] * len(before),
        out_specs=(vmem,) * (1 + chunk),
        scratch_shapes=[
            pltpu.VMEM((2 * rows, width), BF16),
            pltpu.VMEM((2 * rows, width), BF16),
            pltpu.SemaphoreType.DMA((2, 4)),
        ],
        compiler_params=pltpu.CompilerParams(vmem_limit_bytes=24 << 20),
        name="skip_grad",
    )(core, own, sib, dec, enc, *before)


def skip_back_kernel(chunk, core_ref, w_ref, own_ref, sib_ref, *refs):
    back_ref, whole_ref, held, sems = refs[-4:]
    rows = own_ref.shape[0] // 2
    for side, part in enumerate((own_ref, sib_ref)):
        at = slice(side * 2 * rows, (side + 1) * 2 * rows)
        back_ref[at] = mm(part[...], w_ref[1], NT).astype(BF16)
        held[at] = mm(part[...], w_ref[0], NT)
    for copy in row_copies(core_ref[0], chunk, rows, held, whole_ref, sems, reverse=True):
        copy.wait()


def skip_back(chunk, core, w_skip, own, sib, group_rows, before=(), ahead=()):
    rows = own.shape[0]
    width = w_skip.shape[1]
    vmem = pl.BlockSpec(memory_space=pltpu.VMEM)
    hbm = pl.BlockSpec(memory_space=pl.ANY)
    return pl.pallas_call(
        functools.partial(skip_back_kernel, chunk),
        out_shape=(
            jax.ShapeDtypeStruct((2 * rows, width), BF16),
            jax.ShapeDtypeStruct((group_rows, width), F32),
        ),
        in_specs=[pl.BlockSpec(memory_space=pltpu.SMEM), vmem, vmem, vmem]
        + [hbm] * (len(before) + len(ahead)),
        out_specs=(vmem, hbm),
        scratch_shapes=[pltpu.VMEM((2 * rows, width), F32), pltpu.SemaphoreType.DMA((4,))],
        input_output_aliases={4: 1} if before else {},
        compiler_params=pltpu.CompilerParams(vmem_limit_bytes=24 << 20),
        name="skip_back",
    )(core, w_skip, own, sib, *before, *ahead)


def restore_kernel(core_ref, *refs):
    out_ref = refs[-1]
    for chunk, part in enumerate(refs[:-1]):
        rows = part.shape[0] // 4
        for i in range(4):
            side, y = i // 2, i % 2
            first = y * (4 * rows) + (core_ref[0] ^ side) * (2 * rows) + chunk * rows
            out_ref[pl.ds(pl.multiple_of(first, rows), rows)] = part[i * rows : (i + 1) * rows]


def restore(core, parts):
    vmem = pl.BlockSpec(memory_space=pltpu.VMEM)
    rows, width = parts[0].shape
    return pl.pallas_call(
        restore_kernel,
        out_shape=jax.ShapeDtypeStruct((rows * len(parts), width), parts[0].dtype),
        in_specs=[pl.BlockSpec(memory_space=pltpu.SMEM)] + [vmem] * len(parts),
        out_specs=vmem,
        compiler_params=pltpu.CompilerParams(vmem_limit_bytes=12 << 20),
        name="restore",
    )(core, *parts)


def skip_kernel(chunk, core_ref, w_ref, dec_ref, enc_ref, own_ref, *refs):
    sib_refs, (dec_v, enc_v, sems) = refs[:PARTS], refs[PARTS:]
    rows = own_ref.shape[0] // 2
    copies = row_copies(core_ref[0], chunk, rows, dec_ref, dec_v, sems.at[0])
    for i in range(4):
        side, y = i // 2, i % 2
        first = (y * 2 + (core_ref[0] ^ side)) * rows
        copy = pltpu.make_async_copy(
            enc_ref.at[pl.ds(pl.multiple_of(first, rows), rows)],
            enc_v.at[i * rows : (i + 1) * rows],
            sems.at[1, i],
        )
        copy.start()
        copies.append(copy)
    for copy in copies:
        copy.wait()
    half = 2 * rows
    strip = half // PARTS
    for n, sib_ref in enumerate(sib_refs):
        at = slice(half + n * strip, half + (n + 1) * strip)
        sib_ref[...] = (mm(dec_v[at], w_ref[0], NN) + mm(enc_v[at], w_ref[1], NN)).astype(BF16)
    own_ref[...] = (mm(dec_v[:half], w_ref[0], NN) + mm(enc_v[:half], w_ref[1], NN)).astype(BF16)


def skip(chunk, core, w_skip, dec, enc):
    rows = enc.shape[0] // 2
    width, cols = w_skip.shape[1:]
    vmem = pl.BlockSpec(memory_space=pltpu.VMEM)
    hbm = pl.BlockSpec(memory_space=pl.ANY)
    return pl.pallas_call(
        functools.partial(skip_kernel, chunk),
        out_shape=(jax.ShapeDtypeStruct((rows, cols), BF16),)
        + (jax.ShapeDtypeStruct((rows // PARTS, cols), BF16),) * PARTS,
        in_specs=[pl.BlockSpec(memory_space=pltpu.SMEM), vmem, hbm, hbm],
        out_specs=(vmem,) * (1 + PARTS),
        scratch_shapes=[
            pltpu.VMEM((2 * rows, width), BF16),
            pltpu.VMEM((2 * rows, width), BF16),
            pltpu.SemaphoreType.DMA((2, 4)),
        ],
        compiler_params=pltpu.CompilerParams(vmem_limit_bytes=16 << 20),
        name="skip",
    )(core, w_skip, dec, enc)


def shards(
    decoder_in,
    encoder_out,
    segments,
    w_skip,
    b_skip,
    ln1_gain,
    ln1_bias,
    w_qkv,
    w_out,
    ln2_gain,
    ln2_bias,
    w_up,
    c_up,
    w_down,
    cotangent,
):
    group_rows = decoder_in.shape[0]
    tensor_rank = lax.axis_index("tensor")
    core = tensor_rank & 1
    chip = tensor_rank >> 1
    heads_here = HEADS // lax.axis_size("tensor")
    local_width = heads_here * HEAD_DIM
    block = group_rows // (4 * CHUNKS)
    qkv_matrix = w_qkv.reshape(D, 3 * local_width)
    steps = group_steps()
    mines = [((lax.axis_index(axis) >> bit) & 1).astype(jnp.int32) for axis, bit in steps]
    core_scalar = jnp.stack([core.astype(jnp.int32), mines[0]])
    slopes = jnp.exp2(
        -8.0
        * (tensor_rank * heads_here + jnp.arange(heads_here, dtype=jnp.int32) + 1).astype(F32)
        / HEADS
    )
    spots = [(chunk, side) for chunk in range(CHUNKS) for side in range(2)]

    def piece_of(array, chunk, side):
        width = array.shape[-1]
        parts = array.reshape(2, 2, CHUNKS, block, width)[:, :, chunk]
        return lax.dynamic_index_in_dim(parts, core ^ side, 1, keepdims=False).reshape(
            2 * block, width
        )

    cot = [piece_of(cotangent, chunk, 0) for chunk in range(CHUNKS)]
    encoder_parts = encoder_out.reshape(2, 2, CHUNKS, block, encoder_out.shape[1])
    partner = [
        partner_swap(encoder_parts[:, :, chunk].reshape(4 * block, -1)) for chunk in range(CHUNKS)
    ]

    def chip_total(half):
        sent = core_swap(half(1).astype(BF16))
        return (half(0) + sent.astype(F32)).astype(BF16)

    merged, norm_one, qkv = [], {}, {}
    sums = []
    for chunk in range(CHUNKS):
        own, *sib = skip(chunk, core_scalar, w_skip, decoder_in, partner[chunk])
        sums.append(add_low(own, jnp.concatenate([core_swap(part) for part in sib], axis=0)))
        if chunk + 1 < CHUNKS:
            partner[chunk + 1] = gate(partner[chunk + 1], sums[chunk])
    others = [chip_swap(part) for part in sums]
    ahead = (qkv_matrix, *sums)
    for chunk in range(CHUNKS):
        value, normal = norm_rows(
            b_skip[None], sums[chunk], others[chunk], ln1_gain, ln1_bias, ahead
        )
        merged.append(value)
        norm_one[chunk, 0] = normal
        norm_one[chunk, 1] = core_swap(normal)
        for side in range(2):
            qkv[chunk, side] = jnp.dot(
                norm_one[chunk, side], qkv_matrix, preferred_element_type=F32
            ).astype(BF16)
        ahead = (qkv[chunk, 0], qkv[chunk, 1], *cot)
    qkv_pieces = [qkv[spot].reshape(2, block, 3 * local_width) for spot in spots]

    heads_out, lse, sums = [], [], []
    for chunk in range(CHUNKS):
        mixed, log_total, own, *sib = attend(
            chunk, core_scalar, slopes, segments, w_out, qkv_pieces, sums
        )
        heads_out.append(mixed)
        lse.append(log_total)
        sums.append(add_low(own, jnp.concatenate([core_swap(part) for part in sib], axis=0)))
    others = [chip_swap(part) for part in sums]

    attended, activated, d_sums, d_others = [], [], [], []
    ahead = tuple(sums)
    grads = ()
    for chunk in range(CHUNKS):
        value, normal = norm_rows(
            merged[chunk], sums[chunk], others[chunk], ln2_gain, ln2_bias, ahead
        )
        attended.append(value)
        acts, weights_sum, bias_sum, own, *sib = feed(
            chunk, core_scalar, w_up, c_up, w_down, normal, core_swap(normal), cotangent, grads
        )
        grads = (weights_sum, bias_sum)
        activated.append(acts)
        sib = gate([core_swap(part) for part in sib], d_others[chunk - 1] if chunk else others[1])
        d_sums.append(add_low(own, jnp.concatenate(sib, axis=0)))
        d_others.append(chip_swap(d_sums[chunk]))
        ahead = (d_sums[chunk],)
    d_w_ff, c_up_sum = grads
    both = ("section", "dp")
    d_w_ff = lax.psum_scatter(
        gate(d_w_ff, d_sums[-1]), both, scatter_dimension=0, tiled=True
    )

    d_attended, d_attended_rows = [], {}
    sums_two = jnp.zeros((3, 8, D), F32)
    before = ()
    for chunk in range(CHUNKS):
        value, low, sums_two = norm_back_rows(
            cot[chunk], attended[chunk], d_sums[chunk], d_others[chunk], ln2_gain, sums_two,
            ahead,
        )
        d_attended.append(value)
        d_attended_rows[chunk, 0] = low
        d_attended_rows[chunk, 1] = core_swap(low)
        d_heads = [
            mm(d_attended_rows[chunk, side], w_out, NT).astype(BF16) for side in range(2)
        ]
        before = attend_back(
            chunk, core_scalar, slopes, segments, qkv_pieces, d_heads, heads_out[chunk],
            lse[chunk], before,
        )
        ahead = (before[0],)
    d_qkv = before

    sums = [
        chip_total(lambda side: mm(d_qkv[2 * chunk + side], qkv_matrix, NT))
        for chunk in range(CHUNKS)
    ]
    others = [chip_swap(part) for part in sums]
    kept, sent = late_grads(
        mines[0],
        [norm_one[spot] for spot in spots],
        d_qkv,
        heads_out,
        [d_attended_rows[spot] for spot in spots],
        sums,
    )
    late = GroupSum(kept, sent, steps, mines)
    activated = gate(activated, kept)
    down = [
        chip_total(
            lambda side: jnp.dot(activated[chunk][side], w_down, preferred_element_type=F32)
        )
        for chunk in range(CHUNKS)
    ]

    aways = [
        lax.dynamic_index_in_dim(part.reshape(2, block, D), 1 - chip, 0, keepdims=False)
        for part in down
    ]
    lows = []
    sums_one = jnp.zeros((3, 8, D), F32)
    ahead = (kept,)
    for chunk in range(CHUNKS):
        _, low, sums_one = norm_back_rows(
            d_attended[chunk], merged[chunk], sums[chunk], others[chunk], ln1_gain, sums_one, ahead
        )
        lows.append(low)
        if chunk == 0:
            ahead = (late.step(low, *aways),)
    d_w_ff = lax.all_gather(gate(d_w_ff, lows[0]), both, axis=0, tiled=True)
    sibs = [core_swap(low) for low in lows]
    small = jnp.sum(jnp.concatenate([sums_one, sums_two], axis=0), axis=1) * 0.5
    small = small + core_swap(small)
    small = small + chip_swap(small)
    small = jnp.concatenate([small, jnp.sum(c_up_sum, axis=0)[None]], axis=0)
    small = jnp.pad(small, ((0, 16 - small.shape[0]), (0, 0)))
    before = ()
    for chunk in range(CHUNKS):
        before = skip_grad(
            chunk, core_scalar, lows[chunk], sibs[chunk], decoder_in, partner[chunk],
            (*before, small) if chunk else (),
        )
    kept, sent = before
    last = GroupSum(kept, sent, steps, mines)
    d_encoder, before = [], ()
    for chunk in range(CHUNKS):
        returned, *before = skip_back(
            chunk, core_scalar, w_skip, lows[chunk], sibs[chunk], group_rows, before, (kept,)
        )
        d_encoder.append(returned)
    (d_decoder_in,) = before
    d_encoder_out = restore(core_scalar, [partner_swap(part) for part in d_encoder])
    last.step(*d_encoder)

    moved = [chip_swap(part) for part in gate(aways, lows[-1])]
    d_w_down, d_w_up = d_w_ff[: w_down.shape[0]].astype(F32), d_w_ff[w_down.shape[0] :].astype(F32)
    total = 2 * len(steps)
    while last.count < total - 1:
        if late.count < total - 1:
            late.step(last.kept)
        last.step()
    moved = gate(moved, last.kept)
    layer_out = []
    for chunk in range(CHUNKS):
        home, base = (
            lax.dynamic_index_in_dim(part.reshape(2, block, D), chip, 0, keepdims=False)
            for part in (down[chunk], attended[chunk])
        )
        layer_out.append(base + (home.astype(F32) + moved[chunk].astype(F32)))
    layer_out = jnp.concatenate(layer_out, axis=0)
    while not late.done:
        late.step(last.kept, d_w_down, d_w_up, layer_out)
    last.step(d_encoder_out)
    d_w_qkv = jnp.stack(
        [late.kept[:, n * local_width : (n + 1) * local_width] for n in range(3)], axis=0
    )
    d_w_qkv = jnp.transpose(d_w_qkv.astype(F32), (1, 0, 2))
    d_w_out = late.kept[:, 3 * local_width :].T
    d_w_skip = last.kept[:, :D].reshape(w_skip.shape)
    small = last.kept[: 8 * D // 128, D:].astype(F32).reshape(8, D)
    return (
        layer_out,
        d_decoder_in,
        d_encoder_out,
        d_w_skip.astype(F32),
        small[2],
        small[0],
        small[1],
        d_w_qkv.astype(F32),
        d_w_out.astype(F32),
        small[3],
        small[4],
        d_w_up,
        small[6],
        d_w_down,
    )


def solution(mesh):
    return jax.shard_map(
        shards,
        mesh=mesh,
        in_specs=(
            P(("section", "dp"), "tensor"),
            P(("section", "dp"), "tensor"),
            P(("section", "dp"), None),
            P(None, "tensor", None),
            P(),
            P(),
            P(),
            P(None, None, "tensor"),
            P("tensor", None),
            P(),
            P(),
            P(None, "tensor"),
            P("tensor"),
            P("tensor", None),
            P(("section", "dp"), None),
        ),
        out_specs=(
            P(("section", "dp", "tensor"), None),
            P(("section", "dp"), "tensor"),
            P(("section", "dp"), "tensor"),
            P(None, "tensor", None),
            P(),
            P(),
            P(),
            P(None, None, "tensor"),
            P("tensor", None),
            P(),
            P(),
            P(None, "tensor"),
            P("tensor"),
            P("tensor", None),
        ),
        check_vma=False,
    )
```

```python
import functools
import jax
import jax.numpy as jnp
from jax import lax
from jax.experimental import pallas as pl
from jax.experimental.pallas import tpu as pltpu
from jax.sharding import PartitionSpec as P

D = 1024
HEADS = 16
UTTS = 6
HEAD_DIM = D // HEADS
SCALE = HEAD_DIM**-0.5

EPSILON = 1e-05
FAR = 1e30
ROOT_HALF = 0.7071067811865476
INV_ROOT_TAU = 0.3989422804014327
BF16 = jnp.bfloat16
F32 = jnp.float32
NT = (((1,), (1,)), ((), ()))
NN = (((1,), (0,)), ((), ()))
TN = (((0,), (0,)), ((), ()))
CHUNKS = 2
PARTS = 4


def mm(left, right, dims):
    return lax.dot_general(left, right, dims, preferred_element_type=F32)


def starts_of(seg):
    return [jnp.sum((seg < u).astype(jnp.int32)) for u in range(1, UTTS)]


def tile_range(starts, first, count, tile, total):
    low = jnp.int32(0)
    high = jnp.int32(total)
    for s in starts:
        low = jnp.maximum(low, jnp.where(s <= first, s, 0))
        high = jnp.minimum(high, jnp.where(s >= first + count, s, total))
    return low // tile, (high + tile - 1) // tile


def eye(n):
    r = lax.broadcasted_iota(jnp.int32, (n, n), 0)
    c = lax.broadcasted_iota(jnp.int32, (n, n), 1)
    return jnp.where(r == c, 1.0, 0.0).astype(BF16)


def far_tile(starts, seg_row, q_first, k_first, bk, bq):
    kpos = k_first + lax.broadcasted_iota(jnp.int32, (bk, bq), 0)
    qpos = q_first + lax.broadcasted_iota(jnp.int32, (bk, bq), 1)
    lo = jnp.zeros_like(seg_row)
    hi = jnp.full_like(seg_row, starts[0])
    for u in range(1, UTTS):
        lo = jnp.where(seg_row == u, starts[u - 1], lo)
        hi = jnp.where(seg_row == u, starts[u] if u < UTTS - 1 else 1 << 30, hi)
    ok = (kpos >= lo) & (kpos < hi)
    return jnp.where(ok, jnp.abs(kpos - qpos).astype(F32), FAR)


def head_masked(pair, which):
    lane = lax.broadcasted_iota(jnp.int32, pair.shape, 1)
    keep = (lane < HEAD_DIM) if which == 0 else (lane >= HEAD_DIM)
    return jnp.where(keep, pair, 0.0).astype(BF16)


def load_pieces(core, pieces, whole_ref):
    rows = pieces[0].shape[1]
    for n, piece in enumerate(pieces):
        chunk, side = n // 2, n % 2
        for y in range(2):
            first = y * (4 * rows) + (core ^ side) * (2 * rows) + chunk * rows
            whole_ref[pl.ds(pl.multiple_of(first, rows), rows)] = piece[y]


def fwd_kernel(
    heads, bk, chunk, core_ref, slope_ref, seg_ref, w_ref, q00, q01, q10, q11, *refs
):
    out_ref, lse_ref, own_ref, *sib_refs = refs[-8 - PARTS : -5]
    qkv_ref, vt_ref, acc_ref, s_ref, top_ref = refs[-5:]
    strip = sib_refs[0].shape[0]
    total = seg_ref.shape[1]
    width = heads * HEAD_DIM
    bq = out_ref.shape[1] // 2
    core = core_ref[0]
    load_pieces(core, (q00, q01, q10, q11), qkv_ref)
    starts = starts_of(seg_ref[...])
    ident = eye(width)

    def prep(j, c):
        at = pl.ds(pl.multiple_of(j * bk, bk), bk)
        vt = mm(ident, qkv_ref[at, 2 * width : 3 * width], NT).astype(BF16)
        for h in range(heads):
            vt_ref[h * 80 : h * 80 + 64, at] = vt[h * 64 : (h + 1) * 64]
            vt_ref[h * 80 + 64 : (h + 1) * 80, at] = jnp.ones((16, bk), BF16)
        return c

    lax.fori_loop(0, total // bk, prep, 0)

    def q_step(i, c):
        side, y = i // 2, i % 2
        qi = pl.multiple_of(y * (4 * bq) + (core ^ side) * (2 * bq) + chunk * bq, bq)
        lo, hi = tile_range(starts, qi, bq, bk, total)
        seg_row = seg_ref[:, pl.ds(qi, bq)]
        acc_ref[...] = jnp.zeros_like(acc_ref)
        top_ref[...] = jnp.full_like(top_ref, -3e38)
        qs = []
        for h in range(heads):
            p = h // 2
            qp = qkv_ref[pl.ds(qi, bq), p * 128 : (p + 1) * 128].astype(F32) * SCALE
            qs.append(head_masked(qp, h % 2))

        def score_step(j, c):
            kj = pl.multiple_of(j * bk, bk)
            far = far_tile(starts, seg_row, qi, kj, bk, bq)
            for h in range(heads):
                p = h // 2
                kp = qkv_ref[pl.ds(kj, bk), width + p * 128 : width + (p + 1) * 128]
                s = mm(kp, qs[h], NT) - far * slope_ref[h]
                s_ref[h, pl.ds(kj, bk)] = s
                top_ref[h] = jnp.maximum(top_ref[h], jnp.max(s.reshape(bk // 8, 8, bq), axis=0))
            return c

        lax.fori_loop(lo, hi, score_step, 0)
        tops = [jnp.max(top_ref[h], axis=0, keepdims=True) for h in range(heads)]

        def mix_step(j, c):
            kj = pl.multiple_of(j * bk, bk)
            for h in range(heads):
                e = jnp.exp(s_ref[h, pl.ds(kj, bk)] - tops[h]).astype(BF16)
                hs = slice(h * 80, (h + 1) * 80)
                acc_ref[hs] = acc_ref[hs] + mm(vt_ref[hs, pl.ds(kj, bk)], e, NN)
            return c

        lax.fori_loop(lo, hi, mix_step, 0)
        outs = []
        for h in range(heads):
            whole = acc_ref[h * 80 + 64 : h * 80 + 65]
            outs.append((acc_ref[h * 80 : h * 80 + 64] * (1.0 / whole)).astype(BF16))
            lse_ref[i, h : h + 1] = tops[h] + jnp.log(whole)
        ot = jnp.concatenate(outs, axis=0)
        here = pl.ds(pl.multiple_of(y * bq, bq), bq)
        mixed = mm(eye(bq), ot, NT).astype(BF16)
        out_ref[side, here] = mixed
        part = mm(mixed, w_ref[...], NN).astype(BF16)

        @pl.when(side == 0)
        def _():
            own_ref[here] = part

        for n, sib_ref in enumerate(sib_refs):
            first = n * strip % bq

            @pl.when((side == 1) & (y == n * strip // bq))
            def _(sib_ref=sib_ref, first=first):
                sib_ref[...] = part[first : first + strip]

        return c

    lax.fori_loop(0, 4, q_step, 0)


def attend(chunk, core, slopes, seg, w_out, pieces, ahead=()):
    total = seg.shape[1]
    rows = pieces[0].shape[1]
    heads = pieces[0].shape[2] // (3 * HEAD_DIM)
    width = heads * HEAD_DIM
    bk = 512
    smem = pl.BlockSpec(memory_space=pltpu.SMEM)
    vmem = pl.BlockSpec(memory_space=pltpu.VMEM)
    hbm = pl.BlockSpec(memory_space=pl.ANY)
    return pl.pallas_call(
        functools.partial(fwd_kernel, heads, bk, chunk),
        out_shape=(
            jax.ShapeDtypeStruct((2, 2 * rows, width), BF16),
            jax.ShapeDtypeStruct((4, heads, rows), F32),
            jax.ShapeDtypeStruct((2 * rows, w_out.shape[1]), BF16),
        )
        + (jax.ShapeDtypeStruct((2 * rows // PARTS, w_out.shape[1]), BF16),) * PARTS,
        in_specs=[smem, smem] + [vmem] * 6 + [hbm] * len(ahead),
        out_specs=(vmem,) * (3 + PARTS),
        scratch_shapes=[
            pltpu.VMEM((total, 3 * width), BF16),
            pltpu.VMEM((heads * 80, total), BF16),
            pltpu.VMEM((heads * 80, rows), F32),
            pltpu.VMEM((heads, total, rows), F32),
            pltpu.VMEM((heads, 8, rows), F32),
        ],
        compiler_params=pltpu.CompilerParams(vmem_limit_bytes=28 << 20),
        name="attend",
    )(core, slopes, seg, w_out, *pieces, *ahead)


def bwd_kernel(heads, bk, chunk, *refs):
    core_ref, slope_ref, seg_ref, q00, q01, q10, q11, do0, do1, o_ref, lse_ref = refs[:11]
    if chunk == 0:
        dq_ref, dkv_ref = refs[-8:-6]
    else:
        dq_in, dkv_in = refs[11:13]
        dqkv_ref = refs[-7]
    qkv_ref, kt_ref, dqt_ref, dk_ref, dv_ref, delta_ref = refs[-6:]
    total = seg_ref.shape[1]
    width = heads * HEAD_DIM
    bq = o_ref.shape[1] // 2
    core = core_ref[0]
    load_pieces(core, (q00, q01, q10, q11), qkv_ref)
    starts = starts_of(seg_ref[...])
    ident = eye(width)
    hr = lax.broadcasted_iota(jnp.int32, (8, width), 0)
    hc = lax.broadcasted_iota(jnp.int32, (8, width), 1)
    pick = jnp.where(hr == hc // HEAD_DIM, 1.0, 0.0)

    def prep(j, c):
        at = pl.ds(pl.multiple_of(j * bk, bk), bk)
        kj = qkv_ref[at, width : 2 * width]
        kt_ref[:, at] = (mm(ident, kj, NT) * SCALE).astype(BF16)
        if chunk == 0:
            dk_ref[at] = jnp.zeros((bk, width), F32)
            dv_ref[at] = jnp.zeros((bk, width), F32)
        else:
            dk_ref[at] = dkv_in[at, :width]
            dv_ref[at] = dkv_in[at, width:]
        return c

    lax.fori_loop(0, total // bk, prep, 0)
    for side, do_ref in enumerate((do0, do1)):
        for y in range(2):
            at = slice(y * bq, (y + 1) * bq)
            prod = do_ref[at].astype(F32) * o_ref[side, at].astype(F32)
            delta_ref[side * 2 + y] = lax.dot_general(
                pick, prod, NT, precision=lax.Precision.HIGHEST, preferred_element_type=F32
            )

    for side, do_ref in enumerate((do0, do1)):

        def q_step(y, c, side=side, do_ref=do_ref):
            i = side * 2 + y
            qi = pl.multiple_of(y * (4 * bq) + (core ^ side) * (2 * bq) + chunk * bq, bq)
            here = pl.ds(pl.multiple_of(y * bq, bq), bq)
            lo, hi = tile_range(starts, qi, bq, bk, total)
            seg_row = seg_ref[:, pl.ds(qi, bq)]
            dqt_ref[...] = jnp.zeros_like(dqt_ref)
            qs, dos = [], []
            for h in range(heads):
                p = h // 2
                qp = qkv_ref[pl.ds(qi, bq), p * 128 : (p + 1) * 128].astype(F32) * SCALE
                qs.append(head_masked(qp, h % 2))
                dp = do_ref[here, p * 128 : (p + 1) * 128].astype(F32)
                dos.append(head_masked(dp, h % 2))
            lses = [lse_ref[i, h : h + 1] for h in range(heads)]
            deltas = [delta_ref[i, h : h + 1] for h in range(heads)]

            def k_step(j, c):
                kj = pl.multiple_of(j * bk, bk)
                at = pl.ds(kj, bk)
                far = far_tile(starts, seg_row, qi, kj, bk, bq)
                for p in range(heads // 2):
                    cols = slice(p * 128, (p + 1) * 128)
                    kp = qkv_ref[at, width + p * 128 : width + (p + 1) * 128]
                    vp = qkv_ref[at, 2 * width + p * 128 : 2 * width + (p + 1) * 128]
                    dv = dv_ref[at, cols]
                    dk = dk_ref[at, cols]
                    for h in (2 * p, 2 * p + 1):
                        s = mm(kp, qs[h], NT) - far * slope_ref[h]
                        w = jnp.exp(s - lses[h])
                        dw = mm(vp, dos[h], NT)
                        ds = (w * (dw - deltas[h])).astype(BF16)
                        dv = dv + mm(w.astype(BF16), dos[h], NN)
                        dk = dk + mm(ds, qs[h], NN)
                        hs = slice(h * HEAD_DIM, (h + 1) * HEAD_DIM)
                        dqt_ref[hs] = dqt_ref[hs] + mm(kt_ref[hs, at], ds, NN)
                    dv_ref[at, cols] = dv
                    dk_ref[at, cols] = dk
                return c

            lax.fori_loop(lo, hi, k_step, 0)
            dq = mm(eye(bq), dqt_ref[...].astype(BF16), NT).astype(BF16)
            if chunk == 0:
                dq_ref[side, here] = dq
            else:
                dqkv_ref[2 + side, here, :width] = dq
            return c

        lax.fori_loop(0, 2, q_step, 0)

    if chunk == 0:

        def finish(j, c):
            at = pl.ds(pl.multiple_of(j * bk, bk), bk)
            dkv_ref[at, :width] = dk_ref[at]
            dkv_ref[at, width:] = dv_ref[at]
            return c

        lax.fori_loop(0, total // bk, finish, 0)
    else:
        for side in range(2):
            dqkv_ref[side, :, :width] = dq_in[side]
        for n in range(4):
            part, side = n // 2, n % 2
            for y in range(2):
                first = y * (4 * bq) + (core ^ side) * (2 * bq) + part * bq
                at = pl.ds(pl.multiple_of(first, bq), bq)
                here = slice(y * bq, (y + 1) * bq)
                dqkv_ref[n, here, width : 2 * width] = dk_ref[at].astype(BF16)
                dqkv_ref[n, here, 2 * width :] = dv_ref[at].astype(BF16)


def attend_back(chunk, core, slopes, seg, pieces, d_heads, heads_out, lse, before=(), ahead=()):
    total = seg.shape[1]
    rows = pieces[0].shape[1]
    heads = pieces[0].shape[2] // (3 * HEAD_DIM)
    width = heads * HEAD_DIM
    bk = 512
    smem = pl.BlockSpec(memory_space=pltpu.SMEM)
    vmem = pl.BlockSpec(memory_space=pltpu.VMEM)
    hbm = pl.BlockSpec(memory_space=pl.ANY)
    if chunk == 0:
        out_shape = (
            jax.ShapeDtypeStruct((2, 2 * rows, width), BF16),
            jax.ShapeDtypeStruct((total, 2 * width), F32),
        )
        out_specs = (vmem, vmem)
    else:
        out_shape = jax.ShapeDtypeStruct((4, 2 * rows, 3 * width), BF16)
        out_specs = vmem
    return pl.pallas_call(
        functools.partial(bwd_kernel, heads, bk, chunk),
        out_shape=out_shape,
        in_specs=[smem, smem] + [vmem] * (9 + len(before)) + [hbm] * len(ahead),
        out_specs=out_specs,
        scratch_shapes=[
            pltpu.VMEM((total, 3 * width), BF16),
            pltpu.VMEM((width, total), BF16),
            pltpu.VMEM((width, rows), F32),
            pltpu.VMEM((total, width), F32),
            pltpu.VMEM((total, width), F32),
            pltpu.VMEM((4, 8, rows), F32),
        ],
        compiler_params=pltpu.CompilerParams(vmem_limit_bytes=34 << 20),
        name="attend_back",
    )(core, slopes, seg, *pieces, *d_heads, heads_out, lse, *before, *ahead)


def swap(value, axis, bit):
    pairs = [(source, source ^ (1 << bit)) for source in range(lax.axis_size(axis))]
    return lax.ppermute(value, axis, pairs)


core_swap = functools.partial(swap, axis="tensor", bit=0)
chip_swap = functools.partial(swap, axis="tensor", bit=1)
partner_swap = functools.partial(swap, axis="section", bit=0)


def add_low(*terms):
    return sum(term.astype(F32) for term in terms).astype(BF16)


def group_steps():
    steps = [("section", 0)]
    for bit in range((lax.axis_size("dp") - 1).bit_length()):
        steps.append(("dp", bit))
    return steps


def gate(values, *ahead):
    hbm = pl.BlockSpec(memory_space=pl.ANY)
    many = isinstance(values, (list, tuple))
    values = tuple(values) if many else (values,)
    out = pl.pallas_call(
        lambda *refs: None,
        out_shape=tuple(jax.ShapeDtypeStruct(value.shape, value.dtype) for value in values),
        in_specs=[hbm] * (len(values) + len(ahead)),
        out_specs=(hbm,) * len(values),
        input_output_aliases={n: n for n in range(len(values))},
        name="gate",
    )(*values, *ahead)
    return out if many else out[0]


def fold_kernel(halving, mine_ref, kept_ref, came_ref, *refs):
    total = (kept_ref[...].astype(F32) + came_ref[...].astype(F32)).astype(BF16)
    if halving:
        put_halves(mine_ref[0], total, *refs[-2:])
    else:
        refs[-1][...] = total


def put_halves(mine, total, kept_ref, sent_ref, half=None):
    rows = kept_ref.shape[0]
    for n in range(2) if half is None else (half,):
        part = total[n * rows : (n + 1) * rows] if half is None else total

        @pl.when(mine == n)
        def _(part=part):
            kept_ref[...] = part

        @pl.when(mine != n)
        def _(part=part):
            sent_ref[...] = part


def fold(kept, came, mine, ahead):
    rows, width = kept.shape
    vmem = pl.BlockSpec(memory_space=pltpu.VMEM)
    halving = mine is not None
    shape = jax.ShapeDtypeStruct((rows // 2 if halving else rows, width), BF16)
    scalar = mine if halving else jnp.int32(0)
    out = pl.pallas_call(
        functools.partial(fold_kernel, halving),
        out_shape=(shape,) * (2 if halving else 1),
        in_specs=[pl.BlockSpec(memory_space=pltpu.SMEM), vmem, vmem]
        + [pl.BlockSpec(memory_space=pl.ANY)] * len(ahead),
        out_specs=(vmem,) * (2 if halving else 1),
        compiler_params=pltpu.CompilerParams(vmem_limit_bytes=12 << 20),
        name="fold",
    )(scalar.reshape(1), kept, came, *ahead)
    return out if halving else (out[0], None)


def join_kernel(mine_ref, value_ref, came_ref, *refs):
    out_ref = refs[-1]
    rows = value_ref.shape[0]
    mine = mine_ref[0]
    out_ref[pl.ds(pl.multiple_of(mine * rows, rows), rows)] = value_ref[...]
    out_ref[pl.ds(pl.multiple_of((1 - mine) * rows, rows), rows)] = came_ref[...]


def join(value, came, mine, ahead):
    rows, width = value.shape
    if rows % 16:
        came = gate(came, *ahead) if ahead else came
        first = mine == 0
        return jnp.concatenate(
            [jnp.where(first, value, came), jnp.where(first, came, value)], axis=0
        )
    vmem = pl.BlockSpec(memory_space=pltpu.VMEM)
    return pl.pallas_call(
        join_kernel,
        out_shape=jax.ShapeDtypeStruct((2 * rows, width), BF16),
        in_specs=[pl.BlockSpec(memory_space=pltpu.SMEM), vmem, vmem]
        + [pl.BlockSpec(memory_space=pl.ANY)] * len(ahead),
        out_specs=vmem,
        compiler_params=pltpu.CompilerParams(vmem_limit_bytes=12 << 20),
        name="join",
    )(mine.reshape(1), value, came, *ahead)


class GroupSum:
    def __init__(self, kept, sent, steps, mines):
        self.steps, self.mines = steps, mines
        self.count, self.kept = 0, kept
        self.done = False
        self.came = swap(sent, *steps[0])

    def step(self, *ahead):
        levels = len(self.steps)
        self.count += 1
        if self.count <= levels:
            following = self.mines[self.count] if self.count < levels else None
            rows = self.kept.shape[0]
            if self.count < levels and rows % 32:
                came = gate(self.came, *ahead) if ahead else self.came
                halves = add_low(self.kept, came).reshape(2, rows // 2, -1)
                self.kept = lax.dynamic_index_in_dim(halves, following, 0, keepdims=False)
                sent = lax.dynamic_index_in_dim(halves, 1 - following, 0, keepdims=False)
            else:
                self.kept, sent = fold(self.kept, self.came, following, ahead)
            if self.count < levels:
                self.came = swap(sent, *self.steps[self.count])
        else:
            level = 2 * levels - self.count
            self.kept = join(self.kept, self.came, self.mines[level], ahead)
        if self.count == 2 * levels:
            self.done = True
        elif self.count >= levels:
            self.came = swap(self.kept, *self.steps[2 * levels - 1 - self.count])
        return self.kept


def grads_kernel(mine_ref, *refs):
    norms, d_qkv_ref, heads, d_rows = refs[:4], refs[4], refs[5:7], refs[7:11]
    kept_ref, sent_ref, held_ref = refs[-3:]
    width = d_qkv_ref.shape[2]
    strip = 256
    half = kept_ref.shape[0]
    for n in range(2):
        for first in range(0, half, strip):
            at = slice(n * half + first, n * half + first + strip)
            to = slice(first, first + strip)
            total = sum(mm(norms[k][:, at], d_qkv_ref[k], TN) for k in range(4))
            held_ref[to, :width] = total.astype(BF16)
            total = sum(mm(d_rows[k][:, at], heads[k // 2][k % 2], TN) for k in range(4))
            held_ref[to, width:] = total.astype(BF16)
        put_halves(mine_ref[0], held_ref[...], kept_ref, sent_ref, half=n)


def late_grads(mine, norms, d_qkv, heads_out, d_rows, ahead):
    depth = norms[0].shape[1]
    width = d_qkv.shape[2] + heads_out[0].shape[2]
    vmem = pl.BlockSpec(memory_space=pltpu.VMEM)
    shape = jax.ShapeDtypeStruct((depth // 2, width), BF16)
    return pl.pallas_call(
        grads_kernel,
        out_shape=(shape, shape),
        in_specs=[pl.BlockSpec(memory_space=pltpu.SMEM)]
        + [vmem] * 11
        + [pl.BlockSpec(memory_space=pl.ANY)] * len(ahead),
        out_specs=(vmem, vmem),
        scratch_shapes=[pltpu.VMEM((depth // 2, width), BF16)],
        compiler_params=pltpu.CompilerParams(vmem_limit_bytes=32 << 20),
        name="late_grads",
    )(mine.reshape(1), *norms, d_qkv, *heads_out, *d_rows, *ahead)


def row_stats(values):
    row_mean = jnp.mean(values, axis=-1, keepdims=True)
    centered = values - row_mean
    inv_std = lax.rsqrt(jnp.mean(centered * centered, axis=-1, keepdims=True) + EPSILON)
    return centered * inv_std, inv_std


def norm_kernel(base_ref, mine_ref, other_ref, gain_ref, shift_ref, *refs):
    value_ref, low_ref = refs[-2:]
    value = base_ref[...] + (mine_ref[...].astype(F32) + other_ref[...].astype(F32))
    value_ref[...] = value
    normed, _ = row_stats(value)
    low_ref[...] = (normed * gain_ref[...] + shift_ref[...]).astype(BF16)


def norm_rows(base, mine, other, gain, shift, ahead=(), tile=128):
    rows, width = mine.shape
    wide = pl.BlockSpec((tile, width), lambda i: (i, 0))
    one = pl.BlockSpec((1, width), lambda i: (0, 0))
    return pl.pallas_call(
        norm_kernel,
        grid=(rows // tile,),
        out_shape=(
            jax.ShapeDtypeStruct((rows, width), F32),
            jax.ShapeDtypeStruct((rows, width), BF16),
        ),
        in_specs=[wide if base.shape[0] == rows else one, wide, wide, one, one]
        + [pl.BlockSpec(memory_space=pl.ANY)] * len(ahead),
        out_specs=(wide, wide),
        compiler_params=pltpu.CompilerParams(vmem_limit_bytes=24 << 20),
        name="norm_rows",
    )(base, mine, other, gain[None], shift[None], *ahead)


def back_kernel(past_ref, value_ref, mine_ref, other_ref, gain_ref, sums_in, *refs):
    grad_ref, low_ref, sums_ref = refs[-3:]
    d_output = mine_ref[...].astype(F32) + other_ref[...].astype(F32)
    normed, inv_std = row_stats(value_ref[...])
    d_normed = d_output * gain_ref[...]
    grad = past_ref[...].astype(F32) + inv_std * (
        d_normed
        - jnp.mean(d_normed, axis=-1, keepdims=True)
        - normed * jnp.mean(d_normed * normed, axis=-1, keepdims=True)
    )
    grad_ref[...] = grad
    low_ref[...] = grad.astype(BF16)

    @pl.when(pl.program_id(0) == 0)
    def _():
        sums_ref[...] = sums_in[...]

    for n, terms in enumerate((d_output * normed, d_output, grad)):
        part = jnp.sum(terms.reshape(-1, 8, terms.shape[1]), axis=0)
        sums_ref[n] = sums_ref[n] + part


def norm_back_rows(past, value, mine, other, gain, sums, ahead=(), tile=128):
    rows, width = mine.shape
    wide = pl.BlockSpec((tile, width), lambda i: (i, 0))
    one = pl.BlockSpec((1, width), lambda i: (0, 0))
    kept = pl.BlockSpec((3, 8, width), lambda i: (0, 0, 0))
    return pl.pallas_call(
        back_kernel,
        grid=(rows // tile,),
        out_shape=(
            jax.ShapeDtypeStruct((rows, width), F32),
            jax.ShapeDtypeStruct((rows, width), BF16),
            jax.ShapeDtypeStruct((3, 8, width), F32),
        ),
        in_specs=[wide, wide, wide, wide, one, kept]
        + [pl.BlockSpec(memory_space=pl.ANY)] * len(ahead),
        out_specs=(wide, wide, kept),
        compiler_params=pltpu.CompilerParams(vmem_limit_bytes=24 << 20),
        name="norm_back",
    )(past, value, mine, other, gain[None], sums, *ahead)


def feed_kernel(chunk, core_ref, up_ref, bias_ref, down_ref, own_ref, sib_ref, cot_ref, *refs):
    act_ref, grads_ref, bias_out, dn_own, *dn_sib = refs[-8 - PARTS : -4]
    cot_v, d_pre_ref, bias_acc, sems = refs[-4:]
    rows = own_ref.shape[0] // 2
    core = core_ref[0]
    copies = []
    for i in range(4):
        side, y = i // 2, i % 2
        first = y * (4 * rows) + (core ^ side) * (2 * rows) + chunk * rows
        copy = pltpu.make_async_copy(
            cot_ref.at[pl.ds(pl.multiple_of(first, rows), rows)],
            cot_v.at[i * rows : (i + 1) * rows],
            sems.at[i],
        )
        copy.start()
        copies.append(copy)
    bias_acc[...] = refs[1][...] if chunk else jnp.zeros_like(bias_acc)
    for copy in copies:
        copy.wait()
    for side, n_ref in enumerate((own_ref, sib_ref)):
        for y in range(2):
            here = slice(y * rows, (y + 1) * rows)
            there = slice((side * 2 + y) * rows, (side * 2 + y + 1) * rows)
            pre = mm(n_ref[here], up_ref[...], NN) + bias_ref[...]
            d_act = mm(cot_v[there], down_ref[...], NT)
            cdf = 0.5 + 0.5 * lax.erf(pre * ROOT_HALF)
            act_ref[side, here] = (pre * cdf).astype(BF16)
            slope = cdf + pre * jnp.exp(-0.5 * pre * pre) * INV_ROOT_TAU
            d_pre = (d_act * slope).astype(BF16)
            d_pre_ref[there] = d_pre
            parts = d_pre.astype(F32).reshape(-1, 8, d_pre.shape[1])
            bias_acc[...] = bias_acc[...] + jnp.sum(parts, axis=0)
            d_norm = mm(d_pre, up_ref[...], NT).astype(BF16)
            if side == 0:
                dn_own[here] = d_norm
            else:
                strip = dn_sib[0].shape[0]
                for n in range(rows // strip):
                    dn_sib[y * rows // strip + n][...] = d_norm[n * strip : (n + 1) * strip]
    bias_out[...] = bias_acc[...]
    own_rows, sib_rows = slice(0, 2 * rows), slice(2 * rows, 4 * rows)
    units = act_ref.shape[2]
    strip = 256
    for first in range(0, units, strip):
        at = slice(first, first + strip)
        total = mm(act_ref[0, :, at], cot_v[own_rows], TN) + mm(
            act_ref[1, :, at], cot_v[sib_rows], TN
        )
        if chunk:
            total = total + refs[0][at]
        grads_ref[at] = total.astype(grads_ref.dtype)
    for first in range(0, own_ref.shape[1], strip):
        at, to = slice(first, first + strip), slice(units + first, units + first + strip)
        total = mm(own_ref[:, at], d_pre_ref[own_rows], TN) + mm(
            sib_ref[:, at], d_pre_ref[sib_rows], TN
        )
        if chunk:
            total = total + refs[0][to]
        grads_ref[to] = total.astype(grads_ref.dtype)


def feed(chunk, core, w_up, c_up, w_down, own, sib, cot, before=()):
    rows, width = own.shape
    units = w_up.shape[1]
    vmem = pl.BlockSpec(memory_space=pltpu.VMEM)
    return pl.pallas_call(
        functools.partial(feed_kernel, chunk),
        out_shape=(
            jax.ShapeDtypeStruct((2, rows, units), BF16),
            jax.ShapeDtypeStruct((units + width, width), BF16 if chunk else F32),
            jax.ShapeDtypeStruct((8, units), F32),
            jax.ShapeDtypeStruct((rows, width), BF16),
        )
        + (jax.ShapeDtypeStruct((rows // PARTS, width), BF16),) * PARTS,
        in_specs=[pl.BlockSpec(memory_space=pltpu.SMEM)]
        + [vmem] * 5
        + [pl.BlockSpec(memory_space=pl.ANY)]
        + [vmem] * len(before),
        out_specs=(vmem,) * (4 + PARTS),
        scratch_shapes=[
            pltpu.VMEM((2 * rows, width), BF16),
            pltpu.VMEM((2 * rows, units), BF16),
            pltpu.VMEM((8, units), F32),
            pltpu.SemaphoreType.DMA((4,)),
        ],
        compiler_params=pltpu.CompilerParams(vmem_limit_bytes=36 << 20),
        name="feed",
    )(core, w_up, c_up[None], w_down, own, sib, cot, *before)


def row_copies(core, chunk, rows, source, target, sems, reverse=False):
    copies = []
    for i in range(4):
        side, y = i // 2, i % 2
        first = y * (4 * rows) + (core ^ side) * (2 * rows) + chunk * rows
        whole = pl.ds(pl.multiple_of(first, rows), rows)
        here = slice(i * rows, (i + 1) * rows)
        if reverse:
            copy = pltpu.make_async_copy(source.at[here], target.at[whole], sems.at[i])
        else:
            copy = pltpu.make_async_copy(source.at[whole], target.at[here], sems.at[i])
        copy.start()
        copies.append(copy)
    return copies


def skip_grad_kernel(chunk, core_ref, own_ref, sib_ref, dec_ref, enc_ref, *refs):
    outs, (dec_v, enc_v, sems) = refs[2 * chunk : -3], refs[-3:]
    rows = own_ref.shape[0] // 2
    width, cols = dec_v.shape[1], own_ref.shape[1]
    copies = row_copies(core_ref[0], chunk, rows, dec_ref, dec_v, sems.at[0])
    for i in range(4):
        side, y = i // 2, i % 2
        first = (y * 2 + (core_ref[0] ^ side)) * rows
        copy = pltpu.make_async_copy(
            enc_ref.at[pl.ds(pl.multiple_of(first, rows), rows)],
            enc_v.at[i * rows : (i + 1) * rows],
            sems.at[1, i],
        )
        copy.start()
        copies.append(copy)
    for copy in copies:
        copy.wait()
    half = 2 * rows
    for n, part in enumerate((dec_v, enc_v)):
        at = slice(n * width, (n + 1) * width)
        total = mm(part[:half], own_ref[...], TN) + mm(part[half:], sib_ref[...], TN)
        if not chunk:
            outs[0][at] = total
            continue
        total = (total + refs[0][at]).astype(BF16)
        side = jnp.zeros((width, 128), BF16)
        if n == 0:
            small = refs[1]
            lines = [
                small[k : k + 1, j * 128 : (j + 1) * 128] for k in range(8) for j in range(cols // 128)
            ]
            spare = jnp.zeros((width - len(lines), 128), F32)
            side = jnp.concatenate(lines + [spare], axis=0).astype(BF16)
        put_halves(core_ref[1], jnp.concatenate([total, side], axis=1), *outs, half=n)


def skip_grad(chunk, core, own, sib, dec, enc, before=()):
    rows, cols = own.shape
    width = dec.shape[1]
    vmem = pl.BlockSpec(memory_space=pltpu.VMEM)
    hbm = pl.BlockSpec(memory_space=pl.ANY)
    half = jax.ShapeDtypeStruct((width, cols + 128), BF16)
    return pl.pallas_call(
        functools.partial(skip_grad_kernel, chunk),
        out_shape=(half, half) if chunk else (jax.ShapeDtypeStruct((2 * width, cols), F32),),
        in_specs=[pl.BlockSpec(memory_space=pltpu.SMEM), vmem, vmem, hbm, hbm]
        + [vmem] * len(before),
        out_specs=(vmem,) * (1 + chunk),
        scratch_shapes=[
            pltpu.VMEM((2 * rows, width), BF16),
            pltpu.VMEM((2 * rows, width), BF16),
            pltpu.SemaphoreType.DMA((2, 4)),
        ],
        compiler_params=pltpu.CompilerParams(vmem_limit_bytes=24 << 20),
        name="skip_grad",
    )(core, own, sib, dec, enc, *before)


def skip_back_kernel(chunk, core_ref, w_ref, own_ref, sib_ref, *refs):
    back_ref, whole_ref, held, sems = refs[-4:]
    rows = own_ref.shape[0] // 2
    for side, part in enumerate((own_ref, sib_ref)):
        at = slice(side * 2 * rows, (side + 1) * 2 * rows)
        back_ref[at] = mm(part[...], w_ref[1], NT).astype(BF16)
        held[at] = mm(part[...], w_ref[0], NT)
    for copy in row_copies(core_ref[0], chunk, rows, held, whole_ref, sems, reverse=True):
        copy.wait()


def skip_back(chunk, core, w_skip, own, sib, group_rows, before=(), ahead=()):
    rows = own.shape[0]
    width = w_skip.shape[1]
    vmem = pl.BlockSpec(memory_space=pltpu.VMEM)
    hbm = pl.BlockSpec(memory_space=pl.ANY)
    return pl.pallas_call(
        functools.partial(skip_back_kernel, chunk),
        out_shape=(
            jax.ShapeDtypeStruct((2 * rows, width), BF16),
            jax.ShapeDtypeStruct((group_rows, width), F32),
        ),
        in_specs=[pl.BlockSpec(memory_space=pltpu.SMEM), vmem, vmem, vmem]
        + [hbm] * (len(before) + len(ahead)),
        out_specs=(vmem, hbm),
        scratch_shapes=[pltpu.VMEM((2 * rows, width), F32), pltpu.SemaphoreType.DMA((4,))],
        input_output_aliases={4: 1} if before else {},
        compiler_params=pltpu.CompilerParams(vmem_limit_bytes=24 << 20),
        name="skip_back",
    )(core, w_skip, own, sib, *before, *ahead)


def restore_kernel(core_ref, *refs):
    out_ref = refs[-1]
    for chunk, part in enumerate(refs[:-1]):
        rows = part.shape[0] // 4
        for i in range(4):
            side, y = i // 2, i % 2
            first = y * (4 * rows) + (core_ref[0] ^ side) * (2 * rows) + chunk * rows
            out_ref[pl.ds(pl.multiple_of(first, rows), rows)] = part[i * rows : (i + 1) * rows]


def restore(core, parts):
    vmem = pl.BlockSpec(memory_space=pltpu.VMEM)
    rows, width = parts[0].shape
    return pl.pallas_call(
        restore_kernel,
        out_shape=jax.ShapeDtypeStruct((rows * len(parts), width), parts[0].dtype),
        in_specs=[pl.BlockSpec(memory_space=pltpu.SMEM)] + [vmem] * len(parts),
        out_specs=vmem,
        compiler_params=pltpu.CompilerParams(vmem_limit_bytes=12 << 20),
        name="restore",
    )(core, *parts)


def skip_kernel(chunk, core_ref, w_ref, dec_ref, enc_ref, own_ref, *refs):
    sib_refs, (dec_v, enc_v, sems) = refs[:PARTS], refs[PARTS:]
    rows = own_ref.shape[0] // 2
    copies = row_copies(core_ref[0], chunk, rows, dec_ref, dec_v, sems.at[0])
    for i in range(4):
        side, y = i // 2, i % 2
        first = (y * 2 + (core_ref[0] ^ side)) * rows
        copy = pltpu.make_async_copy(
            enc_ref.at[pl.ds(pl.multiple_of(first, rows), rows)],
            enc_v.at[i * rows : (i + 1) * rows],
            sems.at[1, i],
        )
        copy.start()
        copies.append(copy)
    for copy in copies:
        copy.wait()
    half = 2 * rows
    strip = half // PARTS
    for n, sib_ref in enumerate(sib_refs):
        at = slice(half + n * strip, half + (n + 1) * strip)
        sib_ref[...] = (mm(dec_v[at], w_ref[0], NN) + mm(enc_v[at], w_ref[1], NN)).astype(BF16)
    own_ref[...] = (mm(dec_v[:half], w_ref[0], NN) + mm(enc_v[:half], w_ref[1], NN)).astype(BF16)


def skip(chunk, core, w_skip, dec, enc):
    rows = enc.shape[0] // 2
    width, cols = w_skip.shape[1:]
    vmem = pl.BlockSpec(memory_space=pltpu.VMEM)
    hbm = pl.BlockSpec(memory_space=pl.ANY)
    return pl.pallas_call(
        functools.partial(skip_kernel, chunk),
        out_shape=(jax.ShapeDtypeStruct((rows, cols), BF16),)
        + (jax.ShapeDtypeStruct((rows // PARTS, cols), BF16),) * PARTS,
        in_specs=[pl.BlockSpec(memory_space=pltpu.SMEM), vmem, hbm, hbm],
        out_specs=(vmem,) * (1 + PARTS),
        scratch_shapes=[
            pltpu.VMEM((2 * rows, width), BF16),
            pltpu.VMEM((2 * rows, width), BF16),
            pltpu.SemaphoreType.DMA((2, 4)),
        ],
        compiler_params=pltpu.CompilerParams(vmem_limit_bytes=16 << 20),
        name="skip",
    )(core, w_skip, dec, enc)


def shards(
    decoder_in,
    encoder_out,
    segments,
    w_skip,
    b_skip,
    ln1_gain,
    ln1_bias,
    w_qkv,
    w_out,
    ln2_gain,
    ln2_bias,
    w_up,
    c_up,
    w_down,
    cotangent,
):
    group_rows = decoder_in.shape[0]
    tensor_rank = lax.axis_index("tensor")
    core = tensor_rank & 1
    chip = tensor_rank >> 1
    heads_here = HEADS // lax.axis_size("tensor")
    local_width = heads_here * HEAD_DIM
    block = group_rows // (4 * CHUNKS)
    qkv_matrix = w_qkv.reshape(D, 3 * local_width)
    steps = group_steps()
    mines = [((lax.axis_index(axis) >> bit) & 1).astype(jnp.int32) for axis, bit in steps]
    core_scalar = jnp.stack([core.astype(jnp.int32), mines[0]])
    slopes = jnp.exp2(
        -8.0
        * (tensor_rank * heads_here + jnp.arange(heads_here, dtype=jnp.int32) + 1).astype(F32)
        / HEADS
    )
    spots = [(chunk, side) for chunk in range(CHUNKS) for side in range(2)]

    def piece_of(array, chunk, side):
        width = array.shape[-1]
        parts = array.reshape(2, 2, CHUNKS, block, width)[:, :, chunk]
        return lax.dynamic_index_in_dim(parts, core ^ side, 1, keepdims=False).reshape(
            2 * block, width
        )

    cot = [piece_of(cotangent, chunk, 0) for chunk in range(CHUNKS)]
    encoder_parts = encoder_out.reshape(2, 2, CHUNKS, block, encoder_out.shape[1])
    partner = [
        partner_swap(encoder_parts[:, :, chunk].reshape(4 * block, -1)) for chunk in range(CHUNKS)
    ]

    def chip_total(half):
        sent = core_swap(half(1).astype(BF16))
        return (half(0) + sent.astype(F32)).astype(BF16)

    merged, norm_one, qkv = [], {}, {}
    sums = []
    for chunk in range(CHUNKS):
        own, *sib = skip(chunk, core_scalar, w_skip, decoder_in, partner[chunk])
        sums.append(add_low(own, jnp.concatenate([core_swap(part) for part in sib], axis=0)))
        if chunk + 1 < CHUNKS:
            partner[chunk + 1] = gate(partner[chunk + 1], sums[chunk])
    others = [chip_swap(part) for part in sums]
    ahead = (qkv_matrix, *sums)
    for chunk in range(CHUNKS):
        value, normal = norm_rows(
            b_skip[None], sums[chunk], others[chunk], ln1_gain, ln1_bias, ahead
        )
        merged.append(value)
        norm_one[chunk, 0] = normal
        norm_one[chunk, 1] = core_swap(normal)
        for side in range(2):
            qkv[chunk, side] = jnp.dot(
                norm_one[chunk, side], qkv_matrix, preferred_element_type=F32
            ).astype(BF16)
        ahead = (qkv[chunk, 0], qkv[chunk, 1], *cot)
    qkv_pieces = [qkv[spot].reshape(2, block, 3 * local_width) for spot in spots]

    heads_out, lse, sums = [], [], []
    for chunk in range(CHUNKS):
        mixed, log_total, own, *sib = attend(
            chunk, core_scalar, slopes, segments, w_out, qkv_pieces, sums
        )
        heads_out.append(mixed)
        lse.append(log_total)
        sums.append(add_low(own, jnp.concatenate([core_swap(part) for part in sib], axis=0)))
    others = [chip_swap(part) for part in sums]

    attended, activated, d_sums, d_others = [], [], [], []
    ahead = tuple(sums)
    grads = ()
    for chunk in range(CHUNKS):
        value, normal = norm_rows(
            merged[chunk], sums[chunk], others[chunk], ln2_gain, ln2_bias, ahead
        )
        attended.append(value)
        acts, weights_sum, bias_sum, own, *sib = feed(
            chunk, core_scalar, w_up, c_up, w_down, normal, core_swap(normal), cotangent, grads
        )
        grads = (weights_sum, bias_sum)
        activated.append(acts)
        sib = gate([core_swap(part) for part in sib], d_others[chunk - 1] if chunk else others[1])
        d_sums.append(add_low(own, jnp.concatenate(sib, axis=0)))
        d_others.append(chip_swap(d_sums[chunk]))
        ahead = (d_sums[chunk],)
    d_w_ff, c_up_sum = grads
    both = ("section", "dp")
    d_w_ff = lax.psum_scatter(
        gate(d_w_ff, d_sums[-1]), both, scatter_dimension=0, tiled=True
    )

    d_attended, d_attended_rows = [], {}
    sums_two = jnp.zeros((3, 8, D), F32)
    before = ()
    for chunk in range(CHUNKS):
        value, low, sums_two = norm_back_rows(
            cot[chunk], attended[chunk], d_sums[chunk], d_others[chunk], ln2_gain, sums_two,
            ahead,
        )
        d_attended.append(value)
        d_attended_rows[chunk, 0] = low
        d_attended_rows[chunk, 1] = core_swap(low)
        d_heads = [
            mm(d_attended_rows[chunk, side], w_out, NT).astype(BF16) for side in range(2)
        ]
        before = attend_back(
            chunk, core_scalar, slopes, segments, qkv_pieces, d_heads, heads_out[chunk],
            lse[chunk], before,
        )
        ahead = (before[0],)
    d_qkv = before

    sums = [
        chip_total(lambda side: mm(d_qkv[2 * chunk + side], qkv_matrix, NT))
        for chunk in range(CHUNKS)
    ]
    others = [chip_swap(part) for part in sums]
    kept, sent = late_grads(
        mines[0],
        [norm_one[spot] for spot in spots],
        d_qkv,
        heads_out,
        [d_attended_rows[spot] for spot in spots],
        sums,
    )
    late = GroupSum(kept, sent, steps, mines)
    activated = gate(activated, kept)
    down = [
        chip_total(
            lambda side: jnp.dot(activated[chunk][side], w_down, preferred_element_type=F32)
        )
        for chunk in range(CHUNKS)
    ]

    aways = [
        lax.dynamic_index_in_dim(part.reshape(2, block, D), 1 - chip, 0, keepdims=False)
        for part in down
    ]
    lows = []
    sums_one = jnp.zeros((3, 8, D), F32)
    ahead = (kept,)
    for chunk in range(CHUNKS):
        _, low, sums_one = norm_back_rows(
            d_attended[chunk], merged[chunk], sums[chunk], others[chunk], ln1_gain, sums_one, ahead
        )
        lows.append(low)
        if chunk == 0:
            ahead = (late.step(low, *aways),)
    d_w_ff = lax.all_gather(gate(d_w_ff, lows[0]), both, axis=0, tiled=True)
    sibs = [core_swap(low) for low in lows]
    small = jnp.sum(jnp.concatenate([sums_one, sums_two], axis=0), axis=1) * 0.5
    small = small + core_swap(small)
    small = small + chip_swap(small)
    small = jnp.concatenate([small, jnp.sum(c_up_sum, axis=0)[None]], axis=0)
    small = jnp.pad(small, ((0, 16 - small.shape[0]), (0, 0)))
    before = ()
    for chunk in range(CHUNKS):
        before = skip_grad(
            chunk, core_scalar, lows[chunk], sibs[chunk], decoder_in, partner[chunk],
            (*before, small) if chunk else (),
        )
    kept, sent = before
    last = GroupSum(kept, sent, steps, mines)
    d_encoder, before = [], ()
    for chunk in range(CHUNKS):
        returned, *before = skip_back(
            chunk, core_scalar, w_skip, lows[chunk], sibs[chunk], group_rows, before, (kept,)
        )
        d_encoder.append(returned)
    (d_decoder_in,) = before
    d_encoder_out = restore(core_scalar, [partner_swap(part) for part in d_encoder])
    last.step(*d_encoder)

    moved = [chip_swap(part) for part in gate(aways, lows[-1])]
    d_w_down, d_w_up = d_w_ff[: w_down.shape[0]].astype(F32), d_w_ff[w_down.shape[0] :].astype(F32)
    total = 2 * len(steps)
    while last.count < total - 1:
        if late.count < total - 1:
            late.step(last.kept)
        last.step()
    moved = gate(moved, last.kept)
    layer_out = []
    for chunk in range(CHUNKS):
        home, base = (
            lax.dynamic_index_in_dim(part.reshape(2, block, D), chip, 0, keepdims=False)
            for part in (down[chunk], attended[chunk])
        )
        layer_out.append(base + (home.astype(F32) + moved[chunk].astype(F32)))
    layer_out = jnp.concatenate(layer_out, axis=0)
    while not late.done:
        late.step(last.kept, d_w_down, d_w_up, layer_out)
    last.step(d_encoder_out)
    d_w_qkv = jnp.stack(
        [late.kept[:, n * local_width : (n + 1) * local_width] for n in range(3)], axis=0
    )
    d_w_qkv = jnp.transpose(d_w_qkv.astype(F32), (1, 0, 2))
    d_w_out = late.kept[:, 3 * local_width :].T
    d_w_skip = last.kept[:, :D].reshape(w_skip.shape)
    small = last.kept[: 8 * D // 128, D:].astype(F32).reshape(8, D)
    return (
        layer_out,
        d_decoder_in,
        d_encoder_out,
        d_w_skip.astype(F32),
        small[2],
        small[0],
        small[1],
        d_w_qkv.astype(F32),
        d_w_out.astype(F32),
        small[3],
        small[4],
        d_w_up,
        small[6],
        d_w_down,
    )


def solution(mesh):
    return jax.shard_map(
        shards,
        mesh=mesh,
        in_specs=(
            P(("section", "dp"), "tensor"),
            P(("section", "dp"), "tensor"),
            P(("section", "dp"), None),
            P(None, "tensor", None),
            P(),
            P(),
            P(),
            P(None, None, "tensor"),
            P("tensor", None),
            P(),
            P(),
            P(None, "tensor"),
            P("tensor"),
            P("tensor", None),
            P(("section", "dp"), None),
        ),
        out_specs=(
            P(("section", "dp", "tensor"), None),
            P(("section", "dp"), "tensor"),
            P(("section", "dp"), "tensor"),
            P(None, "tensor", None),
            P(),
            P(),
            P(),
            P(None, None, "tensor"),
            P("tensor", None),
            P(),
            P(),
            P(None, "tensor"),
            P("tensor"),
            P("tensor", None),
        ),
        check_vma=False,
    )
```
